32 devices in a mesh: segment: 2 (over core), img: 16 (over z, y, x).
Axes of the slice: x: 2, y: 2, z: 4, core: 2. Of those that a mesh axis runs over, the one named last changes fastest.
Arguments:
- patch_tokens: bfloat16 [4, 128, 256, 384], P('segment', 'img'), may hold values from -6 to 6
- class_tokens: bfloat16 [4, 128, 384], P('segment', 'img'), may hold values from -6 to 6
- region_number: int32 [4, 128], P('segment'), may hold values from 0 to 2, as said below
- frozen_gain: bfloat16 [384], replicated, may hold values from 0.099609375 to 1.8984375
- frozen_triple: bfloat16 [384, 1152], replicated, may hold values from -0.3125 to 0.3125
- frozen_merge: bfloat16 [384, 384], replicated, may hold values from -1.25 to 1.25
- frozen_regain: bfloat16 [384], replicated, may hold values from 0.099609375 to 1.8984375
- frozen_expand: bfloat16 [384, 1536], replicated, may hold values from -0.3125 to 0.3125
- frozen_shrink: bfloat16 [1536, 384], replicated, may hold values from -0.15625 to 0.15625
- gain_first: bfloat16 [384], P('img'), may hold values from 0.099609375 to 1.8984375
- weight_triple: bfloat16 [384, 1152], P('img'), may hold values from -0.3125 to 0.3125
- weight_merge: bfloat16 [384, 384], P('img'), may hold values from -1.25 to 1.25
- gain_second: bfloat16 [384], P('img'), may hold values from 0.099609375 to 1.8984375
- weight_expand: bfloat16 [384, 1536], P('img'), may hold values from -0.3125 to 0.3125
- weight_shrink: bfloat16 [1536, 384], P('img'), may hold values from -0.15625 to 0.15625
- patch_cotangent: bfloat16 [4, 128, 256, 384], P('segment', 'img'), may hold values from -6 to 6
- region_cotangent: bfloat16 [4, 128, 384], P('segment', 'img'), may hold values from -6 to 6
Outputs:
- patch_output: bfloat16 [4, 128, 256, 384], P('segment', 'img')
- region_output: bfloat16 [4, 128, 384], P('segment', 'img')
- patch_gradient: bfloat16 [4, 128, 256, 384], P('segment', 'img')
- class_gradient: bfloat16 [4, 128, 384], P('segment', 'img')
- first_gradient: float32 [384], P('img')
- triple_gradient: float32 [384, 1152], P('img')
- merge_gradient: float32 [384, 384], P('img')
- second_gradient: float32 [384], P('img')
- expand_gradient: float32 [384, 1536], P('img')
- shrink_gradient: float32 [1536, 384], P('img')
The draws below stay inside these ranges and needn't reach their ends.
Inputs may be any that keep to these rules, and one draw needn't show every extreme that they name: `region_number`: region numbers start at 0 and never fall along a micro-batch's 128 images; in each micro-batch one region begins among the first 8 images and ends among the last 8, with at most one region before it and one after it.
All inputs are finite; a program needn't handle non-finite values.
Results may differ from the reference program's by a relative error of at most 0.025.
Values may be sent and summed in bfloat16 or wider, within the bound.
A program may use at most 256 MiB of HBM per device.

```python
import jax
import jax.numpy as jnp
from jax import lax

D = 384
HD = 64
FF = 1536
P_SIZE = 256
IMG_DEV = 8
MICRO = 4
SLOTS = 128


def draw_region_number(key, part):
    key = jax.random.fold_in(key, 11)
    begin_key, finish_key = jax.random.split(key)
    begin = jax.random.randint(begin_key, (MICRO, 1), 0, IMG_DEV)
    begin = begin.at[0, 0].set(jnp.maximum(begin[0, 0], 1))
    finish = SLOTS - jax.random.randint(finish_key, (MICRO, 1), 1, IMG_DEV)
    place = jnp.arange(SLOTS, dtype=jnp.int32)[None, :]
    number = jnp.where((place >= begin) & (begin > 0), 1, 0) + jnp.where(place >= finish, 1, 0)
    return number.astype(jnp.int32)


def block_levels(own_key, shape, shards, smallest, high):
    def one(dim, parts):
        draws = jax.random.uniform(jax.random.fold_in(jax.random.fold_in(own_key, 6), dim), (parts,), jnp.float32, smallest / len(shards), high / len(shards))
        return jnp.repeat(jnp.exp(draws), shape[dim] // parts).reshape((-1,) + (1,) * (len(shape) - dim - 1))

    level = one(*shards[0])
    for cut in shards[1:]:
        level = level * one(*cut)
    return level


def scatter_about(own_key, extent, spread, most, cuts=(), held_as=jnp.bfloat16):
    gain = block_levels(own_key, extent, cuts, -0.22, 0.18) if cuts else 1.0
    array = jax.random.normal(own_key, extent, jnp.float32) * spread * gain
    return jnp.minimum(jnp.maximum(array, -most), most).astype(held_as)


def setup_inputs(seed: int = 0) -> dict:
    key_of = jax.random.split(jax.random.key(seed), 18)
    patch_tokens = scatter_about(key_of[0], (MICRO, SLOTS, P_SIZE, D), 1.0, 6.0, ((0, 2), (1, 16)))
    class_tokens = scatter_about(key_of[1], (MICRO, SLOTS, D), 1.0, 6.0, ((0, 2), (1, 16)))
    region_number = draw_region_number(jax.random.fold_in(key_of[17], 71), 0)
    frozen_gain = jnp.clip(1.0 + 0.18 * jax.random.normal(key_of[3], (D,), jnp.float32), 0.099609375, 1.8984375).astype(jnp.bfloat16)
    frozen_triple = scatter_about(key_of[4], (D, 3 * D), D ** -0.5, 0.3125)
    frozen_merge = scatter_about(key_of[5], (D, D), (D // 16) ** -0.5, 1.25)
    frozen_regain = jnp.clip(1.0 + 0.18 * jax.random.normal(key_of[6], (D,), jnp.float32), 0.099609375, 1.8984375).astype(jnp.bfloat16)
    frozen_expand = scatter_about(key_of[7], (D, FF), D ** -0.5, 0.3125)
    frozen_shrink = scatter_about(key_of[8], (FF, D), FF ** -0.5, 0.15625)
    gain_first = jnp.clip(1.0 + 0.18 * jax.random.normal(key_of[9], (D,), jnp.float32), 0.099609375, 1.8984375).astype(jnp.bfloat16)
    weight_triple = scatter_about(key_of[10], (D, 3 * D), D ** -0.5, 0.3125, ((0, 16),))
    weight_merge = scatter_about(key_of[11], (D, D), (D // 16) ** -0.5, 1.25, ((0, 16),))
    gain_second = jnp.clip(1.0 + 0.18 * jax.random.normal(key_of[12], (D,), jnp.float32), 0.099609375, 1.8984375).astype(jnp.bfloat16)
    weight_expand = scatter_about(key_of[13], (D, FF), D ** -0.5, 0.3125, ((0, 16),))
    weight_shrink = scatter_about(key_of[14], (FF, D), FF ** -0.5, 0.15625, ((0, 16),))
    patch_cotangent = scatter_about(key_of[15], (MICRO, SLOTS, P_SIZE, D), 1.0, 6.0, ((0, 2), (1, 16)))
    region_cotangent = scatter_about(key_of[16], (MICRO, SLOTS, D), 1.0, 6.0, ((0, 2), (1, 16)))
    return dict(patch_tokens=patch_tokens, class_tokens=class_tokens, region_number=region_number, frozen_gain=frozen_gain, frozen_triple=frozen_triple, frozen_merge=frozen_merge, frozen_regain=frozen_regain, frozen_expand=frozen_expand, frozen_shrink=frozen_shrink, gain_first=gain_first, weight_triple=weight_triple, weight_merge=weight_merge, gain_second=gain_second, weight_expand=weight_expand, weight_shrink=weight_shrink, patch_cotangent=patch_cotangent, region_cotangent=region_cotangent)


@jax.custom_vjp
def low(v):
    return lax.optimization_barrier(v.astype(jnp.bfloat16)).astype(jnp.float32)

@jax.custom_vjp
def low_back(v):
    return v

def low_keep(v):
    return (low(v), None)

def low_pass(kept, grad):
    return (grad,)

def back_keep(v):
    return (v, None)

def back_low(kept, grad):
    return (low(grad),)
low.defvjp(low_keep, low_pass)
low_back.defvjp(back_keep, back_low)
highest = lax.Precision.HIGHEST
epsilon = 1e-06

def normalize(values, scaling):
    centred = values - lax.optimization_barrier(jnp.mean(values, axis=-1, keepdims=True))
    return centred * lax.rsqrt(lax.optimization_barrier(jnp.mean(centred * centred, axis=-1, keepdims=True)) + epsilon) * scaling

def block(inputs, weights, allowed):
    gain_a, triple, merger, gain_b, expand, shrink = weights
    model_width = inputs.shape[-1]
    head_shape = inputs.shape[:-1] + (model_width // HD, HD)
    first_low = low(normalize(inputs, gain_a))
    packed = low_back(low(jnp.einsum('bsd,de->bse', first_low, triple, precision=highest)))
    queries = packed[..., :model_width].reshape(head_shape)
    keyset = packed[..., model_width:2 * model_width].reshape(head_shape)
    valueset = packed[..., 2 * model_width:].reshape(head_shape)
    scores = low_back(jnp.einsum('bqhd,bkhd->bhqk', queries, keyset, precision=highest) * HD ** (-0.5))
    if allowed is not None:
        scores = jnp.where(allowed[:, None], scores, -1e+30)
    weighting = low(jax.nn.softmax(scores, axis=-1))
    mixed = jnp.einsum('bhqk,bkhd->bqhd', weighting, valueset, precision=highest).reshape(inputs.shape)
    context = low_back(low(mixed))
    middle = inputs + low_back(jnp.einsum('bsd,de->bse', context, merger, precision=highest))
    second = low(normalize(middle, gain_b))
    hidden = low_back(jnp.einsum('bsd,df->bsf', second, expand, precision=highest))
    active = low(jax.nn.gelu(hidden, approximate=False))
    return middle + low_back(jnp.einsum('bsf,fd->bsd', active, shrink, precision=highest))

def reference(patch_tokens, class_tokens, region_number, frozen_gain, frozen_triple, frozen_merge, frozen_regain, frozen_expand, frozen_shrink, gain_first, weight_triple, weight_merge, gain_second, weight_expand, weight_shrink, patch_cotangent, region_cotangent):
    frozen = tuple((weight.astype(jnp.float32) for weight in (frozen_gain, frozen_triple, frozen_merge, frozen_regain, frozen_expand, frozen_shrink)))
    micros, images, patches, model_width = patch_tokens.shape
    allowed = region_number[:, :, None] == region_number[:, None, :]

    def image_block(group):
        return block(group, frozen, None)

    def forward(tokens, heads_in, gain_a, triple, merger, gain_b, expand, shrink):
        joined = jnp.concatenate([heads_in[:, :, None, :], tokens], axis=2)
        groups = joined.reshape(micros * images // 8, 8, patches + 1, model_width)
        passed = lax.map(jax.checkpoint(image_block), groups).reshape(micros, images, patches + 1, model_width)
        crossed = low_back(low(jnp.roll(passed[:, :, 0, :], micros // 2, axis=0)))
        region = block(crossed, (gain_a, triple, merger, gain_b, expand, shrink), allowed)
        return (passed[:, :, 1:, :], region)
    outputs, pullback = jax.vjp(forward, patch_tokens.astype(jnp.float32), class_tokens.astype(jnp.float32), gain_first.astype(jnp.float32), weight_triple.astype(jnp.float32), weight_merge.astype(jnp.float32), gain_second.astype(jnp.float32), weight_expand.astype(jnp.float32), weight_shrink.astype(jnp.float32))
    grads = pullback((patch_cotangent.astype(jnp.float32), region_cotangent.astype(jnp.float32)))
    return (outputs[0].astype(jnp.bfloat16), outputs[1].astype(jnp.bfloat16), grads[0].astype(jnp.bfloat16), grads[1].astype(jnp.bfloat16), grads[2], grads[3], grads[4], grads[5], grads[6], grads[7])
```

```python
import functools
from types import SimpleNamespace

import jax
import jax.numpy as jnp
from jax import lax
from jax.experimental import pallas as pl
from jax.experimental.pallas import tpu as pltpu
from jax.sharding import PartitionSpec as P

SEG = "segment"
IMG = "img"
HD = 64
HEADS8 = 8
EPSILON = 1e-06
LOG2E = 1.4426950408889634
LN2 = 0.6931471805599453
ROOT_HALF = 0.7071067811865476
DENSITY = 0.3989422804014327
F32 = jnp.float32
BF16 = jnp.bfloat16
MESH = pl.DeviceIdType.MESH
NEG = -1e30
PAD = 32

AT_FORWARD = 6
AT_REGION = 7


def nn(a, b):
    return lax.dot_general(a, b, (((1,), (0,)), ((), ())), preferred_element_type=F32)


def nt(a, b):
    return lax.dot_general(a, b, (((1,), (1,)), ((), ())), preferred_element_type=F32)


def tn(a, b):
    return lax.dot_general(a, b, (((0,), (0,)), ((), ())), preferred_element_type=F32)


def mean(values, axis):
    return jnp.sum(values, axis=axis, keepdims=True) * (1.0 / values.shape[axis])


def standardize(values, axis):
    centre = mean(values, axis)
    centred = values - centre
    inverse = lax.rsqrt(mean(centred * centred, axis) + EPSILON)
    return centred * inverse, centre, inverse


def norm_back(scaled, standard, inverse, axis):
    return inverse * (
        scaled - mean(scaled, axis) - standard * mean(scaled * standard, axis)
    )


def gelu_pair(hidden):
    upto = 0.5 + 0.5 * lax.erf(hidden * ROOT_HALF)
    bell = jnp.exp2(hidden * hidden * (-0.5 * LOG2E))
    return hidden * upto, upto + hidden * (bell * DENSITY)


def own_heads(rows, width):
    shape = (rows * HEADS8, width)
    lane = lax.broadcasted_iota(jnp.int32, shape, 1) // HD
    return lane == lax.rem(lax.broadcasted_iota(jnp.int32, shape, 0), HEADS8)


def spread(values):
    rows, width = values.shape
    tall = jnp.broadcast_to(values[:, None, :], (rows, HEADS8, width))
    return jnp.where(own_heads(rows, width), tall.reshape(rows * HEADS8, width), 0.0)


def gather_heads(values):
    tall, width = values.shape
    kept = jnp.where(own_heads(tall // HEADS8, width), values, 0.0)
    return jnp.sum(kept.reshape(tall // HEADS8, HEADS8, width), axis=1)


def wide_row(vectors, first, count):
    return jnp.concatenate([vectors[k : k + 1, :] for k in range(first, first + count)], axis=1)


def column(row, lanes):
    tall = jnp.broadcast_to(row, (128, row.shape[1])).T
    return jnp.concatenate([tall] * (lanes // 128), axis=1)


def pair_copy(source, target, sems, it):
    part = pl.ds(2 * it, 2)
    return pltpu.make_async_copy(source.at[part], target.at[part], sems.at[it])


def padded(values, shard, n):
    blank = jnp.zeros((PAD - shard, values.shape[1]), values.dtype)
    parts = []
    for j in range(n):
        parts += [values[shard * j : shard * (j + 1)], blank]
    return jnp.concatenate(parts, axis=0)


def trimmed(values, shard, n):
    return jnp.concatenate([values[PAD * j : PAD * j + shard] for j in range(n)], axis=0)


def patch_kernel(dims, *refs):
    r = SimpleNamespace(**dict(zip(dims.names, refs, strict=True)))
    n_img, width, hidden, inside = dims.n_img, dims.width, dims.hidden, dims.inside
    heads = width // HD
    rows, patches = dims.images, dims.patches
    pairs, lanes = rows // 2, 2 * patches
    shard = width // n_img
    shard_ff = hidden // n_img

    if inside:
        seg = lax.axis_index(SEG)
        me = lax.axis_index(IMG)
        barrier = pltpu.get_barrier_semaphore()

        def sibling(src, dst, link):
            return pltpu.make_async_remote_copy(
                src_ref=src,
                dst_ref=dst,
                send_sem=link.at[0],
                recv_sem=link.at[1],
                device_id={SEG: 1 - seg},
                device_id_type=MESH,
            )

        def to_peers(source, target, link):
            def send(step, carry):
                pltpu.make_async_remote_copy(
                    src_ref=source,
                    dst_ref=target,
                    send_sem=link.at[0],
                    recv_sem=link.at[1],
                    device_id={IMG: lax.rem(me + step, n_img)},
                    device_id_type=MESH,
                ).start()
                return carry

            lax.fori_loop(1, n_img, send, 0)
            pltpu.make_async_copy(source, target, link.at[1]).start()

        def to_other_segment(source, target, link):
            def send(step, carry):
                pltpu.make_async_remote_copy(
                    src_ref=source,
                    dst_ref=target,
                    send_sem=link.at[0],
                    recv_sem=link.at[1],
                    device_id={SEG: 1 - seg, IMG: lax.rem(me + step, n_img)},
                    device_id_type=MESH,
                ).start()
                return carry

            lax.fori_loop(0, n_img, send, 0)

        def wait_all(whole, sem):
            pltpu.make_async_copy(whole, whole, sem).wait()

        def greet(step, carry):
            peer = lax.rem(me + step, n_img)
            for other in range(2):
                pl.semaphore_signal(
                    barrier,
                    inc=1,
                    device_id={SEG: lax.rem(seg + other, 2), IMG: peer},
                    device_id_type=MESH,
                )
            return carry

        lax.fori_loop(1, n_img, greet, 0)
        pl.semaphore_signal(barrier, inc=1, device_id={SEG: 1 - seg}, device_id_type=MESH)

    for it in range(pairs):
        pair_copy(r.tokens, r.tok, r.tok_sem, it).start()
    for it in range(pairs):
        pair_copy(r.cotangent, r.cot, r.cot_sem, it).start()

    vectors = r.vectors[...]
    gain_row = wide_row(vectors, 0, width // 128)
    regain_row = wide_row(vectors, width // 128, width // 128)
    if inside:
        blank = jnp.zeros((PAD - shard, 4 * width), F32)
        triple = r.weight_triple[...].astype(F32)
        merge = r.weight_merge[...].astype(F32)
        expand = r.weight_expand[...].astype(F32)
        first_half = jnp.concatenate([triple, merge], axis=1)
        r.w_own[0] = jnp.concatenate([first_half, blank], axis=0).astype(BF16)
        r.w_own[1] = jnp.concatenate([expand, blank], axis=0).astype(BF16)
        for k in range(2):
            r.s_own[k] = r.weight_shrink[k * shard_ff // 2 : (k + 1) * shard_ff // 2, :]
            row = vectors[2 * width // 128 + k : 2 * width // 128 + k + 1, :]
            r.gain_own[k * shard : (k + 1) * shard, :] = column(row, 128)[0:shard]
        pl.semaphore_wait(barrier, 2 * n_img - 1)
        to_peers(r.gain_own, r.gains.at[me], r.l_gain)
        to_peers(r.region_cotangent, r.region_up.at[me], r.l_up)
        to_peers(r.w_own.at[seg], r.w_all.at[seg, me], r.l_weights)
        to_peers(r.s_own.at[seg], r.s_all.at[seg, me], r.l_shrink)

    r.tripleT[...] = r.frozen_triple[...].T
    r.mergeT[...] = r.frozen_merge[...].T
    r.expandT[...] = r.frozen_expand[...].T
    r.shrinkT[...] = r.frozen_shrink[...].T
    r.gainT[...] = column(gain_row, lanes)
    r.regainT[...] = column(regain_row, lanes)

    block_head = own_heads(1, width)
    class_in = r.class_tokens[...].astype(F32)
    class_unit, _, _ = standardize(class_in, 1)
    class_first = (class_unit * gain_row).astype(BF16)
    class_packed = nn(class_first, r.frozen_triple[...]).astype(BF16).astype(F32)
    r.class_packed[...] = class_packed
    tall_q = spread(class_packed[:, 0:width])
    tall_k = spread(class_packed[:, width : 2 * width])
    tall_v = spread(class_packed[:, 2 * width :])
    r.class_k[...] = tall_k.reshape(rows, HEADS8, width)
    r.class_v[...] = tall_v.reshape(rows, HEADS8, width)
    query_map = nt(tall_q.astype(BF16), r.frozen_triple[:, width : 2 * width])
    query_map = query_map * (LOG2E * HD ** (-0.5))
    r.query_map[...] = query_map.reshape(rows, HEADS8, width)
    self_score = jnp.sum(tall_q * tall_k, axis=1, keepdims=True) * (LOG2E * HD ** (-0.5))
    r.self_score[...] = jnp.broadcast_to(self_score, (rows * HEADS8, 128)).reshape(
        rows, HEADS8, 128
    )
    r.class_first[...] = jnp.broadcast_to(
        class_first.astype(F32)[:, None, :], (rows, HEADS8, width)
    )

    def class_forward(it, carry):
        pair_copy(r.tokens, r.tok, r.tok_sem, it).wait()
        values = jnp.concatenate([r.tok[2 * it + b].T for b in range(2)], axis=1).astype(F32)
        unit, centre, inverse = standardize(values, 0)
        first = (unit * r.gainT[...]).astype(BF16)
        r.firstT[it] = first
        r.stat[it, 0:1, :] = centre
        r.stat[it, 1:2, :] = inverse
        maps = jnp.concatenate([r.query_map[2 * it + b] for b in range(2)], axis=0)
        scores = nn(maps.astype(BF16), first)
        for b in range(2):
            part = scores[b * HEADS8 : (b + 1) * HEADS8, b * patches : (b + 1) * patches]
            alone = r.self_score[2 * it + b][:, 0:1]
            top = jnp.maximum(jnp.max(part, axis=1, keepdims=True), alone)
            weights = jnp.exp2(part - top)
            weight_alone = jnp.exp2(alone - top)
            share = 1.0 / (jnp.sum(weights, axis=1, keepdims=True) + weight_alone)
            weights = weights * share
            weight_alone = weight_alone * share
            r.class_probs[2 * it + b] = weights
            r.self_prob[2 * it + b] = jnp.broadcast_to(weight_alone, (HEADS8, 128))
            mixed = nt(weights.astype(BF16), first[:, b * patches : (b + 1) * patches])
            r.mixed[2 * it + b] = mixed + weight_alone * r.class_first[2 * it + b]
        return carry

    lax.fori_loop(0, pairs, class_forward, 0)

    mixed = r.mixed[...].reshape(rows * HEADS8, width).astype(BF16)
    class_context = gather_heads(nn(mixed, r.frozen_triple[:, 2 * width :])).astype(BF16)
    class_middle = class_in + nn(class_context, r.frozen_merge[...])
    class_unit_b, _, _ = standardize(class_middle, 1)
    class_second = (class_unit_b * regain_row).astype(BF16)
    class_active, class_slope = gelu_pair(nn(class_second, r.frozen_expand[...]))
    class_out = class_middle + nn(class_active.astype(BF16), r.frozen_shrink[...])
    r.class_context[...] = class_context.astype(F32)
    r.class_middle[...] = class_middle
    r.class_slope[...] = class_slope
    r.class_out[...] = class_out.astype(BF16)
    if inside:
        to_other_segment(r.class_out, r.crossed.at[me], r.l_crossed)

    def region():
        keys = n_img * rows
        wait_all(r.gains, r.l_gain.at[1])
        wait_all(r.region_up, r.l_up.at[1])
        wait_all(r.crossed, r.l_crossed.at[1])
        sibling(r.w_all.at[seg], r.w_all.at[seg], r.l_forward).wait()
        sibling(r.s_all.at[seg], r.s_all.at[seg], r.l_forward_shrink).wait()
        half = shard_ff // 2
        for j in range(n_img):
            for k in range(2):
                down = shard_ff * j + half * k
                r.region_shrink[down : down + half, :] = r.s_all[k, j]
        deep = PAD * n_img
        w_triple = r.w_all[0, :, :, 0 : 3 * width].reshape(deep, 3 * width)
        w_merge = r.w_all[0, :, :, 3 * width :].reshape(deep, width)
        w_expand = r.w_all[1].reshape(deep, hidden)
        wide = [r.gains[:, k * shard : (k + 1) * shard, :].reshape(width, 128) for k in range(2)]
        gain, regain = (jnp.concatenate([g] * (keys // 128), axis=1) for g in wide)

        slots = r.region_number.shape[1]
        per = slots // n_img
        micros = rows // per
        numbers = r.region_number[...].astype(F32)
        numbers = jnp.concatenate([numbers, jnp.zeros((8 - micros, slots), F32)], axis=0)
        at = lax.broadcasted_iota(jnp.int32, (slots, keys), 1)
        slot = lax.broadcasted_iota(jnp.int32, (slots, keys), 0)
        chosen = slot == per * (at // rows) + lax.rem(at, per)
        numbers = nn(numbers.astype(BF16), jnp.where(chosen, 1.0, 0.0).astype(BF16))
        at = lax.rem(lax.broadcasted_iota(jnp.int32, (1, keys), 1), rows) // per
        code = jnp.zeros((1, keys), F32)
        for m in range(micros):
            code = jnp.where(at == m, numbers[m : m + 1, :] * micros + m, code)
        code_down = jnp.broadcast_to(code, (128, keys)).T
        code_down = jnp.concatenate([code_down] * (keys // 128), axis=1)
        bias = jnp.where(code_down == code, 0.0, NEG)

        qkv, probs, ctx = r.qkv, r.probs, r.ctx
        values = r.crossed[...].reshape(keys, width).T.astype(F32)
        unit, _, inverse = standardize(values, 0)
        r.region_first[...] = padded(unit * gain, shard, n_img).astype(BF16)
        packed = tn(w_triple, r.region_first[...])
        qkv[0:width, 0:keys] = (packed[0:width] * (LOG2E * HD ** (-0.5))).astype(BF16)
        qkv[width:, 0:keys] = packed[width:].astype(BF16)
        mixes = []
        for h in range(heads):
            q = qkv[HD * h : HD * (h + 1), 0:keys]
            k = qkv[width + HD * h : width + HD * (h + 1), 0:keys]
            v = qkv[2 * width + HD * h : 2 * width + HD * (h + 1), 0:keys]
            scores = tn(k, q) + bias
            weights = jnp.exp2(scores - jnp.max(scores, axis=0, keepdims=True))
            share = 1.0 / jnp.sum(weights, axis=0, keepdims=True)
            low = weights.astype(BF16)
            probs[h] = low
            r.shares[0, h : h + 1, :] = share
            mixes.append(nn(v, low) * share)
        context = jnp.concatenate(mixes, axis=0)
        r.region_context[...] = padded(context, shard, n_img).astype(BF16)
        middle = values + tn(w_merge, r.region_context[...])
        unit_b, _, inverse_b = standardize(middle, 0)
        r.region_second[...] = padded(unit_b * regain, shard, n_img).astype(BF16)
        for c in range(0, hidden, width):
            at = slice(c, c + width)
            active, slope = gelu_pair(tn(w_expand[:, at], r.region_second[...]))
            r.region_active[at, :] = active.astype(BF16)
            r.slope[at, 0:keys] = slope.astype(BF16)
        result = middle + tn(r.region_shrink[...], r.region_active[...])
        mine = pl.ds(pl.multiple_of(me * rows, rows), rows)
        r.region_rows[...] = result.T
        r.region_out[...] = r.region_rows[mine, :].astype(BF16)

        upstream = r.region_up[...].reshape(keys, width).T
        for c in range(0, hidden, width):
            at = slice(c, c + width)
            active_grad = nn(r.region_shrink[at, :], upstream)
            r.active[at, 0:keys] = (active_grad * r.slope[at, 0:keys].astype(F32)).astype(BF16)
        hidden_low = r.active[:, 0:keys]
        second_grad = trimmed(nn(w_expand, hidden_low), shard, n_img)
        middle_grad = upstream.astype(F32) + norm_back(second_grad * regain, unit_b, inverse_b, 0)
        middle_low = middle_grad.astype(BF16)
        context_grad = trimmed(nn(w_merge, middle_low), shard, n_img)
        packed_grad = r.packed_grad
        for h in range(heads):
            at = slice(HD * h, HD * (h + 1))
            q = qkv[at, 0:keys]
            k = qkv[width + HD * h : width + HD * (h + 1), 0:keys]
            v = qkv[2 * width + HD * h : 2 * width + HD * (h + 1), 0:keys]
            part = context_grad[at] * r.shares[0, h : h + 1, :]
            total = jnp.sum(part * context[at], axis=0, keepdims=True)
            low = part.astype(BF16)
            weights = probs[h]
            score_grad = (weights.astype(F32) * (tn(v, low) - total)).astype(BF16)
            packed_grad[at, 0:keys] = (nn(k, score_grad) * HD ** (-0.5)).astype(BF16)
            packed_grad[width + HD * h : width + HD * (h + 1), 0:keys] = (
                nt(q, score_grad) * LN2
            ).astype(BF16)
            packed_grad[2 * width + HD * h : 2 * width + HD * (h + 1), 0:keys] = (
                nt(low, weights).astype(BF16)
            )
        first_grad = trimmed(nn(w_triple, packed_grad[:, 0:keys]), shard, n_img)
        back = norm_back(first_grad * gain, unit, inverse, 0)
        r.region_rows[...] = (middle_grad + back).T
        r.crossed_grad[...] = r.region_rows[mine, :].astype(BF16)
        sibling(r.crossed_grad, r.returned, r.l_returned).start()

        mine = pl.ds(pl.multiple_of(me * PAD, PAD), PAD)
        grads = r.grads
        grads[:, 0 : 3 * width] = nt(r.region_first[mine, :], packed_grad[:, 0:keys])[0:shard]
        grads[:, 3 * width : 4 * width] = nt(r.region_context[mine, :], middle_low)[0:shard]
        grads[:, 4 * width : 4 * width + hidden] = nt(r.region_second[mine, :], hidden_low)[0:shard]
        mine = pl.ds(pl.multiple_of(me * shard_ff, shard_ff), shard_ff)
        r.grads_shrink[...] = nt(r.region_active[mine, :], upstream)
        mine = pl.ds(pl.multiple_of(me * shard, shard), shard)
        for k, (grad, standard) in enumerate(((first_grad, unit), (second_grad, unit_b))):
            total = jnp.sum(grad * standard, axis=1, keepdims=True)
            r.gain_columns[...] = jnp.broadcast_to(total, (width, 128))
            at = 4 * width + hidden + 128 * k
            grads[:, at : at + 128] = r.gain_columns[mine, :]
        sibling(grads, r.grads_in, r.l_grads).start()
        sibling(r.grads_shrink, r.grads_shrink_in, r.l_grads_shrink).start()

    def patch_pair(it, carry):
        span = [slice(b * patches, (b + 1) * patches) for b in range(2)]
        qkv, ctx, probs = r.qkv, r.ctx, r.probs
        values = jnp.concatenate([r.tok[2 * it + b].T for b in range(2)], axis=1).astype(F32)
        first = r.firstT[it]
        queries = nn(r.tripleT[0:width, :], first) * (LOG2E * HD ** (-0.5))
        qkv[0:width, :] = queries.astype(BF16)
        qkv[width:, :] = nn(r.tripleT[width:, :], first).astype(BF16)
        for b in range(2):
            key_row = r.class_k[2 * it + b].astype(BF16)
            value_row = r.class_v[2 * it + b].astype(BF16)
            class_scores = nn(key_row, qkv[0:width, span[b]])
            mixes, class_weights, shares = [], [], []
            for h in range(heads):
                q = qkv[HD * h : HD * (h + 1), span[b]]
                k = qkv[width + HD * h : width + HD * (h + 1), span[b]]
                v = qkv[2 * width + HD * h : 2 * width + HD * (h + 1), span[b]]
                scores = tn(k, q)
                class_score = class_scores[h : h + 1, :]
                top = jnp.maximum(jnp.max(scores, axis=0, keepdims=True), class_score)
                weights = jnp.exp2(scores - top)
                class_weight = jnp.exp2(class_score - top)
                share = 1.0 / (jnp.sum(weights, axis=0, keepdims=True) + class_weight)
                low = weights.astype(BF16)
                probs[b * heads + h] = low
                mixes.append(nn(v, low))
                class_weights.append(class_weight)
                shares.append(share)
            blank = [jnp.zeros((HEADS8 - heads, patches), F32)]
            class_weights = jnp.concatenate(class_weights + blank, axis=0)
            r.class_weights[b] = class_weights
            r.shares[b] = jnp.concatenate(shares + blank, axis=0)
            from_class = tn(value_row, class_weights.astype(BF16))
            for h in range(heads):
                at = slice(HD * h, HD * (h + 1))
                ctx[at, span[b]] = ((mixes[h] + from_class[at]) * shares[h]).astype(BF16)
        middle = values + nn(r.mergeT[...], ctx[...])
        unit_b, _, inverse_b = standardize(middle, 0)
        second = (unit_b * r.regainT[...]).astype(BF16)
        chunk = width
        for c in range(0, hidden, chunk):
            at = slice(c, c + chunk)
            active, slope = gelu_pair(nn(r.expandT[at, :], second))
            r.active[at, :] = active.astype(BF16)
            r.slope[at, :] = slope.astype(BF16)
        result = middle + nn(r.shrinkT[...], r.active[...])
        for b in range(2):
            r.tok[2 * it + b] = result[:, span[b]].astype(BF16).T
        pair_copy(r.tok, r.patch_rows, r.out_sem, it).start()
        pair_copy(r.cotangent, r.cot, r.cot_sem, it).wait()
        upstream = jnp.concatenate([r.cot[2 * it + b].T for b in range(2)], axis=1)
        for c in range(0, hidden, chunk):
            at = slice(c, c + chunk)
            active_grad = nn(r.frozen_shrink[at, :], upstream)
            r.active[at, :] = active_grad.astype(BF16) * r.slope[at, :]
        second_grad = nn(r.frozen_expand[...], r.active[...])
        middle_grad = upstream.astype(F32) + norm_back(
            second_grad * r.regainT[...], unit_b, inverse_b, 0
        )
        context_grad = nn(r.frozen_merge[...], middle_grad.astype(BF16))
        low_grad, packed_grad = r.low_grad, r.packed_grad
        for b in range(2):
            key_row = r.class_k[2 * it + b].astype(BF16)
            value_row = r.class_v[2 * it + b].astype(BF16)
            totals = []
            for h in range(heads):
                at = slice(HD * h, HD * (h + 1))
                part = context_grad[at, span[b]] * r.shares[b][h : h + 1, :]
                totals.append(
                    jnp.sum(part * ctx[at, span[b]].astype(F32), axis=0, keepdims=True)
                )
                low_grad[at, span[b]] = part.astype(BF16)
            blank = [jnp.zeros((HEADS8 - heads, patches), F32)]
            all_low = low_grad[:, span[b]]
            class_weights = r.class_weights[b]
            class_grad = class_weights * (
                nn(value_row, all_low) - jnp.concatenate(totals + blank, axis=0)
            )
            class_grad = class_grad.astype(BF16)
            from_class = tn(key_row, class_grad)
            dk = nt(class_grad, qkv[0:width, span[b]]) * LN2
            dv = nt(class_weights.astype(BF16), all_low)
            r.class_dk[2 * it + b] = jnp.where(block_head, dk, 0.0)
            r.class_dv[2 * it + b] = jnp.where(block_head, dv, 0.0)
            for h in range(heads):
                at = slice(HD * h, HD * (h + 1))
                q = qkv[at, span[b]]
                k = qkv[width + HD * h : width + HD * (h + 1), span[b]]
                v = qkv[2 * width + HD * h : 2 * width + HD * (h + 1), span[b]]
                low = low_grad[at, span[b]]
                weights = probs[b * heads + h]
                score_grad = weights * (tn(v, low) - totals[h]).astype(BF16)
                value_grad = nt(low, weights)
                key_grad = nt(q, score_grad) * LN2
                query_grad = (nn(k, score_grad) + from_class[at]) * HD ** (-0.5)
                packed_grad[at, span[b]] = query_grad.astype(BF16)
                packed_grad[width + HD * h : width + HD * (h + 1), span[b]] = key_grad.astype(BF16)
                packed_grad[2 * width + HD * h : 2 * width + HD * (h + 1), span[b]] = (
                    value_grad.astype(BF16)
                )
        first_grad = nn(r.frozen_triple[...], packed_grad[...])
        centre, inverse = r.stat[it, 0:1, :], r.stat[it, 1:2, :]
        unit = (values - centre) * inverse
        back = norm_back(first_grad * r.gainT[...], unit, inverse, 0)
        r.input_grad[it] = (middle_grad + back).astype(BF16)

        pltpu.make_async_copy(r.input_grad.at[it], r.grad_rows.at[it], r.grad_sem.at[it]).start()

        if inside:

            @pl.when(it == AT_FORWARD)
            def _():
                wait_all(r.w_all.at[seg], r.l_weights.at[1])
                wait_all(r.s_all.at[seg], r.l_shrink.at[1])
                sibling(r.w_all.at[seg], r.w_all.at[seg], r.l_forward).start()
                sibling(r.s_all.at[seg], r.s_all.at[seg], r.l_forward_shrink).start()

            pl.when(it == AT_REGION)(region)
        return carry

    for it in range(pairs):
        pltpu.make_async_copy(r.firstT.at[it], r.first_rows.at[it], r.first_sem.at[it]).start()
    lax.fori_loop(0, pairs, patch_pair, 0)

    r.class_grads[:, 0:width] = jnp.sum(r.class_dk[...], axis=1)
    r.class_grads[:, width:] = jnp.sum(r.class_dv[...], axis=1)
    if inside:
        sibling(r.crossed_grad, r.returned, r.l_returned).wait()
        sibling(r.grads, r.grads_in, r.l_grads).wait()
        sibling(r.grads_shrink, r.grads_shrink_in, r.l_grads_shrink).wait()
        r.class_up[...] = r.returned[...]
        r.grads_out[...] = r.grads[...] + r.grads_in[...]
        r.shrink_out[...] = r.grads_shrink[...] + r.grads_shrink_in[...]
        peers = pl.ds(0, n_img - 1)
        wait_all(r.gains.at[peers], r.l_gain.at[0])
        wait_all(r.region_up.at[peers], r.l_up.at[0])
        wait_all(r.w_all.at[0, peers], r.l_weights.at[0])
        wait_all(r.s_all.at[0, peers], r.l_shrink.at[0])
        wait_all(r.crossed, r.l_crossed.at[0])
    for it in range(pairs):
        pair_copy(r.tok, r.patch_rows, r.out_sem, it).wait()
        pltpu.make_async_copy(r.firstT.at[it], r.first_rows.at[it], r.first_sem.at[it]).wait()
        pltpu.make_async_copy(r.input_grad.at[it], r.grad_rows.at[it], r.grad_sem.at[it]).wait()


def class_kernel(dims, *refs):
    r = SimpleNamespace(**dict(zip(dims.names, refs, strict=True)))
    width = dims.width
    rows, patches = dims.images, dims.patches
    pairs, lanes = rows // 2, 2 * patches
    it = pl.program_id(0)
    gain_row = wide_row(r.vectors[...], 0, width // 128)
    regain_row = wide_row(r.vectors[...], width // 128, width // 128)

    @pl.when(it == 0)
    def _():
        r.gainT[...] = column(gain_row, lanes)
        r.ungainT[...] = 1.0 / r.gainT[...]
        upstream = r.class_up[...]
        middle = r.class_middle[...]
        unit, _, inverse = standardize(middle, 1)
        hidden_low = (nt(upstream, r.frozen_shrink[...]) * r.class_slope[...]).astype(BF16)
        second_grad = nt(hidden_low, r.frozen_expand[...])
        middle_grad = upstream.astype(F32) + norm_back(second_grad * regain_row, unit, inverse, 1)
        r.middle_grad[...] = middle_grad
        low = nt(middle_grad.astype(BF16), r.frozen_merge[...]).astype(BF16).astype(F32)
        r.class_low[...] = low
        low_map = nt(spread(low).astype(BF16), r.frozen_triple[:, 2 * width :])
        r.low_map[...] = low_map.reshape(rows, HEADS8, width)
        total = jnp.sum(spread(low * r.class_context[...]), axis=1, keepdims=True)
        r.class_total[...] = jnp.broadcast_to(total, (rows * HEADS8, 128)).reshape(
            rows, HEADS8, 128
        )

    first = r.first_rows[0]
    maps = jnp.concatenate([r.low_map[2 * it + b] for b in range(2)], axis=0)
    probs_grads = nn(maps.astype(BF16), first)
    corrections = []
    for b in range(2):
        image = 2 * it + b
        own_first = first[:, b * patches : (b + 1) * patches]
        part = probs_grads[b * HEADS8 : (b + 1) * HEADS8, b * patches : (b + 1) * patches]
        weights = r.class_probs[b]
        score_grad = weights * (part - r.class_total[image][:, 0:1])
        r.mixed[image] = nt(score_grad.astype(BF16), own_first)
        left = jnp.concatenate([r.query_map[b], r.low_map[image]], axis=0)
        right = jnp.concatenate([score_grad * LN2, weights], axis=0)
        corrections.append(tn(left.astype(BF16), right.astype(BF16)))
    correction = jnp.concatenate(corrections, axis=1)
    inverse = r.stat[0, 1:2, :]
    scaled = correction * r.gainT[...]
    firsts = first.astype(F32)
    along = mean(correction * firsts, 0)
    back = inverse * (scaled - mean(scaled, 0) - firsts * r.ungainT[...] * along)
    result = r.grad_rows[0].astype(F32) + back
    for b in range(2):
        r.patch_gradient[b] = result[:, b * patches : (b + 1) * patches].astype(BF16).T
    r.patch_output[...] = r.patch_rows[...]

    @pl.when(it == pairs - 1)
    def _():
        low = r.class_low[...]
        packed = r.class_packed[...]
        tall_low = spread(low)
        total = r.class_total[...].reshape(rows * HEADS8, 128)[:, 0:1]
        self_prob = r.self_prob[...].reshape(rows * HEADS8, 128)[:, 0:1]
        tall_q = spread(packed[:, 0:width])
        tall_v = spread(packed[:, 2 * width :])
        self_grad = self_prob * (jnp.sum(tall_low * tall_v, axis=1, keepdims=True) - total)
        unit, _, inverse = standardize(r.class_tokens[...].astype(F32), 1)
        first = (unit * gain_row).astype(BF16).astype(F32)
        firsts = jnp.broadcast_to(first[:, None, :], (rows, HEADS8, width))
        mixed = r.mixed[...].reshape(rows * HEADS8, width)
        mixed = mixed + self_grad * firsts.reshape(rows * HEADS8, width)
        triple = r.frozen_triple
        query_grad = gather_heads(nn(mixed.astype(BF16), triple[:, width : 2 * width]))
        key_grad = jnp.sum((tall_q * self_grad).reshape(rows, HEADS8, width), axis=1)
        value_grad = jnp.sum((tall_low * self_prob).reshape(rows, HEADS8, width), axis=1)
        packed_grad = jnp.concatenate(
            [
                query_grad * HD ** (-0.5),
                r.class_grads[:, 0:width] + key_grad * HD ** (-0.5),
                r.class_grads[:, width:] + value_grad,
            ],
            axis=1,
        ).astype(BF16)
        first_grad = nt(packed_grad, triple[...])
        back = norm_back(first_grad * gain_row, unit, inverse, 1)
        r.class_gradient[...] = (r.middle_grad[...] + back).astype(BF16)
        if dims.inside:
            wide = width * 4 + dims.hidden
            r.region_output[...] = r.region_out[...]
            r.triple_gradient[...] = r.grads_out[:, 0 : 3 * width]
            r.merge_gradient[...] = r.grads_out[:, 3 * width : 4 * width]
            r.expand_gradient[...] = r.grads_out[:, 4 * width : wide]
            r.shrink_gradient[...] = r.shrink_out[...]
            shard = r.grads_out.shape[0]
            blank = jnp.zeros((128 - shard, 128), F32)
            for k, target in enumerate((r.first_gradient, r.second_gradient)):
                columns = r.grads_out[:, wide + 128 * k : wide + 128 * (k + 1)]
                columns = jnp.concatenate([columns, blank], axis=0).T
                target[...] = columns[0:1, 0:shard]


def normalize(values, scaling):
    centred = values - jnp.mean(values, axis=-1, keepdims=True)
    inverse = lax.rsqrt(jnp.mean(centred * centred, axis=-1, keepdims=True) + EPSILON)
    standard = centred * inverse
    return (standard * scaling, standard, inverse)


def normalize_back(upstream, standard, inverse, scaling):
    scaled = upstream * scaling
    centred = scaled - jnp.mean(scaled, axis=-1, keepdims=True)
    centred = centred - standard * jnp.mean(scaled * standard, axis=-1, keepdims=True)
    gain_grad = jnp.sum((upstream * standard).reshape(-1, upstream.shape[-1]), axis=0)
    return (centred * inverse, gain_grad)


def gelu_slope(hidden):
    return (
        0.5 * (1.0 + lax.erf(hidden * 0.7071067811865476))
        + hidden * jnp.exp(-0.5 * hidden * hidden) * 0.3989422804014327
    )


def forward_product(operand, weight):
    return lax.dot_general(
        operand, weight, (((operand.ndim - 1,), (0,)), ((), ())), preferred_element_type=F32
    )


def backward_product(upstream, weight):
    return lax.dot_general(
        upstream,
        weight,
        (((upstream.ndim - 1,), (1,)), ((), ())),
        preferred_element_type=F32,
    )


def row_product(operand, cotangent):
    left_rows = operand.reshape(-1, operand.shape[-1])
    right_rows = cotangent.reshape(-1, cotangent.shape[-1])
    return lax.dot_general(
        left_rows, right_rows, (((0,), (0,)), ((), ())), preferred_element_type=F32
    )


def heads_of(packed, portion):
    section_width = packed.shape[-1] // 3
    section = packed[..., portion * section_width : (portion + 1) * section_width]
    return section.reshape(packed.shape[:-1] + (section_width // HD, HD))


def raw_scores(queries, keyset, allowed):
    scores = jnp.einsum(
        "bqhd,bkhd->bhqk", queries, keyset, preferred_element_type=F32
    ) * HD ** (-0.5)
    if allowed is None:
        return scores
    return jnp.where(allowed[:, None], scores, -1e30)


def attend(queries, keyset, valueset, allowed):
    scores = raw_scores(queries, keyset, allowed)
    highest = jnp.max(scores, axis=-1, keepdims=True)
    logsum = highest + jnp.log(jnp.sum(jnp.exp(scores - highest), axis=-1, keepdims=True))
    weighting = jnp.exp(scores - logsum).astype(BF16)
    context = jnp.einsum("bhqk,bkhd->bqhd", weighting, valueset, preferred_element_type=F32)
    return (context.astype(BF16), logsum)


def score_terms(queries, keyset, valueset, allowed, logsum, context_grad):
    scores = raw_scores(queries, keyset, allowed)
    weighting = jnp.exp(scores - logsum)
    weight_grad = jnp.einsum(
        "bqhd,bkhd->bhqk", context_grad, valueset, preferred_element_type=F32
    )
    row_total = jnp.sum(weighting * weight_grad, axis=-1, keepdims=True)
    score_grad = (weighting * (weight_grad - row_total)).astype(BF16)
    return (weighting, score_grad, row_total)


def attend_back(queries, keyset, valueset, allowed, logsum, context_grad):
    weighting, score_grad, row_total = score_terms(
        queries, keyset, valueset, allowed, logsum, context_grad
    )
    value_grad = jnp.einsum(
        "bhqk,bqhd->bkhd",
        weighting.astype(BF16),
        context_grad,
        preferred_element_type=F32,
    )
    query_grad = jnp.einsum(
        "bhqk,bkhd->bqhd", score_grad, keyset, preferred_element_type=F32
    ) * HD ** (-0.5)
    key_grad = jnp.einsum(
        "bhqk,bqhd->bkhd", score_grad, queries, preferred_element_type=F32
    ) * HD ** (-0.5)
    return (query_grad, key_grad, value_grad)


def block_head(inputs, scaling, triple):
    normed, standard, inverse = normalize(inputs, scaling)
    first_low = normed.astype(BF16)
    packed = forward_product(first_low, triple).astype(BF16)
    return (first_low, standard, inverse, packed)


def block_tail(inputs, context, regain, merger, expand, shrink):
    middle = inputs + forward_product(context, merger)
    normed, standard, inverse = normalize(middle, regain)
    second = normed.astype(BF16)
    hidden = forward_product(second, expand)
    active = jax.nn.gelu(hidden, approximate=False).astype(BF16)
    result = middle + forward_product(active, shrink)
    return (result, (standard, inverse, second, hidden, active))


def tail_back(upstream, kept_tail, regain, merger, expand, shrink):
    standard, inverse, second, hidden, active = kept_tail
    out_low = upstream.astype(BF16)
    active_grad = backward_product(out_low, shrink)
    hidden_low = (active_grad * gelu_slope(hidden)).astype(BF16)
    second_grad = backward_product(hidden_low, expand)
    norm_grad, regain_grad = normalize_back(second_grad, standard, inverse, regain)
    middle_grad = upstream + norm_grad
    middle_low = middle_grad.astype(BF16)
    context_low = backward_product(middle_low, merger).astype(BF16)
    return (middle_grad, context_low, regain_grad, (middle_low, hidden_low, out_low))


def region_outside(crossed, region_number, region_cotangent, shards_in):
    crossed = lax.ppermute(crossed, SEG, [(0, 1), (1, 0)])
    images = crossed.shape[1]
    model_width = crossed.shape[2]
    gathered = [lax.all_gather(shard, IMG, axis=0, tiled=True) for shard in shards_in]
    full_gain, triple, merger, full_regain, expand, shrink = gathered
    scaling = full_gain.astype(F32)
    regain = full_regain.astype(F32)
    region_in = crossed.astype(F32)
    first_low, standard, inverse, packed = block_head(region_in, scaling, triple)
    local_keys = packed[..., model_width : 2 * model_width]
    local_values = packed[..., 2 * model_width :]
    all_keys, all_values = (
        lax.all_gather(local_keys, IMG, axis=1, tiled=True),
        lax.all_gather(local_values, IMG, axis=1, tiled=True),
    )
    head_shape = all_keys.shape[:-1] + (model_width // HD, HD)
    keyset = all_keys.reshape(head_shape)
    valueset = all_values.reshape(head_shape)
    queries = heads_of(packed, 0)
    first_slot = lax.axis_index(IMG) * images
    own_number = lax.dynamic_slice_in_dim(region_number, first_slot, images, 1)
    allowed = own_number[:, :, None] == region_number[:, None, :]
    context, logsum = attend(queries, keyset, valueset, allowed)
    context = context.reshape(region_in.shape)
    region_result, kept_tail = block_tail(region_in, context, regain, merger, expand, shrink)
    region_output = region_result.astype(BF16)
    upstream = region_cotangent.astype(F32)
    middle_grad, context_low, second_gain_grad, low_rows = tail_back(
        upstream, kept_tail, regain, merger, expand, shrink
    )
    middle_low, hidden_low, out_low = low_rows
    context_heads = context_low.reshape(queries.shape)
    query_grad, key_grad, value_grad = attend_back(
        queries, keyset, valueset, allowed, logsum, context_heads
    )
    key_sum, value_sum = (
        lax.psum_scatter(key_grad.reshape(all_keys.shape), IMG, scatter_dimension=1, tiled=True),
        lax.psum_scatter(
            value_grad.reshape(all_values.shape), IMG, scatter_dimension=1, tiled=True
        ),
    )
    packed_grad = jnp.concatenate(
        [query_grad.reshape(region_in.shape), key_sum, value_sum], axis=-1
    ).astype(BF16)
    norm_grad, first_gain_grad = normalize_back(
        backward_product(packed_grad, triple), standard, inverse, scaling
    )
    input_grad = (middle_grad + norm_grad).astype(BF16)
    second_low = kept_tail[2]
    active_low = kept_tail[4]
    shards = (
        lax.psum_scatter(first_gain_grad, IMG, scatter_dimension=0, tiled=True),
        lax.psum_scatter(
            row_product(first_low, packed_grad), IMG, scatter_dimension=0, tiled=True
        ),
        lax.psum_scatter(row_product(context, middle_low), IMG, scatter_dimension=0, tiled=True),
        lax.psum_scatter(second_gain_grad, IMG, scatter_dimension=0, tiled=True),
        lax.psum_scatter(
            row_product(second_low, hidden_low), IMG, scatter_dimension=0, tiled=True
        ),
        lax.psum_scatter(row_product(active_low, out_low), IMG, scatter_dimension=0, tiled=True),
    )
    totals = tuple(lax.psum(shard.astype(BF16), SEG).astype(F32) for shard in shards)
    return region_output, lax.ppermute(input_grad, SEG, [(0, 1), (1, 0)]), totals


def local(
    n_img,
    patch_tokens,
    class_tokens,
    region_number,
    frozen_gain,
    frozen_triple,
    frozen_merge,
    frozen_regain,
    frozen_expand,
    frozen_shrink,
    gain_first,
    weight_triple,
    weight_merge,
    gain_second,
    weight_expand,
    weight_shrink,
    patch_cotangent,
    region_cotangent,
):
    micros, per, patches, width = patch_tokens.shape
    hidden = frozen_expand.shape[1]
    images = micros * per
    shard, shard_ff = width // n_img, hidden // n_img
    lanes, pairs, keys, heads = 2 * patches, images // 2, n_img * images, width // HD
    inside = keys == patches and shard % 8 == 0 and shard <= PAD

    vectors = [frozen_gain, frozen_regain]
    if inside:
        vectors += [jnp.pad(g, (0, 128 - shard)) for g in (gain_first, gain_second)]
    vectors = jnp.concatenate(vectors)
    vectors = jnp.pad(vectors, (0, 1024 - vectors.shape[0])).astype(F32).reshape(8, 128)
    class_rows = class_tokens.reshape(images, width)
    inputs = dict(
        tokens=patch_tokens.reshape(images, patches, width),
        cotangent=patch_cotangent.reshape(images, patches, width),
        class_tokens=class_rows,
        vectors=vectors,
        frozen_triple=frozen_triple,
        frozen_merge=frozen_merge,
        frozen_expand=frozen_expand,
        frozen_shrink=frozen_shrink,
    )
    if inside:
        inputs |= dict(
            region_cotangent=region_cotangent.reshape(images, width),
            region_number=region_number,
            weight_triple=weight_triple,
            weight_merge=weight_merge,
            weight_expand=weight_expand,
            weight_shrink=weight_shrink,
        )
    vmem = pl.BlockSpec(memory_space=pltpu.VMEM)
    hbm = pl.BlockSpec(memory_space=pl.ANY)
    streams = 2
    in_specs = [hbm] * streams + [vmem] * (len(inputs) - streams)

    shape = jax.ShapeDtypeStruct
    columns = 4 * width + hidden + 256
    large = dict(
        patch_rows=shape((images, patches, width), BF16),
        first_rows=shape((pairs, width, lanes), BF16),
        grad_rows=shape((pairs, width, lanes), BF16),
    )
    small = dict(
        stat=shape((pairs, 8, lanes), F32),
        class_packed=shape((images, 3 * width), F32),
        class_context=shape((images, width), F32),
        class_middle=shape((images, width), F32),
        class_slope=shape((images, hidden), F32),
        query_map=shape((images, HEADS8, width), F32),
        class_probs=shape((images, HEADS8, patches), F32),
        self_prob=shape((images, HEADS8, 128), F32),
        class_grads=shape((images, 2 * width), F32),
    )
    if inside:
        small |= dict(
            class_up=shape((images, width), BF16),
            region_out=shape((images, width), BF16),
            grads_out=shape((shard, columns), F32),
            shrink_out=shape((shard_ff, width), F32),
        )
    else:
        small |= dict(class_out=shape((images, width), BF16))
    outputs = large | small
    out_specs = [hbm] * len(large) + [vmem] * len(small)

    v = pltpu.VMEM
    dma = pltpu.SemaphoreType.DMA
    scratch = dict(
        tok=v((images, patches, width), BF16),
        cot=v((images, patches, width), BF16),
        firstT=v((pairs, width, lanes), BF16),
        input_grad=v((pairs, width, lanes), BF16),
        tripleT=v((3 * width, width), BF16),
        mergeT=v((width, width), BF16),
        expandT=v((hidden, width), BF16),
        shrinkT=v((width, hidden), BF16),
        gainT=v((width, lanes), F32),
        regainT=v((width, lanes), F32),
        qkv=v((3 * width, lanes), BF16),
        ctx=v((width, lanes), BF16),
        probs=v((2 * heads, patches, patches), BF16),
        shares=v((2, HEADS8, patches), F32),
        class_weights=v((2, HEADS8, patches), F32),
        active=v((hidden, lanes), BF16),
        slope=v((hidden, lanes), BF16),
        packed_grad=v((3 * width, lanes), BF16),
        low_grad=v((width, lanes), BF16),
        class_k=v((images, HEADS8, width), F32),
        class_v=v((images, HEADS8, width), F32),
        class_dk=v((images, HEADS8, width), F32),
        class_dv=v((images, HEADS8, width), F32),
        class_first=v((images, HEADS8, width), F32),
        mixed=v((images, HEADS8, width), F32),
        self_score=v((images, HEADS8, 128), F32),
        tok_sem=dma((pairs,)),
        cot_sem=dma((pairs,)),
        out_sem=dma((pairs,)),
        first_sem=dma((pairs,)),
        grad_sem=dma((pairs,)),
    )
    if inside:
        deep = PAD * n_img
        scratch |= dict(
            class_out=v((images, width), BF16),
            crossed=v((n_img, images, width), BF16),
            crossed_grad=v((images, width), BF16),
            returned=v((images, width), BF16),
            region_up=v((n_img, images, width), BF16),
            gain_own=v((2 * shard, 128), F32),
            gains=v((n_img, 2 * shard, 128), F32),
            w_own=v((2, PAD, 4 * width), BF16),
            w_all=v((2, n_img, PAD, 4 * width), BF16),
            s_own=v((2, shard_ff // 2, width), BF16),
            s_all=v((2, n_img, shard_ff // 2, width), BF16),
            region_shrink=v((hidden, width), BF16),
            region_first=v((deep, keys), BF16),
            region_context=v((deep, keys), BF16),
            region_second=v((deep, keys), BF16),
            region_active=v((hidden, keys), BF16),
            region_rows=v((keys, width), F32),
            gain_columns=v((width, 128), F32),
            grads=v((shard, columns), F32),
            grads_in=v((shard, columns), F32),
            grads_shrink=v((shard_ff, width), F32),
            grads_shrink_in=v((shard_ff, width), F32),
            l_gain=dma((2,)),
            l_up=dma((2,)),
            l_weights=dma((2,)),
            l_shrink=dma((2,)),
            l_forward=dma((2,)),
            l_forward_shrink=dma((2,)),
            l_crossed=dma((2,)),
            l_returned=dma((2,)),
            l_grads=dma((2,)),
            l_grads_shrink=dma((2,)),
        )
    sizes = dict(
        n_img=n_img, width=width, hidden=hidden, images=images, patches=patches, inside=inside
    )
    limit = dict(vmem_limit_bytes=60 * 1024 * 1024)
    remote = dict(collective_id=0, has_side_effects=True) if inside else {}
    names = list(inputs) + list(outputs) + list(scratch)
    results = pl.pallas_call(
        functools.partial(patch_kernel, SimpleNamespace(names=names, **sizes)),
        out_shape=list(outputs.values()),
        in_specs=in_specs,
        out_specs=out_specs,
        scratch_shapes=list(scratch.values()),
        compiler_params=pltpu.CompilerParams(**limit, **remote),
    )(*inputs.values())
    done = dict(zip(outputs, results, strict=True))

    if not inside:
        class_out = done.pop(list(small)[-1])
        region_output, class_up, grads = region_outside(
            class_out.reshape(class_tokens.shape),
            region_number,
            region_cotangent,
            (gain_first, weight_triple, weight_merge, gain_second, weight_expand, weight_shrink),
        )
        done |= dict(class_up=class_up.reshape(images, width))

    def step(*block):
        return pl.BlockSpec(block, lambda it: (it,) + (0,) * (len(block) - 1))

    specs = dict(
        patch_rows=step(2, patches, width),
        first_rows=step(1, width, lanes),
        grad_rows=step(1, width, lanes),
        stat=step(1, 8, lanes),
        query_map=step(2, HEADS8, width),
        class_probs=step(2, HEADS8, patches),
    )
    inputs = done | dict(
        class_tokens=class_rows,
        vectors=vectors,
        frozen_triple=frozen_triple,
        frozen_merge=frozen_merge,
        frozen_expand=frozen_expand,
        frozen_shrink=frozen_shrink,
    )
    outputs = dict(
        patch_output=shape((images, patches, width), BF16),
        patch_gradient=shape((images, patches, width), BF16),
        class_gradient=shape((images, width), BF16),
    )
    out_specs = [step(2, patches, width)] * 2 + [vmem]
    if inside:
        ready = dict(
            region_output=shape((images, width), BF16),
            first_gradient=shape((1, shard), F32),
            triple_gradient=shape((shard, 3 * width), F32),
            merge_gradient=shape((shard, width), F32),
            second_gradient=shape((1, shard), F32),
            expand_gradient=shape((shard, hidden), F32),
            shrink_gradient=shape((shard_ff, width), F32),
        )
        outputs |= ready
        out_specs += [vmem] * len(ready)
    scratch = dict(
        gainT=v((width, lanes), F32),
        ungainT=v((width, lanes), F32),
        middle_grad=v((images, width), F32),
        class_low=v((images, width), F32),
        low_map=v((images, HEADS8, width), F32),
        class_total=v((images, HEADS8, 128), F32),
        mixed=v((images, HEADS8, width), F32),
    )
    names = list(inputs) + list(outputs) + list(scratch)
    results = pl.pallas_call(
        functools.partial(class_kernel, SimpleNamespace(names=names, **sizes)),
        grid=(pairs,),
        out_shape=list(outputs.values()),
        in_specs=[specs.get(name, vmem) for name in inputs],
        out_specs=out_specs,
        scratch_shapes=list(scratch.values()),
        compiler_params=pltpu.CompilerParams(**limit),
    )(*inputs.values())
    done = SimpleNamespace(**dict(zip(outputs, results, strict=True)))
    if inside:
        region_output = done.region_output.reshape(class_tokens.shape)
        grads = (
            done.first_gradient.reshape(shard),
            done.triple_gradient,
            done.merge_gradient,
            done.second_gradient.reshape(shard),
            done.expand_gradient,
            done.shrink_gradient,
        )
    return (
        done.patch_output.reshape(patch_tokens.shape),
        region_output,
        done.patch_gradient.reshape(patch_tokens.shape),
        done.class_gradient.reshape(class_tokens.shape),
        *grads,
    )


def solution(mesh):
    patch, row = P(SEG, IMG, None, None), P(SEG, IMG, None)
    gain, weight, whole = P(IMG), P(IMG, None), P()
    block = (gain, weight, weight, gain, weight, weight)
    placed = (patch, row, P(SEG, None)) + (whole,) * 6 + block + (patch, row)
    return jax.shard_map(
        functools.partial(local, mesh.shape[IMG]),
        mesh=mesh,
        in_specs=placed,
        out_specs=(patch, row, patch, row) + block,
        check_vma=False,
    )
```

```python
import functools
from types import SimpleNamespace

import jax
import jax.numpy as jnp
from jax import lax
from jax.experimental import pallas as pl
from jax.experimental.pallas import tpu as pltpu
from jax.sharding import PartitionSpec as P

SEG = "segment"
IMG = "img"
HD = 64
HEADS8 = 8
EPSILON = 1e-06
LOG2E = 1.4426950408889634
LN2 = 0.6931471805599453
ROOT_HALF = 0.7071067811865476
DENSITY = 0.3989422804014327
F32 = jnp.float32
BF16 = jnp.bfloat16
MESH = pl.DeviceIdType.MESH
NEG = -1e30
PAD = 32
BESIDE = "_"

AT_FORWARD = 5
AT_REGION = 6
LATE = 1


def nn(a, b):
    return lax.dot_general(a, b, (((1,), (0,)), ((), ())), preferred_element_type=F32)


def nt(a, b):
    return lax.dot_general(a, b, (((1,), (1,)), ((), ())), preferred_element_type=F32)


def tn(a, b):
    return lax.dot_general(a, b, (((0,), (0,)), ((), ())), preferred_element_type=F32)


def mean(values, axis):
    return jnp.sum(values, axis=axis, keepdims=True) * (1.0 / values.shape[axis])


def standardize(values, axis):
    centre = mean(values, axis)
    centred = values - centre
    inverse = lax.rsqrt(mean(centred * centred, axis) + EPSILON)
    return centred * inverse, centre, inverse


def norm_back(scaled, standard, inverse, axis):
    return inverse * (
        scaled - mean(scaled, axis) - standard * mean(scaled * standard, axis)
    )


def gelu_pair(hidden):
    upto = 0.5 + 0.5 * lax.erf(hidden * ROOT_HALF)
    bell = jnp.exp2(hidden * hidden * (-0.5 * LOG2E))
    return hidden * upto, upto + hidden * (bell * DENSITY)


def own_heads(rows, width):
    shape = (rows * HEADS8, width)
    lane = lax.broadcasted_iota(jnp.int32, shape, 1) // HD
    return lane == lax.rem(lax.broadcasted_iota(jnp.int32, shape, 0), HEADS8)


def spread(values):
    rows, width = values.shape
    tall = jnp.broadcast_to(values[:, None, :], (rows, HEADS8, width))
    return jnp.where(own_heads(rows, width), tall.reshape(rows * HEADS8, width), 0.0)


def gather_heads(values):
    tall, width = values.shape
    kept = jnp.where(own_heads(tall // HEADS8, width), values, 0.0)
    return jnp.sum(kept.reshape(tall // HEADS8, HEADS8, width), axis=1)


def wide_row(vectors, first, count):
    return jnp.concatenate([vectors[k : k + 1, :] for k in range(first, first + count)], axis=1)


def column(row, lanes):
    tall = jnp.broadcast_to(row, (128, row.shape[1])).T
    return jnp.concatenate([tall] * (lanes // 128), axis=1)


def pair_copy(source, target, sems, it):
    part = pl.ds(2 * it, 2)
    return pltpu.make_async_copy(source.at[part], target.at[part], sems.at[it])


def one_copy(source, target, sems, it):
    return pltpu.make_async_copy(source.at[it], target.at[it], sems.at[it])


def padded(values, shard, n):
    blank = jnp.zeros((PAD - shard, values.shape[1]), values.dtype)
    parts = []
    for j in range(n):
        parts += [values[shard * j : shard * (j + 1)], blank]
    return jnp.concatenate(parts, axis=0)


def trimmed(values, shard, n):
    return jnp.concatenate([values[PAD * j : PAD * j + shard] for j in range(n)], axis=0)


def patch_pair(r, dims, it, slot, ready=lambda stage: None):
    width, hidden, patches = dims.width, dims.hidden, dims.patches
    heads = width // HD
    block_head = own_heads(1, width)
    span = [slice(b * patches, (b + 1) * patches) for b in range(2)]
    qkv, ctx, probs = r.qkv, r.ctx, r.probs
    values = jnp.concatenate([r.tok[2 * slot + b].T for b in range(2)], axis=1).astype(F32)
    ready(0)
    first = r.firstT[it]
    queries = nn(r.tripleT[0:width, :], first) * (LOG2E * HD ** (-0.5))
    qkv[0:width, :] = queries.astype(BF16)
    qkv[width:, :] = nn(r.tripleT[width:, :], first).astype(BF16)
    order = [(b, h) for h in range(heads) for b in range(2)]
    key_rows = [r.class_k[2 * it + b].astype(BF16) for b in range(2)]
    value_rows = [r.class_v[2 * it + b].astype(BF16) for b in range(2)]
    class_scores = [nn(key_rows[b], qkv[0:width, span[b]]) for b in range(2)]

    def part(which, turn):
        b, h = order[turn]
        return qkv[which * width + HD * h : which * width + HD * (h + 1), span[b]]

    scores, mixes, class_weights, shares = {0: tn(part(1, 0), part(0, 0))}, [], [], []
    for turn, (b, h) in enumerate(order):
        if turn + 1 < len(order):
            scores[turn + 1] = tn(part(1, turn + 1), part(0, turn + 1))
        class_score = class_scores[b][h : h + 1, :]
        top = jnp.maximum(jnp.max(scores[turn], axis=0, keepdims=True), class_score)
        weights = jnp.exp2(scores.pop(turn) - top)
        class_weight = jnp.exp2(class_score - top)
        shares.append(1.0 / (jnp.sum(weights, axis=0, keepdims=True) + class_weight))
        class_weights.append(class_weight)
        probs[b * heads + h] = weights.astype(BF16)
        if turn:
            last = order[turn - 1]
            mixes.append(nn(part(2, turn - 1), probs[last[0] * heads + last[1]]))
    mixes.append(nn(part(2, len(order) - 1), probs[2 * heads - 1]))
    blank = [jnp.zeros((HEADS8 - heads, patches), F32)]
    for b in range(2):
        weights = jnp.concatenate(class_weights[b::2] + blank, axis=0)
        r.class_weights[b] = weights
        r.shares[b] = jnp.concatenate(shares[b::2] + blank, axis=0)
        from_class = tn(value_rows[b], weights.astype(BF16))
        for h in range(heads):
            at = slice(HD * h, HD * (h + 1))
            mix = mixes[2 * h + b] + from_class[at]
            ctx[at, span[b]] = (mix * shares[2 * h + b]).astype(BF16)
    ready(1)
    middle = values + nn(r.mergeT[...], ctx[...])
    unit_b, _, inverse_b = standardize(middle, 0)
    second = (unit_b * r.regainT[...]).astype(BF16)
    chunk = width
    for c in range(0, hidden, chunk):
        at = slice(c, c + chunk)
        active, slope = gelu_pair(nn(r.expandT[at, :], second))
        r.active[at, :] = active.astype(BF16)
        r.slope[at, :] = slope.astype(BF16)
    result = middle + nn(r.shrinkT[...], r.active[...])
    for b in range(2):
        r.tok[2 * slot + b] = result[:, span[b]].astype(BF16).T
    ready(2)
    upstream = jnp.concatenate([r.cot[2 * slot + b].T for b in range(2)], axis=1)
    for c in range(0, hidden, chunk):
        at = slice(c, c + chunk)
        active_grad = nn(r.frozen_shrink[at, :], upstream)
        r.active[at, :] = active_grad.astype(BF16) * r.slope[at, :]
    second_grad = nn(r.frozen_expand[...], r.active[...])
    middle_grad = upstream.astype(F32) + norm_back(
        second_grad * r.regainT[...], unit_b, inverse_b, 0
    )
    context_grad = nn(r.frozen_merge[...], middle_grad.astype(BF16))
    low_grad, packed_grad = r.low_grad, r.packed_grad
    totals, from_class = [[], []], []
    for b in range(2):
        for h in range(heads):
            at = slice(HD * h, HD * (h + 1))
            low = context_grad[at, span[b]] * r.shares[b][h : h + 1, :]
            totals[b].append(
                jnp.sum(low * ctx[at, span[b]].astype(F32), axis=0, keepdims=True)
            )
            low_grad[at, span[b]] = low.astype(BF16)
        all_low = low_grad[:, span[b]]
        weights = r.class_weights[b]
        class_grad = weights * (
            nn(value_rows[b], all_low) - jnp.concatenate(totals[b] + blank, axis=0)
        )
        class_grad = class_grad.astype(BF16)
        from_class.append(tn(key_rows[b], class_grad))
        dk = nt(class_grad, qkv[0:width, span[b]]) * LN2
        dv = nt(weights.astype(BF16), all_low)
        r.class_dk[2 * it + b] = jnp.where(block_head, dk, 0.0)
        r.class_dv[2 * it + b] = jnp.where(block_head, dv, 0.0)

    def low_part(turn):
        b, h = order[turn]
        return low_grad[HD * h : HD * (h + 1), span[b]]

    def put(which, turn, grad):
        b, h = order[turn]
        rows_at = slice(which * width + HD * h, which * width + HD * (h + 1))
        packed_grad[rows_at, span[b]] = grad.astype(BF16)

    def key_and_query(turn, score_grad):
        b, h = order[turn]
        put(1, turn, nt(part(0, turn), score_grad) * LN2)
        query_grad = nn(part(1, turn), score_grad) + from_class[b][HD * h : HD * (h + 1)]
        put(0, turn, query_grad * HD ** (-0.5))

    grads, score_grads = {0: tn(part(2, 0), low_part(0))}, {}
    for turn, (b, h) in enumerate(order):
        if turn + 1 < len(order):
            grads[turn + 1] = tn(part(2, turn + 1), low_part(turn + 1))
        weights = probs[b * heads + h]
        put(2, turn, nt(low_part(turn), weights))
        score_grads[turn] = weights * (grads.pop(turn) - totals[b][h]).astype(BF16)
        if turn:
            key_and_query(turn - 1, score_grads.pop(turn - 1))
    key_and_query(len(order) - 1, score_grads.pop(len(order) - 1))
    first_grad = nn(r.frozen_triple[...], packed_grad[...])
    centre, inverse = r.stat[it, 0:1, :], r.stat[it, 1:2, :]
    unit = (values - centre) * inverse
    back = norm_back(first_grad * r.gainT[...], unit, inverse, 0)
    r.input_grad[it] = (middle_grad + back).astype(BF16)


def patch_kernel(dims, *refs):
    r = SimpleNamespace(**dict(zip(dims.names, refs, strict=True)))
    n_img, width, hidden, inside = dims.n_img, dims.width, dims.hidden, dims.inside
    heads = width // HD
    rows, patches = dims.images, dims.patches
    pairs, lanes = rows // 2, 2 * patches
    shard = width // n_img
    shard_ff = hidden // n_img

    if inside:
        seg = lax.axis_index(SEG)
        me = lax.axis_index(IMG)
        barrier = pltpu.get_barrier_semaphore()

        def sibling(src, dst, link):
            return pltpu.make_async_remote_copy(
                src_ref=src,
                dst_ref=dst,
                send_sem=link.at[0],
                recv_sem=link.at[1],
                device_id={SEG: 1 - seg},
                device_id_type=MESH,
            )

        def to_peers(source, target, link):
            def send(step, carry):
                pltpu.make_async_remote_copy(
                    src_ref=source,
                    dst_ref=target,
                    send_sem=link.at[0],
                    recv_sem=link.at[1],
                    device_id={IMG: lax.rem(me + step, n_img)},
                    device_id_type=MESH,
                ).start()
                return carry

            lax.fori_loop(1, n_img, send, 0)
            pltpu.make_async_copy(source, target, link.at[1]).start()

        def to_other_segment(source, target, link):
            def send(step, carry):
                pltpu.make_async_remote_copy(
                    src_ref=source,
                    dst_ref=target,
                    send_sem=link.at[0],
                    recv_sem=link.at[1],
                    device_id={SEG: 1 - seg, IMG: lax.rem(me + step, n_img)},
                    device_id_type=MESH,
                ).start()
                return carry

            lax.fori_loop(0, n_img, send, 0)

        def wait_all(whole, sem):
            pltpu.make_async_copy(whole, whole, sem).wait()

        def greet(step, carry):
            peer = lax.rem(me + step, n_img)
            for other in range(2):
                pl.semaphore_signal(
                    barrier,
                    inc=1,
                    device_id={SEG: lax.rem(seg + other, 2), IMG: peer},
                    device_id_type=MESH,
                )
            return carry

        lax.fori_loop(1, n_img, greet, 0)
        pl.semaphore_signal(barrier, inc=1, device_id={SEG: 1 - seg}, device_id_type=MESH)

    for it in range(pairs):
        pair_copy(r.tokens, r.tok, r.tok_sem, it).start()
    for it in range(dims.early):
        pair_copy(r.cotangent, r.cot, r.cot_sem, it).start()

    vectors = r.vectors[...]
    gain_row = wide_row(vectors, 0, width // 128)
    regain_row = wide_row(vectors, width // 128, width // 128)
    r.tripleT[...] = r.frozen_triple[...].T
    r.mergeT[...] = r.frozen_merge[...].T
    r.expandT[...] = r.frozen_expand[...].T
    r.shrinkT[...] = r.frozen_shrink[...].T
    turns = (
        (r.tripleT, r.triple_turned),
        (r.mergeT, r.merge_turned),
        (r.expandT, r.expand_turned),
        (r.shrinkT, r.shrink_turned),
    )
    for k, (turned, target) in enumerate(turns):
        pltpu.make_async_copy(turned, target, r.turn_sem.at[k]).start()
    r.gainT[...] = column(gain_row, lanes)
    r.regainT[...] = column(regain_row, lanes)

    if inside:
        upstream = r.region_cotangent[...].astype(F32)
        fill = [upstream[8 * k : 8 * k + 8] for k in range(rows // 8)]
        for k in range(2):
            row = vectors[2 * width // 128 + k : 2 * width // 128 + k + 1, :]
            tall = column(row, 128)
            fill += [tall[at : at + 8] for at in range(0, shard, 8)]
        fill = jnp.concatenate(fill, axis=1)
        triple = r.weight_triple[...].astype(F32)
        merge = r.weight_merge[...].astype(F32)
        expand = r.weight_expand[...].astype(F32)
        first_half = jnp.concatenate([triple, merge], axis=1)
        r.w_own[0] = jnp.concatenate([first_half, fill], axis=0).astype(BF16)
        r.w_own[1] = jnp.concatenate([expand, fill], axis=0).astype(BF16)
        for k in range(2):
            r.s_own[k] = r.weight_shrink[k * shard_ff // 2 : (k + 1) * shard_ff // 2, :]

    class_in = r.class_tokens[...].astype(F32)
    class_unit, _, _ = standardize(class_in, 1)
    class_first = (class_unit * gain_row).astype(BF16)
    class_packed = nn(class_first, r.frozen_triple[...]).astype(BF16).astype(F32)
    r.class_packed[...] = class_packed
    tall_q = spread(class_packed[:, 0:width])
    tall_k = spread(class_packed[:, width : 2 * width])
    tall_v = spread(class_packed[:, 2 * width :])
    r.class_k[...] = tall_k.reshape(rows, HEADS8, width)
    r.class_v[...] = tall_v.reshape(rows, HEADS8, width)
    query_map = nt(tall_q.astype(BF16), r.frozen_triple[:, width : 2 * width])
    query_map = query_map * (LOG2E * HD ** (-0.5))
    r.query_map[...] = query_map.reshape(rows, HEADS8, width)
    self_score = jnp.sum(tall_q * tall_k, axis=1, keepdims=True) * (LOG2E * HD ** (-0.5))
    r.self_score[...] = jnp.broadcast_to(self_score, (rows * HEADS8, 128)).reshape(
        rows, HEADS8, 128
    )
    r.class_first[...] = jnp.broadcast_to(
        class_first.astype(F32)[:, None, :], (rows, HEADS8, width)
    )

    def class_forward(it, carry):
        pair_copy(r.tokens, r.tok, r.tok_sem, it).wait()
        values = jnp.concatenate([r.tok[2 * it + b].T for b in range(2)], axis=1).astype(F32)
        unit, centre, inverse = standardize(values, 0)
        first = (unit * r.gainT[...]).astype(BF16)
        r.firstT[it] = first
        r.stat[it, 0:1, :] = centre
        r.stat[it, 1:2, :] = inverse
        maps = jnp.concatenate([r.query_map[2 * it + b] for b in range(2)], axis=0)
        scores = nn(maps.astype(BF16), first)
        for b in range(2):
            part = scores[b * HEADS8 : (b + 1) * HEADS8, b * patches : (b + 1) * patches]
            r.class_scores[2 * it + b] = part
            alone = r.self_score[2 * it + b][:, 0:1]
            top = jnp.maximum(jnp.max(part, axis=1, keepdims=True), alone)
            weights = jnp.exp2(part - top)
            weight_alone = jnp.exp2(alone - top)
            share = 1.0 / (jnp.sum(weights, axis=1, keepdims=True) + weight_alone)
            weights = weights * share
            weight_alone = weight_alone * share
            r.class_probs[2 * it + b] = weights
            r.self_prob[2 * it + b] = jnp.broadcast_to(weight_alone, (HEADS8, 128))
            mixed = nt(weights.astype(BF16), first[:, b * patches : (b + 1) * patches])
            r.mixed[2 * it + b] = mixed + weight_alone * r.class_first[2 * it + b]
        return carry

    lax.fori_loop(0, pairs // 2, class_forward, 0, unroll=2)
    if inside:
        pl.semaphore_wait(barrier, 2 * n_img - 1)
        to_peers(r.w_own.at[seg], r.w_all.at[seg, me], r.l_weights)
        to_peers(r.s_own.at[seg], r.s_all.at[seg, me], r.l_shrink)
    lax.fori_loop(pairs // 2, pairs, class_forward, 0, unroll=2)

    mixed = r.mixed[...].reshape(rows * HEADS8, width).astype(BF16)
    class_context = gather_heads(nn(mixed, r.frozen_triple[:, 2 * width :])).astype(BF16)
    class_middle = class_in + nn(class_context, r.frozen_merge[...])
    class_unit_b, _, _ = standardize(class_middle, 1)
    class_second = (class_unit_b * regain_row).astype(BF16)
    class_active, class_slope = gelu_pair(nn(class_second, r.frozen_expand[...]))
    class_out = class_middle + nn(class_active.astype(BF16), r.frozen_shrink[...])
    r.class_context[...] = class_context.astype(F32)
    r.class_middle[...] = class_middle
    r.class_slope[...] = class_slope
    r.class_out[...] = class_out.astype(BF16)
    if inside:
        to_other_segment(r.class_out, r.crossed.at[me], r.l_crossed)

    def region():
        keys = n_img * rows
        wait_all(r.crossed, r.l_crossed.at[1])
        sibling(r.w_all.at[seg], r.w_all.at[seg], r.l_forward).wait()
        sibling(r.s_all.at[seg], r.s_all.at[seg], r.l_forward_shrink).wait()
        half = shard_ff // 2
        for j in range(n_img):
            for k in range(2):
                down = shard_ff * j + half * k
                r.region_shrink[down : down + half, :] = r.s_all[k, j]
        deep = PAD * n_img
        w_triple = r.w_all[0, :, :, 0 : 3 * width].reshape(deep, 3 * width)
        w_merge = r.w_all[0, :, :, 3 * width :].reshape(deep, width)
        w_expand = r.w_all[1].reshape(deep, hidden)
        ups, wide = [], [[], []]
        for j in range(n_img):
            fill = r.w_all[seg, j].astype(F32)[shard:PAD]
            ups += [fill[:, width * k : width * (k + 1)] for k in range(rows // 8)]
            for k in range(2):
                first_at = width * (rows // 8) + 128 * (shard // 8) * k
                for at in range(first_at, first_at + 128 * (shard // 8), 128):
                    wide[k].append(fill[:, at : at + 128])
        wide = [jnp.concatenate(w, axis=0) for w in wide]
        gain, regain = (jnp.concatenate([g] * (keys // 128), axis=1) for g in wide)
        upstream = jnp.concatenate(ups, axis=0).T.astype(BF16)

        slots = r.region_number.shape[1]
        per = slots // n_img
        micros = rows // per
        numbers = r.region_number[...].astype(F32)
        numbers = jnp.concatenate([numbers, jnp.zeros((8 - micros, slots), F32)], axis=0)
        at = lax.broadcasted_iota(jnp.int32, (slots, keys), 1)
        slot = lax.broadcasted_iota(jnp.int32, (slots, keys), 0)
        chosen = slot == per * (at // rows) + lax.rem(at, per)
        numbers = nn(numbers.astype(BF16), jnp.where(chosen, 1.0, 0.0).astype(BF16))
        at = lax.rem(lax.broadcasted_iota(jnp.int32, (1, keys), 1), rows) // per
        code = jnp.zeros((1, keys), F32)
        for m in range(micros):
            code = jnp.where(at == m, numbers[m : m + 1, :] * micros + m, code)
        code_down = jnp.broadcast_to(code, (128, keys)).T
        code_down = jnp.concatenate([code_down] * (keys // 128), axis=1)
        bias = jnp.where(code_down == code, 0.0, NEG)

        qkv, probs, ctx = r.qkv, r.probs, r.ctx
        values = r.crossed[...].reshape(keys, width).T.astype(F32)
        unit, _, inverse = standardize(values, 0)
        r.region_first[...] = padded(unit * gain, shard, n_img).astype(BF16)
        packed = tn(w_triple, r.region_first[...])
        qkv[0:width, 0:keys] = (packed[0:width] * (LOG2E * HD ** (-0.5))).astype(BF16)
        qkv[width:, 0:keys] = packed[width:].astype(BF16)
        mixes = []
        for h in range(heads):
            q = qkv[HD * h : HD * (h + 1), 0:keys]
            k = qkv[width + HD * h : width + HD * (h + 1), 0:keys]
            v = qkv[2 * width + HD * h : 2 * width + HD * (h + 1), 0:keys]
            scores = tn(k, q) + bias
            weights = jnp.exp2(scores - jnp.max(scores, axis=0, keepdims=True))
            share = 1.0 / jnp.sum(weights, axis=0, keepdims=True)
            low = weights.astype(BF16)
            probs[h] = low
            r.shares[0, h : h + 1, :] = share
            mixes.append(nn(v, low) * share)
        context = jnp.concatenate(mixes, axis=0)
        r.region_context[...] = padded(context, shard, n_img).astype(BF16)
        middle = values + tn(w_merge, r.region_context[...])
        unit_b, _, inverse_b = standardize(middle, 0)
        r.region_second[...] = padded(unit_b * regain, shard, n_img).astype(BF16)
        for c in range(0, hidden, width):
            at = slice(c, c + width)
            active, slope = gelu_pair(tn(w_expand[:, at], r.region_second[...]))
            r.region_active[at, :] = active.astype(BF16)
            r.slope[at, 0:keys] = slope.astype(BF16)
        result = middle + tn(r.region_shrink[...], r.region_active[...])
        mine = pl.ds(pl.multiple_of(me * rows, rows), rows)
        r.region_rows[...] = result.T
        r.region_out[...] = r.region_rows[mine, :].astype(BF16)

        for c in range(0, hidden, width):
            at = slice(c, c + width)
            active_grad = nn(r.region_shrink[at, :], upstream)
            r.active[at, 0:keys] = (active_grad * r.slope[at, 0:keys].astype(F32)).astype(BF16)
        hidden_low = r.active[:, 0:keys]
        second_grad = trimmed(nn(w_expand, hidden_low), shard, n_img)
        middle_grad = upstream.astype(F32) + norm_back(second_grad * regain, unit_b, inverse_b, 0)
        middle_low = middle_grad.astype(BF16)
        context_grad = trimmed(nn(w_merge, middle_low), shard, n_img)
        packed_grad = r.packed_grad
        for h in range(heads):
            at = slice(HD * h, HD * (h + 1))
            q = qkv[at, 0:keys]
            k = qkv[width + HD * h : width + HD * (h + 1), 0:keys]
            v = qkv[2 * width + HD * h : 2 * width + HD * (h + 1), 0:keys]
            part = context_grad[at] * r.shares[0, h : h + 1, :]
            total = jnp.sum(part * context[at], axis=0, keepdims=True)
            low = part.astype(BF16)
            weights = probs[h]
            score_grad = (weights.astype(F32) * (tn(v, low) - total)).astype(BF16)
            packed_grad[at, 0:keys] = (nn(k, score_grad) * HD ** (-0.5)).astype(BF16)
            packed_grad[width + HD * h : width + HD * (h + 1), 0:keys] = (
                nt(q, score_grad) * LN2
            ).astype(BF16)
            packed_grad[2 * width + HD * h : 2 * width + HD * (h + 1), 0:keys] = (
                nt(low, weights).astype(BF16)
            )
        first_grad = trimmed(nn(w_triple, packed_grad[:, 0:keys]), shard, n_img)
        back = norm_back(first_grad * gain, unit, inverse, 0)
        r.region_rows[...] = (middle_grad + back).T
        r.crossed_grad[...] = r.region_rows[mine, :].astype(BF16)
        sibling(r.crossed_grad, r.returned, r.l_returned).start()

        mine = pl.ds(pl.multiple_of(me * PAD, PAD), PAD)
        grads = r.grads
        grads[:, 0 : 3 * width] = nt(r.region_first[mine, :], packed_grad[:, 0:keys])[0:shard]
        grads[:, 3 * width : 4 * width] = nt(r.region_context[mine, :], middle_low)[0:shard]
        grads[:, 4 * width : 4 * width + hidden] = nt(r.region_second[mine, :], hidden_low)[0:shard]
        mine = pl.ds(pl.multiple_of(me * shard_ff, shard_ff), shard_ff)
        r.grads_shrink[...] = nt(r.region_active[mine, :], upstream)
        mine = pl.ds(pl.multiple_of(me * shard, shard), shard)
        for k, (grad, standard) in enumerate(((first_grad, unit), (second_grad, unit_b))):
            total = jnp.sum(grad * standard, axis=1, keepdims=True)
            r.gain_columns[...] = jnp.broadcast_to(total, (width, 128))
            at = 4 * width + hidden + 128 * k
            grads[:, at : at + 128] = r.gain_columns[mine, :]
        sibling(grads, r.grads_in, r.l_grads).start()
        sibling(r.grads_shrink, r.grads_shrink_in, r.l_grads_shrink).start()

    def one_pair(it, carry):
        pair_copy(r.cotangent, r.cot, r.cot_sem, it).wait()
        patch_pair(r, dims, it, it)
        pair_copy(r.tok, r.patch_rows, r.out_sem, it).start()
        one_copy(r.input_grad, r.grad_rows, r.grad_sem, it).start()

        if inside:

            @pl.when(it == AT_FORWARD)
            def _():
                wait_all(r.w_all.at[seg], r.l_weights.at[1])
                wait_all(r.s_all.at[seg], r.l_shrink.at[1])
                sibling(r.w_all.at[seg], r.w_all.at[seg], r.l_forward).start()
                sibling(r.s_all.at[seg], r.s_all.at[seg], r.l_forward_shrink).start()

            pl.when(it == AT_REGION)(region)
        return carry

    for it in range(pairs):
        one_copy(r.firstT, r.first_rows, r.first_sem, it).start()
    lax.fori_loop(0, dims.early, one_pair, 0)

    if inside:
        sibling(r.crossed_grad, r.returned, r.l_returned).wait()
        sibling(r.grads, r.grads_in, r.l_grads).wait()
        sibling(r.grads_shrink, r.grads_shrink_in, r.l_grads_shrink).wait()
        r.class_up[...] = r.returned[...]
        r.grads_out[...] = r.grads[...] + r.grads_in[...]
        r.shrink_out[...] = r.grads_shrink[...] + r.grads_shrink_in[...]
        peers = pl.ds(0, n_img - 1)
        wait_all(r.w_all.at[0, peers], r.l_weights.at[0])
        wait_all(r.s_all.at[0, peers], r.l_shrink.at[0])
        wait_all(r.crossed, r.l_crossed.at[0])
    for it in range(pairs):
        one_copy(r.firstT, r.first_rows, r.first_sem, it).wait()
    for it in range(dims.early):
        pair_copy(r.tok, r.patch_rows, r.out_sem, it).wait()
        one_copy(r.input_grad, r.grad_rows, r.grad_sem, it).wait()
    for k, (turned, target) in enumerate(turns):
        pltpu.make_async_copy(turned, target, r.turn_sem.at[k]).wait()


def finish_kernel(dims, *refs):
    r = SimpleNamespace(**dict(zip(dims.names, refs, strict=True)))
    width, hidden = dims.width, dims.hidden
    rows, patches, early = dims.images, dims.patches, dims.early
    pairs, lanes = rows // 2, 2 * patches
    late = pairs - early

    loads = []
    for k, name in enumerate(dims.staged):
        load = pltpu.make_async_copy(getattr(r, name), getattr(r, name + BESIDE), r.load_sem.at[k])
        setattr(r, name, getattr(r, name + BESIDE))
        loads.append(load)
    last = pl.ds(2 * early, 2 * late)
    tok_in = pltpu.make_async_copy(r.tokens.at[last], r.tok, r.late_sem.at[0])
    cot_in = pltpu.make_async_copy(r.cotangent.at[last], r.cot, r.late_sem.at[1])
    ready = pl.ds(0, 2 * early)
    rows_in = pltpu.make_async_copy(r.patch_rows.at[ready], r.ready, r.late_sem.at[2])
    rows_out = pltpu.make_async_copy(r.ready, r.patch_output.at[ready], r.late_sem.at[4])
    firsts = [one_copy(r.first_rows, r.firstT, r.first_sem, it) for it in range(pairs)]
    earlier = [one_copy(r.grad_rows, r.input_grad, r.grad_sem, it) for it in range(early)]
    bounds = (0,) + dims.bounds
    stages = [loads[a:b] for a, b in zip(bounds, bounds[1:])]
    stages[0] = firsts[early:] + [tok_in] + stages[0]
    stages[2] = [cot_in] + stages[2]
    stages[3] = stages[3] + firsts[:early] + earlier + [rows_in]
    for stage in stages:
        for load in stage:
            load.start()

    def ready(stage):
        for load in stages[stage]:
            load.wait()

    ready(0)
    gain_row = wide_row(r.vectors[...], 0, width // 128)
    regain_row = wide_row(r.vectors[...], width // 128, width // 128)
    r.gainT[...] = column(gain_row, lanes)
    r.regainT[...] = column(regain_row, lanes)
    packed = r.class_packed[...]
    tall_k = spread(packed[:, width : 2 * width])
    tall_v = spread(packed[:, 2 * width :])
    r.class_k[...] = tall_k.reshape(rows, HEADS8, width)
    r.class_v[...] = tall_v.reshape(rows, HEADS8, width)
    for it in range(early, pairs):
        first_one = it == early
        patch_pair(r, dims, it, it - early, lambda k: ready(k) if first_one and k else None)
    ready(3)
    out = pltpu.make_async_copy(r.tok, r.patch_output.at[last], r.late_sem.at[3])
    out.start()
    rows_out.start()

    upstream = r.class_up[...]
    middle = r.class_middle[...]
    unit, _, inverse = standardize(middle, 1)
    hidden_low = (nt(upstream, r.frozen_shrink[...]) * r.class_slope[...]).astype(BF16)
    second_grad = nt(hidden_low, r.frozen_expand[...])
    middle_grad = upstream.astype(F32) + norm_back(second_grad * regain_row, unit, inverse, 1)
    low = nt(middle_grad.astype(BF16), r.frozen_merge[...]).astype(BF16).astype(F32)
    tall_low = spread(low)
    low_map = nt(tall_low.astype(BF16), r.frozen_triple[:, 2 * width :])
    r.low_map[...] = low_map.reshape(rows, HEADS8, width)
    total = jnp.sum(spread(low * r.class_context[...]), axis=1, keepdims=True)
    r.class_total[...] = jnp.broadcast_to(total, (rows * HEADS8, 128)).reshape(rows, HEADS8, 128)
    r.ungainT[...] = 1.0 / r.gainT[:, 0:patches]

    def correct(it, carry):
        first = r.firstT[it]
        inverse = r.stat[it, 1:2, :]
        left, right, along = [], [], []
        maps = jnp.concatenate([r.low_map[2 * it + b] for b in range(2)], axis=0)
        probs_grads = nn(maps.astype(BF16), first)
        for b in range(2):
            image = 2 * it + b
            span = slice(b * patches, (b + 1) * patches)
            part = probs_grads[b * HEADS8 : (b + 1) * HEADS8, span]
            weights = r.class_probs[image]
            score_grad = weights * (part - r.class_total[image][:, 0:1])
            r.mixed[image] = nt(score_grad.astype(BF16), first[:, span])
            toward = jnp.concatenate([r.query_map[image], r.low_map[image]], axis=0) * gain_row
            left.append((toward - mean(toward, 1)).astype(BF16))
            scaled = jnp.concatenate([score_grad * LN2, weights], axis=0) * inverse[:, span]
            right.append(scaled.astype(BF16))
            scores = jnp.concatenate([r.class_scores[image], part], axis=0)
            along.append(jnp.sum(scaled * scores, axis=0, keepdims=True) * (1.0 / width))
        for b in range(2):
            span = slice(b * patches, (b + 1) * patches)
            back = tn(left[b], right[b]) - first[:, span].astype(F32) * (r.ungainT[...] * along[b])
            result = r.input_grad[it, :, span].astype(F32) + back
            r.result[2 * it + b] = result.astype(BF16).T
        pair_copy(r.result, r.patch_gradient, r.back_sem, it).start()
        return carry

    lax.fori_loop(0, pairs, correct, 0, unroll=2)

    self_prob = r.self_prob[...].reshape(rows * HEADS8, 128)[:, 0:1]
    tall_q = spread(packed[:, 0:width])
    self_grad = self_prob * (jnp.sum(tall_low * tall_v, axis=1, keepdims=True) - total)
    unit, _, inverse = standardize(r.class_tokens[...].astype(F32), 1)
    first = (unit * gain_row).astype(BF16).astype(F32)
    tall_first = jnp.broadcast_to(first[:, None, :], (rows, HEADS8, width))
    mixed = r.mixed[...].reshape(rows * HEADS8, width)
    mixed = mixed + self_grad * tall_first.reshape(rows * HEADS8, width)
    triple = r.frozen_triple
    query_grad = gather_heads(nn(mixed.astype(BF16), triple[:, width : 2 * width]))
    key_grad = r.class_dk[...] + (tall_q * (self_grad * HD ** (-0.5))).reshape(
        rows, HEADS8, width
    )
    value_grad = r.class_dv[...] + (tall_low * self_prob).reshape(rows, HEADS8, width)
    packed_grad = jnp.concatenate(
        [query_grad * HD ** (-0.5), jnp.sum(key_grad, axis=1), jnp.sum(value_grad, axis=1)],
        axis=1,
    ).astype(BF16)
    first_grad = nt(packed_grad, triple[...])
    back = norm_back(first_grad * gain_row, unit, inverse, 1)
    r.class_gradient[...] = (middle_grad + back).astype(BF16)
    if dims.inside:
        wide = width * 4 + hidden
        r.region_output[...] = r.region_out[...]
        r.triple_gradient[...] = r.grads_out[:, 0 : 3 * width]
        r.merge_gradient[...] = r.grads_out[:, 3 * width : 4 * width]
        r.expand_gradient[...] = r.grads_out[:, 4 * width : wide]
        r.shrink_gradient[...] = r.shrink_out[...]
        shard = r.grads_out.shape[0]
        blank = jnp.zeros((128 - shard, 128), F32)
        for k, target in enumerate((r.first_gradient, r.second_gradient)):
            columns = r.grads_out[:, wide + 128 * k : wide + 128 * (k + 1)]
            columns = jnp.concatenate([columns, blank], axis=0).T
            target[...] = columns[0:1, 0:shard]
    rows_out.wait()
    out.wait()
    for it in range(pairs):
        pair_copy(r.result, r.patch_gradient, r.back_sem, it).wait()


def normalize(values, scaling):
    centred = values - jnp.mean(values, axis=-1, keepdims=True)
    inverse = lax.rsqrt(jnp.mean(centred * centred, axis=-1, keepdims=True) + EPSILON)
    standard = centred * inverse
    return (standard * scaling, standard, inverse)


def normalize_back(upstream, standard, inverse, scaling):
    scaled = upstream * scaling
    centred = scaled - jnp.mean(scaled, axis=-1, keepdims=True)
    centred = centred - standard * jnp.mean(scaled * standard, axis=-1, keepdims=True)
    gain_grad = jnp.sum((upstream * standard).reshape(-1, upstream.shape[-1]), axis=0)
    return (centred * inverse, gain_grad)


def gelu_slope(hidden):
    return (
        0.5 * (1.0 + lax.erf(hidden * 0.7071067811865476))
        + hidden * jnp.exp(-0.5 * hidden * hidden) * 0.3989422804014327
    )


def forward_product(operand, weight):
    return lax.dot_general(
        operand, weight, (((operand.ndim - 1,), (0,)), ((), ())), preferred_element_type=F32
    )


def backward_product(upstream, weight):
    return lax.dot_general(
        upstream,
        weight,
        (((upstream.ndim - 1,), (1,)), ((), ())),
        preferred_element_type=F32,
    )


def row_product(operand, cotangent):
    left_rows = operand.reshape(-1, operand.shape[-1])
    right_rows = cotangent.reshape(-1, cotangent.shape[-1])
    return lax.dot_general(
        left_rows, right_rows, (((0,), (0,)), ((), ())), preferred_element_type=F32
    )


def heads_of(packed, portion):
    section_width = packed.shape[-1] // 3
    section = packed[..., portion * section_width : (portion + 1) * section_width]
    return section.reshape(packed.shape[:-1] + (section_width // HD, HD))


def raw_scores(queries, keyset, allowed):
    scores = jnp.einsum(
        "bqhd,bkhd->bhqk", queries, keyset, preferred_element_type=F32
    ) * HD ** (-0.5)
    if allowed is None:
        return scores
    return jnp.where(allowed[:, None], scores, -1e30)


def attend(queries, keyset, valueset, allowed):
    scores = raw_scores(queries, keyset, allowed)
    highest = jnp.max(scores, axis=-1, keepdims=True)
    logsum = highest + jnp.log(jnp.sum(jnp.exp(scores - highest), axis=-1, keepdims=True))
    weighting = jnp.exp(scores - logsum).astype(BF16)
    context = jnp.einsum("bhqk,bkhd->bqhd", weighting, valueset, preferred_element_type=F32)
    return (context.astype(BF16), logsum)


def score_terms(queries, keyset, valueset, allowed, logsum, context_grad):
    scores = raw_scores(queries, keyset, allowed)
    weighting = jnp.exp(scores - logsum)
    weight_grad = jnp.einsum(
        "bqhd,bkhd->bhqk", context_grad, valueset, preferred_element_type=F32
    )
    row_total = jnp.sum(weighting * weight_grad, axis=-1, keepdims=True)
    score_grad = (weighting * (weight_grad - row_total)).astype(BF16)
    return (weighting, score_grad, row_total)


def attend_back(queries, keyset, valueset, allowed, logsum, context_grad):
    weighting, score_grad, row_total = score_terms(
        queries, keyset, valueset, allowed, logsum, context_grad
    )
    value_grad = jnp.einsum(
        "bhqk,bqhd->bkhd",
        weighting.astype(BF16),
        context_grad,
        preferred_element_type=F32,
    )
    query_grad = jnp.einsum(
        "bhqk,bkhd->bqhd", score_grad, keyset, preferred_element_type=F32
    ) * HD ** (-0.5)
    key_grad = jnp.einsum(
        "bhqk,bqhd->bkhd", score_grad, queries, preferred_element_type=F32
    ) * HD ** (-0.5)
    return (query_grad, key_grad, value_grad)


def block_head(inputs, scaling, triple):
    normed, standard, inverse = normalize(inputs, scaling)
    first_low = normed.astype(BF16)
    packed = forward_product(first_low, triple).astype(BF16)
    return (first_low, standard, inverse, packed)


def block_tail(inputs, context, regain, merger, expand, shrink):
    middle = inputs + forward_product(context, merger)
    normed, standard, inverse = normalize(middle, regain)
    second = normed.astype(BF16)
    hidden = forward_product(second, expand)
    active = jax.nn.gelu(hidden, approximate=False).astype(BF16)
    result = middle + forward_product(active, shrink)
    return (result, (standard, inverse, second, hidden, active))


def tail_back(upstream, kept_tail, regain, merger, expand, shrink):
    standard, inverse, second, hidden, active = kept_tail
    out_low = upstream.astype(BF16)
    active_grad = backward_product(out_low, shrink)
    hidden_low = (active_grad * gelu_slope(hidden)).astype(BF16)
    second_grad = backward_product(hidden_low, expand)
    norm_grad, regain_grad = normalize_back(second_grad, standard, inverse, regain)
    middle_grad = upstream + norm_grad
    middle_low = middle_grad.astype(BF16)
    context_low = backward_product(middle_low, merger).astype(BF16)
    return (middle_grad, context_low, regain_grad, (middle_low, hidden_low, out_low))


def region_outside(crossed, region_number, region_cotangent, shards_in):
    crossed = lax.ppermute(crossed, SEG, [(0, 1), (1, 0)])
    images = crossed.shape[1]
    model_width = crossed.shape[2]
    gathered = [lax.all_gather(shard, IMG, axis=0, tiled=True) for shard in shards_in]
    full_gain, triple, merger, full_regain, expand, shrink = gathered
    scaling = full_gain.astype(F32)
    regain = full_regain.astype(F32)
    region_in = crossed.astype(F32)
    first_low, standard, inverse, packed = block_head(region_in, scaling, triple)
    local_keys = packed[..., model_width : 2 * model_width]
    local_values = packed[..., 2 * model_width :]
    all_keys, all_values = (
        lax.all_gather(local_keys, IMG, axis=1, tiled=True),
        lax.all_gather(local_values, IMG, axis=1, tiled=True),
    )
    head_shape = all_keys.shape[:-1] + (model_width // HD, HD)
    keyset = all_keys.reshape(head_shape)
    valueset = all_values.reshape(head_shape)
    queries = heads_of(packed, 0)
    first_slot = lax.axis_index(IMG) * images
    own_number = lax.dynamic_slice_in_dim(region_number, first_slot, images, 1)
    allowed = own_number[:, :, None] == region_number[:, None, :]
    context, logsum = attend(queries, keyset, valueset, allowed)
    context = context.reshape(region_in.shape)
    region_result, kept_tail = block_tail(region_in, context, regain, merger, expand, shrink)
    region_output = region_result.astype(BF16)
    upstream = region_cotangent.astype(F32)
    middle_grad, context_low, second_gain_grad, low_rows = tail_back(
        upstream, kept_tail, regain, merger, expand, shrink
    )
    middle_low, hidden_low, out_low = low_rows
    context_heads = context_low.reshape(queries.shape)
    query_grad, key_grad, value_grad = attend_back(
        queries, keyset, valueset, allowed, logsum, context_heads
    )
    key_sum, value_sum = (
        lax.psum_scatter(key_grad.reshape(all_keys.shape), IMG, scatter_dimension=1, tiled=True),
        lax.psum_scatter(
            value_grad.reshape(all_values.shape), IMG, scatter_dimension=1, tiled=True
        ),
    )
    packed_grad = jnp.concatenate(
        [query_grad.reshape(region_in.shape), key_sum, value_sum], axis=-1
    ).astype(BF16)
    norm_grad, first_gain_grad = normalize_back(
        backward_product(packed_grad, triple), standard, inverse, scaling
    )
    input_grad = (middle_grad + norm_grad).astype(BF16)
    second_low = kept_tail[2]
    active_low = kept_tail[4]
    shards = (
        lax.psum_scatter(first_gain_grad, IMG, scatter_dimension=0, tiled=True),
        lax.psum_scatter(
            row_product(first_low, packed_grad), IMG, scatter_dimension=0, tiled=True
        ),
        lax.psum_scatter(row_product(context, middle_low), IMG, scatter_dimension=0, tiled=True),
        lax.psum_scatter(second_gain_grad, IMG, scatter_dimension=0, tiled=True),
        lax.psum_scatter(
            row_product(second_low, hidden_low), IMG, scatter_dimension=0, tiled=True
        ),
        lax.psum_scatter(row_product(active_low, out_low), IMG, scatter_dimension=0, tiled=True),
    )
    totals = tuple(lax.psum(shard.astype(BF16), SEG).astype(F32) for shard in shards)
    return region_output, lax.ppermute(input_grad, SEG, [(0, 1), (1, 0)]), totals


def local(
    n_img,
    patch_tokens,
    class_tokens,
    region_number,
    frozen_gain,
    frozen_triple,
    frozen_merge,
    frozen_regain,
    frozen_expand,
    frozen_shrink,
    gain_first,
    weight_triple,
    weight_merge,
    gain_second,
    weight_expand,
    weight_shrink,
    patch_cotangent,
    region_cotangent,
):
    micros, per, patches, width = patch_tokens.shape
    hidden = frozen_expand.shape[1]
    images = micros * per
    shard, shard_ff = width // n_img, hidden // n_img
    lanes, pairs, keys, heads = 2 * patches, images // 2, n_img * images, width // HD
    inside = keys == patches and shard == PAD - 8 and images == 16 and width == 384

    vectors = [frozen_gain, frozen_regain]
    if inside:
        vectors += [jnp.pad(g, (0, 128 - shard)) for g in (gain_first, gain_second)]
    vectors = jnp.concatenate(vectors)
    vectors = jnp.pad(vectors, (0, 1024 - vectors.shape[0])).astype(F32).reshape(8, 128)
    class_rows = class_tokens.reshape(images, width)
    inputs = dict(
        tokens=patch_tokens.reshape(images, patches, width),
        cotangent=patch_cotangent.reshape(images, patches, width),
        class_tokens=class_rows,
        vectors=vectors,
        frozen_triple=frozen_triple,
        frozen_merge=frozen_merge,
        frozen_expand=frozen_expand,
        frozen_shrink=frozen_shrink,
    )
    if inside:
        inputs |= dict(
            region_cotangent=region_cotangent.reshape(images, width),
            region_number=region_number,
            weight_triple=weight_triple,
            weight_merge=weight_merge,
            weight_expand=weight_expand,
            weight_shrink=weight_shrink,
        )
    vmem = pl.BlockSpec(memory_space=pltpu.VMEM)
    hbm = pl.BlockSpec(memory_space=pl.ANY)
    streams = 2
    in_specs = [hbm] * streams + [vmem] * (len(inputs) - streams)

    shape = jax.ShapeDtypeStruct
    columns = 4 * width + hidden + 256
    large = dict(
        patch_rows=shape((images, patches, width), BF16),
        first_rows=shape((pairs, width, lanes), BF16),
        grad_rows=shape((pairs, width, lanes), BF16),
        triple_turned=shape((3 * width, width), BF16),
        merge_turned=shape((width, width), BF16),
        expand_turned=shape((hidden, width), BF16),
        shrink_turned=shape((width, hidden), BF16),
    )
    small = dict(
        stat=shape((pairs, 8, lanes), F32),
        class_packed=shape((images, 3 * width), F32),
        class_context=shape((images, width), F32),
        class_middle=shape((images, width), F32),
        class_slope=shape((images, hidden), F32),
        query_map=shape((images, HEADS8, width), F32),
        class_probs=shape((images, HEADS8, patches), F32),
        class_scores=shape((images, HEADS8, patches), F32),
        self_prob=shape((images, HEADS8, 128), F32),
        class_dk=shape((images, HEADS8, width), F32),
        class_dv=shape((images, HEADS8, width), F32),
    )
    if inside:
        small |= dict(
            class_up=shape((images, width), BF16),
            region_out=shape((images, width), BF16),
            grads_out=shape((shard, columns), F32),
            shrink_out=shape((shard_ff, width), F32),
        )
    else:
        small |= dict(class_out=shape((images, width), BF16))
    outputs = large | small
    out_specs = [hbm] * len(large) + [vmem] * len(small)

    v = pltpu.VMEM
    dma = pltpu.SemaphoreType.DMA
    working = dict(
        gainT=v((width, lanes), F32),
        regainT=v((width, lanes), F32),
        qkv=v((3 * width, lanes), BF16),
        ctx=v((width, lanes), BF16),
        probs=v((2 * heads, patches, patches), BF16),
        shares=v((2, HEADS8, patches), F32),
        class_weights=v((2, HEADS8, patches), F32),
        active=v((hidden, lanes), BF16),
        slope=v((hidden, lanes), BF16),
        packed_grad=v((3 * width, lanes), BF16),
        low_grad=v((width, lanes), BF16),
        class_k=v((images, HEADS8, width), F32),
        class_v=v((images, HEADS8, width), F32),
        mixed=v((images, HEADS8, width), F32),
        firstT=v((pairs, width, lanes), BF16),
        input_grad=v((pairs, width, lanes), BF16),
        first_sem=dma((pairs,)),
        grad_sem=dma((pairs,)),
    )
    turned = dict(
        tripleT=v((3 * width, width), BF16),
        mergeT=v((width, width), BF16),
        expandT=v((hidden, width), BF16),
        shrinkT=v((width, hidden), BF16),
    )
    scratch = working | turned | dict(
        tok=v((images, patches, width), BF16),
        cot=v((images, patches, width), BF16),
        class_first=v((images, HEADS8, width), F32),
        self_score=v((images, HEADS8, 128), F32),
        tok_sem=dma((pairs,)),
        cot_sem=dma((pairs,)),
        out_sem=dma((pairs,)),
        turn_sem=dma((len(turned),)),
    )
    if inside:
        deep = PAD * n_img
        scratch |= dict(
            class_out=v((images, width), BF16),
            crossed=v((n_img, images, width), BF16),
            crossed_grad=v((images, width), BF16),
            returned=v((images, width), BF16),
            w_own=v((2, PAD, 4 * width), BF16),
            w_all=v((2, n_img, PAD, 4 * width), BF16),
            s_own=v((2, shard_ff // 2, width), BF16),
            s_all=v((2, n_img, shard_ff // 2, width), BF16),
            region_shrink=v((hidden, width), BF16),
            region_first=v((deep, keys), BF16),
            region_context=v((deep, keys), BF16),
            region_second=v((deep, keys), BF16),
            region_active=v((hidden, keys), BF16),
            region_rows=v((keys, width), F32),
            gain_columns=v((width, 128), F32),
            grads=v((shard, columns), F32),
            grads_in=v((shard, columns), F32),
            grads_shrink=v((shard_ff, width), F32),
            grads_shrink_in=v((shard_ff, width), F32),
            l_weights=dma((2,)),
            l_shrink=dma((2,)),
            l_forward=dma((2,)),
            l_forward_shrink=dma((2,)),
            l_crossed=dma((2,)),
            l_returned=dma((2,)),
            l_grads=dma((2,)),
            l_grads_shrink=dma((2,)),
        )
    sizes = dict(
        n_img=n_img,
        width=width,
        hidden=hidden,
        images=images,
        patches=patches,
        inside=inside,
        early=pairs - LATE,
    )
    limit = dict(vmem_limit_bytes=60 * 1024 * 1024)
    remote = dict(collective_id=0, has_side_effects=True) if inside else {}
    names = list(inputs) + list(outputs) + list(scratch)
    results = pl.pallas_call(
        functools.partial(patch_kernel, SimpleNamespace(names=names, **sizes)),
        out_shape=list(outputs.values()),
        in_specs=in_specs,
        out_specs=out_specs,
        scratch_shapes=list(scratch.values()),
        compiler_params=pltpu.CompilerParams(**limit, **remote),
    )(*inputs.values())
    done = dict(zip(outputs, results, strict=True))

    if not inside:
        class_out = done.pop(list(small)[-1])
        region_output, class_up, grads = region_outside(
            class_out.reshape(class_tokens.shape),
            region_number,
            region_cotangent,
            (gain_first, weight_triple, weight_merge, gain_second, weight_expand, weight_shrink),
        )
        done |= dict(class_up=class_up.reshape(images, width))

    streamed = [done.pop(name) for name in large]
    done = SimpleNamespace(**done)
    tripleT, mergeT, expandT, shrinkT = streamed[-len(turned) :]
    stages = (
        dict(vectors=vectors, class_packed=done.class_packed, stat=done.stat, tripleT=tripleT),
        dict(mergeT=mergeT, expandT=expandT, shrinkT=shrinkT),
        dict(
            frozen_shrink=frozen_shrink,
            frozen_expand=frozen_expand,
            frozen_merge=frozen_merge,
            frozen_triple=frozen_triple,
            class_dk=done.class_dk,
            class_dv=done.class_dv,
        ),
        dict(class_tokens=class_rows) | vars(done),
    )
    staged, bounds = {}, ()
    for stage in stages:
        staged |= {name: a for name, a in stage.items() if name not in staged}
        bounds += (len(staged),)
    inputs = dict(
        tokens=patch_tokens.reshape(images, patches, width),
        cotangent=patch_cotangent.reshape(images, patches, width),
        patch_rows=streamed[0],
        first_rows=streamed[1],
        grad_rows=streamed[2],
    )
    inputs |= staged
    outputs = dict(
        patch_output=shape((images, patches, width), BF16),
        patch_gradient=shape((images, patches, width), BF16),
        class_gradient=shape((images, width), BF16),
    )
    out_specs = [hbm] * 2 + [vmem]
    if inside:
        ready = dict(
            region_output=shape((images, width), BF16),
            first_gradient=shape((1, shard), F32),
            triple_gradient=shape((shard, 3 * width), F32),
            merge_gradient=shape((shard, width), F32),
            second_gradient=shape((1, shard), F32),
            expand_gradient=shape((shard, hidden), F32),
            shrink_gradient=shape((shard_ff, width), F32),
        )
        outputs |= ready
        out_specs += [vmem] * len(ready)
    scratch = working | dict(
        tok=v((2 * LATE, patches, width), BF16),
        cot=v((2 * LATE, patches, width), BF16),
        result=v((images, patches, width), BF16),
        ungainT=v((width, patches), F32),
        low_map=v((images, HEADS8, width), F32),
        class_total=v((images, HEADS8, 128), F32),
        load_sem=dma((len(staged),)),
        ready=v((images - 2 * LATE, patches, width), BF16),
        late_sem=dma((5,)),
        back_sem=dma((pairs,)),
    )
    scratch |= {name + BESIDE: v(a.shape, a.dtype) for name, a in staged.items()}
    names = list(inputs) + list(outputs) + list(scratch)
    sizes |= dict(names=names, staged=list(staged), bounds=bounds)
    results = pl.pallas_call(
        functools.partial(finish_kernel, SimpleNamespace(**sizes)),
        out_shape=list(outputs.values()),
        in_specs=[hbm] * len(inputs),
        out_specs=out_specs,
        scratch_shapes=list(scratch.values()),
        compiler_params=pltpu.CompilerParams(**limit),
    )(*inputs.values())
    done = SimpleNamespace(**dict(zip(outputs, results, strict=True)))
    if inside:
        region_output = done.region_output.reshape(class_tokens.shape)
        grads = (
            done.first_gradient.reshape(shard),
            done.triple_gradient,
            done.merge_gradient,
            done.second_gradient.reshape(shard),
            done.expand_gradient,
            done.shrink_gradient,
        )
    return (
        done.patch_output.reshape(patch_tokens.shape),
        region_output,
        done.patch_gradient.reshape(patch_tokens.shape),
        done.class_gradient.reshape(class_tokens.shape),
        *grads,
    )


def solution(mesh):
    patch, row = P(SEG, IMG, None, None), P(SEG, IMG, None)
    gain, weight, whole = P(IMG), P(IMG, None), P()
    block = (gain, weight, weight, gain, weight, weight)
    placed = (patch, row, P(SEG, None)) + (whole,) * 6 + block + (patch, row)
    return jax.shard_map(
        functools.partial(local, mesh.shape[IMG]),
        mesh=mesh,
        in_specs=placed,
        out_specs=(patch, row, patch, row) + block,
        check_vma=False,
    )
```

```python
import functools
from types import SimpleNamespace

import jax
import jax.numpy as jnp
from jax import lax
from jax.experimental import pallas as pl
from jax.experimental.pallas import tpu as pltpu
from jax.sharding import PartitionSpec as P

SEG = "segment"
IMG = "img"
HD = 64
HEADS8 = 8
EPSILON = 1e-06
LOG2E = 1.4426950408889634
LN2 = 0.6931471805599453
ROOT_HALF = 0.7071067811865476
DENSITY = 0.3989422804014327
LOG2_DENSITY = -1.3257480647361593
F32 = jnp.float32
BF16 = jnp.bfloat16
MESH = pl.DeviceIdType.MESH
NEG = -1e30
PAD = 32
BESIDE = "_"

AT_FORWARD = 5
AT_REGION = 6
LATE = 1


def nn(a, b):
    return lax.dot_general(a, b, (((1,), (0,)), ((), ())), preferred_element_type=F32)


def nt(a, b):
    return lax.dot_general(a, b, (((1,), (1,)), ((), ())), preferred_element_type=F32)


def tn(a, b):
    return lax.dot_general(a, b, (((0,), (0,)), ((), ())), preferred_element_type=F32)


def mean(values, axis):
    return jnp.sum(values, axis=axis, keepdims=True) * (1.0 / values.shape[axis])


def standardize(values, axis):
    centre = mean(values, axis)
    centred = values - centre
    inverse = lax.rsqrt(mean(centred * centred, axis) + EPSILON)
    return centred * inverse, centre, inverse


def norm_back(scaled, standard, inverse, axis):
    return inverse * (
        scaled - mean(scaled, axis) - standard * mean(scaled * standard, axis)
    )


def gelu_pair(hidden):
    upto = 0.5 + 0.5 * lax.erf(hidden * ROOT_HALF)
    bell = jnp.exp2(hidden * hidden * (-0.5 * LOG2E))
    return hidden * upto, upto + hidden * (bell * DENSITY)


def gelu_pair_low(half):
    twice = (1.0 + lax.erf(half * (2.0 * ROOT_HALF))).astype(BF16)
    bell = jnp.exp2(half * half * (-2.0 * LOG2E) + (LOG2_DENSITY + 2.0)).astype(BF16)
    low = half.astype(BF16)
    return low * twice, twice + low * bell


def own_heads(rows, width):
    shape = (rows * HEADS8, width)
    lane = lax.broadcasted_iota(jnp.int32, shape, 1) // HD
    return lane == lax.rem(lax.broadcasted_iota(jnp.int32, shape, 0), HEADS8)


def spread(values):
    rows, width = values.shape
    tall = jnp.broadcast_to(values[:, None, :], (rows, HEADS8, width))
    return jnp.where(own_heads(rows, width), tall.reshape(rows * HEADS8, width), 0.0)


def gather_heads(values):
    tall, width = values.shape
    kept = jnp.where(own_heads(tall // HEADS8, width), values, 0.0)
    return jnp.sum(kept.reshape(tall // HEADS8, HEADS8, width), axis=1)


def column(row, lanes):
    tall = jnp.broadcast_to(row, (128, row.shape[1])).T
    return jnp.concatenate([tall] * (lanes // 128), axis=1)


def pair_copy(source, target, sems, it):
    part = pl.ds(2 * it, 2)
    return pltpu.make_async_copy(source.at[part], target.at[part], sems.at[it])


def one_copy(source, target, sems, it):
    return pltpu.make_async_copy(source.at[it], target.at[it], sems.at[it])


def padded(values, shard, n):
    blank = jnp.zeros((PAD - shard, values.shape[1]), values.dtype)
    parts = []
    for j in range(n):
        parts += [values[shard * j : shard * (j + 1)], blank]
    return jnp.concatenate(parts, axis=0)


def trimmed(values, shard, n):
    return jnp.concatenate([values[PAD * j : PAD * j + shard] for j in range(n)], axis=0)


def project(r, dims, it):
    width = dims.width
    first = r.firstT[it]
    queries = nn(r.tripleT[0:width, :], first) * (LOG2E * HD ** (-0.5))
    r.qkv[0:width, :] = queries.astype(BF16)
    r.qkv[width:, :] = nn(r.tripleT[width:, :], first).astype(BF16)


def patch_pair(r, dims, it, slot, following, ready=lambda stage: None):
    width, hidden, patches = dims.width, dims.hidden, dims.patches
    heads = width // HD
    block_head = own_heads(1, width)
    span = [slice(b * patches, (b + 1) * patches) for b in range(2)]
    qkv, ctx, probs = r.qkv, r.ctx, r.probs
    values = jnp.concatenate([r.tok[2 * slot + b].T for b in range(2)], axis=1).astype(F32)
    order = [(b, h) for h in range(heads) for b in range(2)]
    key_rows = [r.class_k[2 * it + b].astype(BF16) for b in range(2)]
    value_rows = [r.class_v[2 * it + b].astype(BF16) for b in range(2)]
    class_scores = [nn(key_rows[b], qkv[0:width, span[b]]) for b in range(2)]

    def part(which, turn):
        b, h = order[turn]
        return qkv[which * width + HD * h : which * width + HD * (h + 1), span[b]]

    scores, mixes, class_weights, shares = {0: tn(part(1, 0), part(0, 0))}, [], [], []
    for turn, (b, h) in enumerate(order):
        if turn + 1 < len(order):
            scores[turn + 1] = tn(part(1, turn + 1), part(0, turn + 1))
        class_score = class_scores[b][h : h + 1, :]
        top = jnp.maximum(jnp.max(scores[turn], axis=0, keepdims=True), class_score)
        weights = jnp.exp2(scores.pop(turn) - top)
        class_weight = jnp.exp2(class_score - top)
        shares.append(1.0 / (jnp.sum(weights, axis=0, keepdims=True) + class_weight))
        class_weights.append(class_weight)
        probs[b * heads + h] = weights.astype(BF16)
        if turn:
            last = order[turn - 1]
            mixes.append(nn(part(2, turn - 1), probs[last[0] * heads + last[1]]))
    mixes.append(nn(part(2, len(order) - 1), probs[2 * heads - 1]))
    blank = [jnp.zeros((HEADS8 - heads, patches), F32)]
    for b in range(2):
        weights = jnp.concatenate(class_weights[b::2] + blank, axis=0)
        r.class_weights[b] = weights
        r.shares[b] = jnp.concatenate(shares[b::2] + blank, axis=0)
        from_class = tn(value_rows[b], weights.astype(BF16))
        for h in range(heads):
            at = slice(HD * h, HD * (h + 1))
            mix = mixes[2 * h + b] + from_class[at]
            ctx[at, span[b]] = (mix * shares[2 * h + b]).astype(BF16)
    ready(1)
    merged = nn(r.mergeT[...], ctx[...])
    upstream = jnp.concatenate([r.cot[2 * slot + b].T for b in range(2)], axis=1)
    half_upstream = upstream * BF16(0.5)
    chunks = [slice(c, c + width) for c in range(0, hidden, width)]

    def active_grad(at):
        return nn(r.frozen_shrink[at, :], half_upstream).astype(BF16)

    ahead = len(chunks) // 2
    active_grads = [active_grad(at) for at in chunks[:ahead]]
    middle = values + merged
    unit_b, _, inverse_b = standardize(middle, 0)
    second = (unit_b * r.regainT[...]).astype(BF16)
    coming = nn(r.expandT[chunks[0], :], second)
    for k, at in enumerate(chunks):
        current = coming
        if k + 1 < len(chunks):
            coming = nn(r.expandT[chunks[k + 1], :], second)
        if ahead + k < len(chunks):
            active_grads.append(active_grad(chunks[ahead + k]))
        active, slope = gelu_pair_low(current)
        r.active[at, :] = active.astype(BF16)
        r.slope[at, :] = active_grads[k] * slope.astype(BF16)
    ready(2)
    second_grad = nn(r.frozen_expand[...], r.slope[...])
    shrunk = nn(r.shrinkT[...], r.active[...])
    middle_grad = upstream.astype(F32) + norm_back(
        second_grad * r.regainT[...], unit_b, inverse_b, 0
    )
    result = middle + shrunk
    for b in range(2):
        r.tok[2 * slot + b] = result[:, span[b]].astype(BF16).T
    context_grad = nn(r.frozen_merge[...], middle_grad.astype(BF16))
    low_grad, packed_grad = r.low_grad, r.packed_grad
    totals, from_class = [[], []], []
    for b in range(2):
        for h in range(heads):
            at = slice(HD * h, HD * (h + 1))
            low = context_grad[at, span[b]] * r.shares[b][h : h + 1, :]
            totals[b].append(
                jnp.sum(low * ctx[at, span[b]].astype(F32), axis=0, keepdims=True)
            )
            low_grad[at, span[b]] = low.astype(BF16)
        all_low = low_grad[:, span[b]]
        weights = r.class_weights[b]
        class_grad = weights * (
            nn(value_rows[b], all_low) - jnp.concatenate(totals[b] + blank, axis=0)
        )
        class_grad = class_grad.astype(BF16)
        from_class.append(tn(key_rows[b], class_grad))
        dk = nt(class_grad, qkv[0:width, span[b]]) * LN2
        dv = nt(weights.astype(BF16), all_low)
        r.class_dk[2 * it + b] = jnp.where(block_head, dk, 0.0)
        r.class_dv[2 * it + b] = jnp.where(block_head, dv, 0.0)

    def low_part(turn):
        b, h = order[turn]
        return low_grad[HD * h : HD * (h + 1), span[b]]

    def put(which, turn, grad):
        b, h = order[turn]
        rows_at = slice(which * width + HD * h, which * width + HD * (h + 1))
        packed_grad[rows_at, span[b]] = grad.astype(BF16)

    def key_and_query(turn, score_grad):
        b, h = order[turn]
        put(1, turn, nt(part(0, turn), score_grad) * LN2)
        query_grad = nn(part(1, turn), score_grad) + from_class[b][HD * h : HD * (h + 1)]
        put(0, turn, query_grad * HD ** (-0.5))

    grads, score_grads = {0: tn(part(2, 0), low_part(0))}, {}
    for turn, (b, h) in enumerate(order):
        if turn + 1 < len(order):
            grads[turn + 1] = tn(part(2, turn + 1), low_part(turn + 1))
        weights = probs[b * heads + h]
        put(2, turn, nt(low_part(turn), weights))
        score_grads[turn] = weights * (grads.pop(turn) - totals[b][h]).astype(BF16)
        if turn:
            key_and_query(turn - 1, score_grads.pop(turn - 1))
    key_and_query(len(order) - 1, score_grads.pop(len(order) - 1))
    first_grad = nn(r.frozen_triple[...], packed_grad[...])
    if following is not None:
        project(r, dims, following)
    centre, inverse = r.stat[it, 0:1, :], r.stat[it, 1:2, :]
    unit = (values - centre) * inverse
    back = norm_back(first_grad * r.gainT[...], unit, inverse, 0)
    r.input_grad[it] = (middle_grad + back).astype(BF16)


def patch_kernel(dims, *refs):
    r = SimpleNamespace(**dict(zip(dims.names, refs, strict=True)))
    n_img, width, hidden, inside = dims.n_img, dims.width, dims.hidden, dims.inside
    heads = width // HD
    rows, patches = dims.images, dims.patches
    pairs, lanes = rows // 2, 2 * patches
    shard = width // n_img
    shard_ff = hidden // n_img

    if inside:
        seg = lax.axis_index(SEG)
        me = lax.axis_index(IMG)
        barrier = pltpu.get_barrier_semaphore()

        def sibling(src, dst, link):
            return pltpu.make_async_remote_copy(
                src_ref=src,
                dst_ref=dst,
                send_sem=link.at[0],
                recv_sem=link.at[1],
                device_id={SEG: 1 - seg},
                device_id_type=MESH,
            )

        def to_peers(source, target, link):
            def send(step, carry):
                pltpu.make_async_remote_copy(
                    src_ref=source,
                    dst_ref=target,
                    send_sem=link.at[0],
                    recv_sem=link.at[1],
                    device_id={IMG: lax.rem(me + step, n_img)},
                    device_id_type=MESH,
                ).start()
                return carry

            lax.fori_loop(1, n_img, send, 0)
            pltpu.make_async_copy(source, target, link.at[1]).start()

        def to_other_segment(source, target, link):
            def send(step, carry):
                pltpu.make_async_remote_copy(
                    src_ref=source,
                    dst_ref=target,
                    send_sem=link.at[0],
                    recv_sem=link.at[1],
                    device_id={SEG: 1 - seg, IMG: lax.rem(me + step, n_img)},
                    device_id_type=MESH,
                ).start()
                return carry

            lax.fori_loop(0, n_img, send, 0)

        def wait_all(whole, sem):
            pltpu.make_async_copy(whole, whole, sem).wait()

        def greet(step, carry):
            peer = lax.rem(me + step, n_img)
            for other in range(2):
                pl.semaphore_signal(
                    barrier,
                    inc=1,
                    device_id={SEG: lax.rem(seg + other, 2), IMG: peer},
                    device_id_type=MESH,
                )
            return carry

        lax.fori_loop(1, n_img, greet, 0)
        pl.semaphore_signal(barrier, inc=1, device_id={SEG: 1 - seg}, device_id_type=MESH)

    for it in range(pairs):
        pair_copy(r.tokens, r.tok, r.tok_sem, it).start()
    for it in range(dims.early):
        pair_copy(r.cotangent, r.cot, r.cot_sem, it).start()

    gain_row = r.frozen_gain[...].astype(F32).reshape(1, width)
    regain_row = r.frozen_regain[...].astype(F32).reshape(1, width)
    r.tripleT[...] = r.frozen_triple[...].T
    r.mergeT[...] = r.frozen_merge[...].T
    r.expandT[...] = r.frozen_expand[...].T * BF16(0.5)
    r.shrinkT[...] = r.frozen_shrink[...].T
    turns = (
        (r.tripleT, r.triple_turned),
        (r.mergeT, r.merge_turned),
        (r.expandT, r.expand_turned),
        (r.shrinkT, r.shrink_turned),
    )
    for k, (turned, target) in enumerate(turns):
        pltpu.make_async_copy(turned, target, r.turn_sem.at[k]).start()
    r.gainT[...] = column(gain_row, lanes)
    r.regainT[...] = column(regain_row, lanes)

    if inside:
        upstream = r.region_cotangent[...].astype(F32)
        fill = [upstream[8 * k : 8 * k + 8] for k in range(rows // 8)]
        r.shard_gains[...] = jnp.zeros_like(r.shard_gains)
        r.shard_gains[0:1, 0:shard] = r.gain_first[...].astype(F32).reshape(1, shard)
        r.shard_gains[1:2, 0:shard] = r.gain_second[...].astype(F32).reshape(1, shard)
        for k in range(2):
            tall = column(r.shard_gains[k : k + 1, :], 128)
            fill += [tall[at : at + 8] for at in range(0, shard, 8)]
        fill = jnp.concatenate(fill, axis=1)
        triple = r.weight_triple[...].astype(F32)
        merge = r.weight_merge[...].astype(F32)
        expand = r.weight_expand[...].astype(F32)
        first_half = jnp.concatenate([triple, merge], axis=1)
        r.w_own[0] = jnp.concatenate([first_half, fill], axis=0).astype(BF16)
        r.w_own[1] = jnp.concatenate([expand, fill], axis=0).astype(BF16)
        for k in range(2):
            r.s_own[k] = r.weight_shrink[k * shard_ff // 2 : (k + 1) * shard_ff // 2, :]

    class_in = r.class_tokens[...].astype(F32)
    class_unit, _, _ = standardize(class_in, 1)
    class_first = (class_unit * gain_row).astype(BF16)
    class_packed = nn(class_first, r.frozen_triple[...]).astype(BF16).astype(F32)
    r.class_packed[...] = class_packed
    tall_q = spread(class_packed[:, 0:width])
    tall_k = spread(class_packed[:, width : 2 * width])
    tall_v = spread(class_packed[:, 2 * width :])
    r.class_k[...] = tall_k.reshape(rows, HEADS8, width)
    r.class_v[...] = tall_v.reshape(rows, HEADS8, width)
    query_map = nt(tall_q.astype(BF16), r.frozen_triple[:, width : 2 * width])
    query_map = query_map * (LOG2E * HD ** (-0.5))
    r.query_map[...] = query_map.reshape(rows, HEADS8, width)
    self_score = jnp.sum(tall_q * tall_k, axis=1, keepdims=True) * (LOG2E * HD ** (-0.5))
    r.self_score[...] = jnp.broadcast_to(self_score, (rows * HEADS8, 128)).reshape(
        rows, HEADS8, 128
    )
    r.class_first[...] = jnp.broadcast_to(
        class_first.astype(F32)[:, None, :], (rows, HEADS8, width)
    )

    def class_forward(it, carry):
        pair_copy(r.tokens, r.tok, r.tok_sem, it).wait()
        values = jnp.concatenate([r.tok[2 * it + b].T for b in range(2)], axis=1).astype(F32)
        unit, centre, inverse = standardize(values, 0)
        first = (unit * r.gainT[...]).astype(BF16)
        r.firstT[it] = first
        r.stat[it, 0:1, :] = centre
        r.stat[it, 1:2, :] = inverse
        maps = jnp.concatenate([r.query_map[2 * it + b] for b in range(2)], axis=0)
        scores = nn(maps.astype(BF16), first)
        for b in range(2):
            part = scores[b * HEADS8 : (b + 1) * HEADS8, b * patches : (b + 1) * patches]
            r.class_scores[2 * it + b] = part
            alone = r.self_score[2 * it + b][:, 0:1]
            top = jnp.maximum(jnp.max(part, axis=1, keepdims=True), alone)
            weights = jnp.exp2(part - top)
            weight_alone = jnp.exp2(alone - top)
            share = 1.0 / (jnp.sum(weights, axis=1, keepdims=True) + weight_alone)
            weights = weights * share
            weight_alone = weight_alone * share
            r.class_probs[2 * it + b] = weights
            r.self_prob[2 * it + b] = jnp.broadcast_to(weight_alone, (HEADS8, 128))
            mixed = nt(weights.astype(BF16), first[:, b * patches : (b + 1) * patches])
            r.mixed[2 * it + b] = mixed + weight_alone * r.class_first[2 * it + b]
        return carry

    lax.fori_loop(0, pairs // 2, class_forward, 0, unroll=2)
    if inside:
        pl.semaphore_wait(barrier, 2 * n_img - 1)
        to_peers(r.w_own.at[seg], r.w_all.at[seg, me], r.l_weights)
        to_peers(r.s_own.at[seg], r.s_all.at[seg, me], r.l_shrink)
    lax.fori_loop(pairs // 2, pairs, class_forward, 0, unroll=2)

    mixed = r.mixed[...].reshape(rows * HEADS8, width).astype(BF16)
    class_context = gather_heads(nn(mixed, r.frozen_triple[:, 2 * width :])).astype(BF16)
    class_middle = class_in + nn(class_context, r.frozen_merge[...])
    class_unit_b, _, _ = standardize(class_middle, 1)
    class_second = (class_unit_b * regain_row).astype(BF16)
    class_active, class_slope = gelu_pair(nn(class_second, r.frozen_expand[...]))
    class_out = class_middle + nn(class_active.astype(BF16), r.frozen_shrink[...])
    r.class_context[...] = class_context.astype(F32)
    r.class_middle[...] = class_middle
    r.class_slope[...] = class_slope
    r.class_out[...] = class_out.astype(BF16)
    if inside:
        to_other_segment(r.class_out, r.crossed.at[me], r.l_crossed)

    def region():
        keys = n_img * rows
        wait_all(r.crossed, r.l_crossed.at[1])
        sibling(r.w_all.at[seg], r.w_all.at[seg], r.l_forward).wait()
        sibling(r.s_all.at[seg], r.s_all.at[seg], r.l_forward_shrink).wait()
        half = shard_ff // 2
        for j in range(n_img):
            for k in range(2):
                down = shard_ff * j + half * k
                r.region_shrink[down : down + half, :] = r.s_all[k, j]
        deep = PAD * n_img
        w_triple = r.w_all[0, :, :, 0 : 3 * width].reshape(deep, 3 * width)
        w_merge = r.w_all[0, :, :, 3 * width :].reshape(deep, width)
        w_expand = r.w_all[1].reshape(deep, hidden)
        ups, wide = [], [[], []]
        for j in range(n_img):
            fill = r.w_all[seg, j].astype(F32)[shard:PAD]
            ups += [fill[:, width * k : width * (k + 1)] for k in range(rows // 8)]
            for k in range(2):
                first_at = width * (rows // 8) + 128 * (shard // 8) * k
                for at in range(first_at, first_at + 128 * (shard // 8), 128):
                    wide[k].append(fill[:, at : at + 128])
        wide = [jnp.concatenate(w, axis=0) for w in wide]
        gain, regain = (jnp.concatenate([g] * (keys // 128), axis=1) for g in wide)
        upstream = jnp.concatenate(ups, axis=0).T.astype(BF16)

        slots = r.region_number.shape[1]
        per = slots // n_img
        micros = rows // per
        numbers = r.region_number[...].astype(F32)
        numbers = jnp.concatenate([numbers, jnp.zeros((8 - micros, slots), F32)], axis=0)
        at = lax.broadcasted_iota(jnp.int32, (slots, keys), 1)
        slot = lax.broadcasted_iota(jnp.int32, (slots, keys), 0)
        chosen = slot == per * (at // rows) + lax.rem(at, per)
        numbers = nn(numbers.astype(BF16), jnp.where(chosen, 1.0, 0.0).astype(BF16))
        at = lax.rem(lax.broadcasted_iota(jnp.int32, (1, keys), 1), rows) // per
        code = jnp.zeros((1, keys), F32)
        for m in range(micros):
            code = jnp.where(at == m, numbers[m : m + 1, :] * micros + m, code)
        code_down = jnp.broadcast_to(code, (128, keys)).T
        code_down = jnp.concatenate([code_down] * (keys // 128), axis=1)
        bias = jnp.where(code_down == code, 0.0, NEG)

        qkv, probs, ctx = r.qkv, r.probs, r.ctx
        values = r.crossed[...].reshape(keys, width).T.astype(F32)
        unit, _, inverse = standardize(values, 0)
        r.region_first[...] = padded(unit * gain, shard, n_img).astype(BF16)
        packed = tn(w_triple, r.region_first[...])
        qkv[0:width, 0:keys] = (packed[0:width] * (LOG2E * HD ** (-0.5))).astype(BF16)
        qkv[width:, 0:keys] = packed[width:].astype(BF16)

        def part(which, h):
            return qkv[which * width + HD * h : which * width + HD * (h + 1), 0:keys]

        mixes, scores = [], [tn(part(1, 0), part(0, 0))]
        for h in range(heads):
            if h + 1 < heads:
                scores.append(tn(part(1, h + 1), part(0, h + 1)))
            biased = scores[h] + bias
            weights = jnp.exp2(biased - jnp.max(biased, axis=0, keepdims=True))
            r.shares[0, h : h + 1, :] = 1.0 / jnp.sum(weights, axis=0, keepdims=True)
            probs[h] = weights.astype(BF16)
            if h:
                mixes.append(nn(part(2, h - 1), probs[h - 1]) * r.shares[0, h - 1 : h, :])
        mixes.append(nn(part(2, heads - 1), probs[heads - 1]) * r.shares[0, heads - 1 : heads, :])
        context = jnp.concatenate(mixes, axis=0)
        r.region_context[...] = padded(context, shard, n_img).astype(BF16)
        middle = values + tn(w_merge, r.region_context[...])
        unit_b, _, inverse_b = standardize(middle, 0)
        r.region_second[...] = padded(unit_b * regain, shard, n_img).astype(BF16)
        for c in range(0, hidden, width):
            at = slice(c, c + width)
            active, slope = gelu_pair(tn(w_expand[:, at], r.region_second[...]))
            r.region_active[at, :] = active.astype(BF16)
            r.slope[at, 0:keys] = slope.astype(BF16)
        result = middle + tn(r.region_shrink[...], r.region_active[...])
        mine = pl.ds(pl.multiple_of(me * rows, rows), rows)
        r.region_rows[...] = result.T
        r.region_out[...] = r.region_rows[mine, :].astype(BF16)

        for c in range(0, hidden, width):
            at = slice(c, c + width)
            active_grad = nn(r.region_shrink[at, :], upstream)
            r.active[at, 0:keys] = (active_grad * r.slope[at, 0:keys].astype(F32)).astype(BF16)
        hidden_low = r.active[:, 0:keys]
        second_grad = trimmed(nn(w_expand, hidden_low), shard, n_img)
        middle_grad = upstream.astype(F32) + norm_back(second_grad * regain, unit_b, inverse_b, 0)
        middle_low = middle_grad.astype(BF16)
        context_grad = trimmed(nn(w_merge, middle_low), shard, n_img)
        packed_grad = r.packed_grad
        lows, totals = [], []
        for h in range(heads):
            at = slice(HD * h, HD * (h + 1))
            low = context_grad[at] * r.shares[0, h : h + 1, :]
            totals.append(jnp.sum(low * context[at], axis=0, keepdims=True))
            lows.append(low.astype(BF16))

        def put(which, h, grad):
            packed_grad[which * width + HD * h : which * width + HD * (h + 1), 0:keys] = (
                grad.astype(BF16)
            )

        def key_and_query(h, score_grad):
            put(1, h, nt(part(0, h), score_grad) * LN2)
            put(0, h, nn(part(1, h), score_grad) * HD ** (-0.5))

        grads, score_grads = [tn(part(2, 0), lows[0])], []
        for h in range(heads):
            if h + 1 < heads:
                grads.append(tn(part(2, h + 1), lows[h + 1]))
            put(2, h, nt(lows[h], probs[h]))
            score_grad = probs[h].astype(F32) * (grads[h] - totals[h])
            score_grads.append(score_grad.astype(BF16))
            if h:
                key_and_query(h - 1, score_grads[h - 1])
        key_and_query(heads - 1, score_grads[heads - 1])
        first_grad = trimmed(nn(w_triple, packed_grad[:, 0:keys]), shard, n_img)
        back = norm_back(first_grad * gain, unit, inverse, 0)
        r.region_rows[...] = (middle_grad + back).T
        r.crossed_grad[...] = r.region_rows[mine, :].astype(BF16)
        sibling(r.crossed_grad, r.returned, r.l_returned).start()

        mine = pl.ds(pl.multiple_of(me * PAD, PAD), PAD)
        grads = r.grads
        grads[:, 0 : 3 * width] = nt(r.region_first[mine, :], packed_grad[:, 0:keys])[0:shard]
        grads[:, 3 * width : 4 * width] = nt(r.region_context[mine, :], middle_low)[0:shard]
        grads[:, 4 * width : 4 * width + hidden] = nt(r.region_second[mine, :], hidden_low)[0:shard]
        mine = pl.ds(pl.multiple_of(me * shard_ff, shard_ff), shard_ff)
        r.grads_shrink[...] = nt(r.region_active[mine, :], upstream)
        mine = pl.ds(pl.multiple_of(me * shard, shard), shard)
        for k, (grad, standard) in enumerate(((first_grad, unit), (second_grad, unit_b))):
            total = jnp.sum(grad * standard, axis=1, keepdims=True)
            r.gain_columns[...] = jnp.broadcast_to(total, (width, 128))
            at = 4 * width + hidden + 128 * k
            grads[:, at : at + 128] = r.gain_columns[mine, :]
        sibling(grads, r.grads_in, r.l_grads).start()
        sibling(r.grads_shrink, r.grads_shrink_in, r.l_grads_shrink).start()

    def one_pair(it, carry):
        pair_copy(r.cotangent, r.cot, r.cot_sem, it).wait()
        patch_pair(r, dims, it, it, jnp.minimum(it + 1, pairs - 1))
        pair_copy(r.tok, r.patch_rows, r.out_sem, it).start()
        one_copy(r.input_grad, r.grad_rows, r.grad_sem, it).start()

        if inside:

            @pl.when(it == AT_FORWARD)
            def _():
                wait_all(r.w_all.at[seg], r.l_weights.at[1])
                wait_all(r.s_all.at[seg], r.l_shrink.at[1])
                sibling(r.w_all.at[seg], r.w_all.at[seg], r.l_forward).start()
                sibling(r.s_all.at[seg], r.s_all.at[seg], r.l_forward_shrink).start()

            pl.when(it == AT_REGION)(region)
        return carry

    for it in range(pairs):
        one_copy(r.firstT, r.first_rows, r.first_sem, it).start()
    project(r, dims, 0)
    lax.fori_loop(0, dims.early, one_pair, 0)

    if inside:
        sibling(r.crossed_grad, r.returned, r.l_returned).wait()
        sibling(r.grads, r.grads_in, r.l_grads).wait()
        sibling(r.grads_shrink, r.grads_shrink_in, r.l_grads_shrink).wait()
        r.class_up[...] = r.returned[...]
        r.grads_out[...] = r.grads[...] + r.grads_in[...]
        r.shrink_out[...] = r.grads_shrink[...] + r.grads_shrink_in[...]
        peers = pl.ds(0, n_img - 1)
        wait_all(r.w_all.at[0, peers], r.l_weights.at[0])
        wait_all(r.s_all.at[0, peers], r.l_shrink.at[0])
        wait_all(r.crossed, r.l_crossed.at[0])
    for it in range(pairs):
        one_copy(r.firstT, r.first_rows, r.first_sem, it).wait()
    for it in range(dims.early):
        pair_copy(r.tok, r.patch_rows, r.out_sem, it).wait()
        one_copy(r.input_grad, r.grad_rows, r.grad_sem, it).wait()
    for k, (turned, target) in enumerate(turns):
        pltpu.make_async_copy(turned, target, r.turn_sem.at[k]).wait()


def finish_kernel(dims, *refs):
    r = SimpleNamespace(**dict(zip(dims.names, refs, strict=True)))
    width, hidden = dims.width, dims.hidden
    rows, patches, early = dims.images, dims.patches, dims.early
    pairs, lanes = rows // 2, 2 * patches
    late = pairs - early

    loads = []
    for k, name in enumerate(dims.staged):
        load = pltpu.make_async_copy(getattr(r, name), getattr(r, name + BESIDE), r.load_sem.at[k])
        setattr(r, name, getattr(r, name + BESIDE))
        loads.append(load)
    last = pl.ds(2 * early, 2 * late)
    tok_in = pltpu.make_async_copy(r.tokens.at[last], r.tok, r.late_sem.at[0])
    cot_in = pltpu.make_async_copy(r.cotangent.at[last], r.cot, r.late_sem.at[1])
    ready = pl.ds(0, 2 * early)
    rows_in = pltpu.make_async_copy(r.patch_rows.at[ready], r.ready, r.late_sem.at[2])
    rows_out = pltpu.make_async_copy(r.ready, r.patch_output.at[ready], r.late_sem.at[4])
    firsts = [one_copy(r.first_rows, r.firstT, r.first_sem, it) for it in range(pairs)]
    earlier = [one_copy(r.grad_rows, r.input_grad, r.grad_sem, it) for it in range(early)]
    bounds = (0,) + dims.bounds
    stages = [loads[a:b] for a, b in zip(bounds, bounds[1:])]
    stages[0] = firsts[early:] + [tok_in] + stages[0]
    stages[1] = [cot_in] + stages[1]
    for stage in stages + [firsts[:early] + earlier + [rows_in]]:
        for load in stage:
            load.start()

    def ready(stage):
        for load in stages[stage]:
            load.wait()

    ready(0)
    gain_row = r.frozen_gain[...].astype(F32).reshape(1, width)
    regain_row = r.frozen_regain[...].astype(F32).reshape(1, width)
    r.gainT[...] = column(gain_row, lanes)
    r.regainT[...] = column(regain_row, lanes)
    packed = r.class_packed[...]
    tall_k = spread(packed[:, width : 2 * width])
    tall_v = spread(packed[:, 2 * width :])
    r.class_k[...] = tall_k.reshape(rows, HEADS8, width)
    r.class_v[...] = tall_v.reshape(rows, HEADS8, width)
    project(r, dims, early)
    for it in range(early, pairs):
        following = it + 1 if it + 1 < pairs else None
        wait = ready if it == early else lambda stage: None
        patch_pair(r, dims, it, it - early, following, wait)
    ready(3)
    out = pltpu.make_async_copy(r.tok, r.patch_output.at[last], r.late_sem.at[3])
    out.start()

    upstream = r.class_up[...]
    middle = r.class_middle[...]
    unit, _, inverse = standardize(middle, 1)
    hidden_low = (nt(upstream, r.frozen_shrink[...]) * r.class_slope[...]).astype(BF16)
    second_grad = nt(hidden_low, r.frozen_expand[...])
    middle_grad = upstream.astype(F32) + norm_back(second_grad * regain_row, unit, inverse, 1)
    low = nt(middle_grad.astype(BF16), r.frozen_merge[...]).astype(BF16).astype(F32)
    tall_low = spread(low)
    low_map = nt(tall_low.astype(BF16), r.frozen_triple[:, 2 * width :])
    r.low_map[...] = low_map.reshape(rows, HEADS8, width)
    total = jnp.sum(spread(low * r.class_context[...]), axis=1, keepdims=True)
    r.class_total[...] = jnp.broadcast_to(total, (rows * HEADS8, 128)).reshape(rows, HEADS8, 128)
    r.ungainT[...] = 1.0 / r.gainT[:, 0:patches]
    for load in firsts[:early] + earlier + [rows_in]:
        load.wait()
    rows_out.start()

    def correct(it, carry):
        first = r.firstT[it]
        inverse = r.stat[it, 1:2, :]
        left, right, along = [], [], []
        maps = jnp.concatenate([r.low_map[2 * it + b] for b in range(2)], axis=0)
        probs_grads = nn(maps.astype(BF16), first)
        for b in range(2):
            image = 2 * it + b
            span = slice(b * patches, (b + 1) * patches)
            part = probs_grads[b * HEADS8 : (b + 1) * HEADS8, span]
            weights = r.class_probs[image]
            score_grad = weights * (part - r.class_total[image][:, 0:1])
            r.mixed[image] = nt(score_grad.astype(BF16), first[:, span])
            toward = jnp.concatenate([r.query_map[image], r.low_map[image]], axis=0) * gain_row
            left.append((toward - mean(toward, 1)).astype(BF16))
            scaled = jnp.concatenate([score_grad * LN2, weights], axis=0) * inverse[:, span]
            right.append(scaled.astype(BF16))
            scores = jnp.concatenate([r.class_scores[image], part], axis=0)
            along.append(jnp.sum(scaled * scores, axis=0, keepdims=True) * (1.0 / width))
        for b in range(2):
            span = slice(b * patches, (b + 1) * patches)
            back = tn(left[b], right[b]) - first[:, span].astype(F32) * (r.ungainT[...] * along[b])
            result = r.input_grad[it, :, span].astype(F32) + back
            r.result[2 * it + b] = result.astype(BF16).T
        pair_copy(r.result, r.patch_gradient, r.back_sem, it).start()
        return carry

    lax.fori_loop(0, pairs, correct, 0, unroll=2)

    self_prob = r.self_prob[...].reshape(rows * HEADS8, 128)[:, 0:1]
    tall_q = spread(packed[:, 0:width])
    self_grad = self_prob * (jnp.sum(tall_low * tall_v, axis=1, keepdims=True) - total)
    unit, _, inverse = standardize(r.class_tokens[...].astype(F32), 1)
    first = (unit * gain_row).astype(BF16).astype(F32)
    tall_first = jnp.broadcast_to(first[:, None, :], (rows, HEADS8, width))
    mixed = r.mixed[...].reshape(rows * HEADS8, width)
    mixed = mixed + self_grad * tall_first.reshape(rows * HEADS8, width)
    triple = r.frozen_triple
    query_grad = gather_heads(nn(mixed.astype(BF16), triple[:, width : 2 * width]))
    key_grad = r.class_dk[...] + (tall_q * (self_grad * HD ** (-0.5))).reshape(
        rows, HEADS8, width
    )
    value_grad = r.class_dv[...] + (tall_low * self_prob).reshape(rows, HEADS8, width)
    packed_grad = jnp.concatenate(
        [query_grad * HD ** (-0.5), jnp.sum(key_grad, axis=1), jnp.sum(value_grad, axis=1)],
        axis=1,
    ).astype(BF16)
    first_grad = nt(packed_grad, triple[...])
    back = norm_back(first_grad * gain_row, unit, inverse, 1)
    r.class_gradient[...] = (middle_grad + back).astype(BF16)
    if dims.inside:
        wide = width * 4 + hidden
        r.region_output[...] = r.region_out[...]
        r.triple_gradient[...] = r.grads_out[:, 0 : 3 * width]
        r.merge_gradient[...] = r.grads_out[:, 3 * width : 4 * width]
        r.expand_gradient[...] = r.grads_out[:, 4 * width : wide]
        r.shrink_gradient[...] = r.shrink_out[...]
        shard = r.grads_out.shape[0]
        blank = jnp.zeros((128 - shard, 128), F32)
        for k, target in enumerate((r.first_gradient, r.second_gradient)):
            columns = r.grads_out[:, wide + 128 * k : wide + 128 * (k + 1)]
            columns = jnp.concatenate([columns, blank], axis=0).T
            target[...] = columns[0:1, 0:shard]
    rows_out.wait()
    out.wait()
    for it in range(pairs):
        pair_copy(r.result, r.patch_gradient, r.back_sem, it).wait()


def normalize(values, scaling):
    centred = values - jnp.mean(values, axis=-1, keepdims=True)
    inverse = lax.rsqrt(jnp.mean(centred * centred, axis=-1, keepdims=True) + EPSILON)
    standard = centred * inverse
    return (standard * scaling, standard, inverse)


def normalize_back(upstream, standard, inverse, scaling):
    scaled = upstream * scaling
    centred = scaled - jnp.mean(scaled, axis=-1, keepdims=True)
    centred = centred - standard * jnp.mean(scaled * standard, axis=-1, keepdims=True)
    gain_grad = jnp.sum((upstream * standard).reshape(-1, upstream.shape[-1]), axis=0)
    return (centred * inverse, gain_grad)


def gelu_slope(hidden):
    return (
        0.5 * (1.0 + lax.erf(hidden * 0.7071067811865476))
        + hidden * jnp.exp(-0.5 * hidden * hidden) * 0.3989422804014327
    )


def forward_product(operand, weight):
    return lax.dot_general(
        operand, weight, (((operand.ndim - 1,), (0,)), ((), ())), preferred_element_type=F32
    )


def backward_product(upstream, weight):
    return lax.dot_general(
        upstream,
        weight,
        (((upstream.ndim - 1,), (1,)), ((), ())),
        preferred_element_type=F32,
    )


def row_product(operand, cotangent):
    left_rows = operand.reshape(-1, operand.shape[-1])
    right_rows = cotangent.reshape(-1, cotangent.shape[-1])
    return lax.dot_general(
        left_rows, right_rows, (((0,), (0,)), ((), ())), preferred_element_type=F32
    )


def heads_of(packed, portion):
    section_width = packed.shape[-1] // 3
    section = packed[..., portion * section_width : (portion + 1) * section_width]
    return section.reshape(packed.shape[:-1] + (section_width // HD, HD))


def raw_scores(queries, keyset, allowed):
    scores = jnp.einsum(
        "bqhd,bkhd->bhqk", queries, keyset, preferred_element_type=F32
    ) * HD ** (-0.5)
    if allowed is None:
        return scores
    return jnp.where(allowed[:, None], scores, -1e30)


def attend(queries, keyset, valueset, allowed):
    scores = raw_scores(queries, keyset, allowed)
    highest = jnp.max(scores, axis=-1, keepdims=True)
    logsum = highest + jnp.log(jnp.sum(jnp.exp(scores - highest), axis=-1, keepdims=True))
    weighting = jnp.exp(scores - logsum).astype(BF16)
    context = jnp.einsum("bhqk,bkhd->bqhd", weighting, valueset, preferred_element_type=F32)
    return (context.astype(BF16), logsum)


def score_terms(queries, keyset, valueset, allowed, logsum, context_grad):
    scores = raw_scores(queries, keyset, allowed)
    weighting = jnp.exp(scores - logsum)
    weight_grad = jnp.einsum(
        "bqhd,bkhd->bhqk", context_grad, valueset, preferred_element_type=F32
    )
    row_total = jnp.sum(weighting * weight_grad, axis=-1, keepdims=True)
    score_grad = (weighting * (weight_grad - row_total)).astype(BF16)
    return (weighting, score_grad, row_total)


def attend_back(queries, keyset, valueset, allowed, logsum, context_grad):
    weighting, score_grad, row_total = score_terms(
        queries, keyset, valueset, allowed, logsum, context_grad
    )
    value_grad = jnp.einsum(
        "bhqk,bqhd->bkhd",
        weighting.astype(BF16),
        context_grad,
        preferred_element_type=F32,
    )
    query_grad = jnp.einsum(
        "bhqk,bkhd->bqhd", score_grad, keyset, preferred_element_type=F32
    ) * HD ** (-0.5)
    key_grad = jnp.einsum(
        "bhqk,bqhd->bkhd", score_grad, queries, preferred_element_type=F32
    ) * HD ** (-0.5)
    return (query_grad, key_grad, value_grad)


def block_head(inputs, scaling, triple):
    normed, standard, inverse = normalize(inputs, scaling)
    first_low = normed.astype(BF16)
    packed = forward_product(first_low, triple).astype(BF16)
    return (first_low, standard, inverse, packed)


def block_tail(inputs, context, regain, merger, expand, shrink):
    middle = inputs + forward_product(context, merger)
    normed, standard, inverse = normalize(middle, regain)
    second = normed.astype(BF16)
    hidden = forward_product(second, expand)
    active = jax.nn.gelu(hidden, approximate=False).astype(BF16)
    result = middle + forward_product(active, shrink)
    return (result, (standard, inverse, second, hidden, active))


def tail_back(upstream, kept_tail, regain, merger, expand, shrink):
    standard, inverse, second, hidden, active = kept_tail
    out_low = upstream.astype(BF16)
    active_grad = backward_product(out_low, shrink)
    hidden_low = (active_grad * gelu_slope(hidden)).astype(BF16)
    second_grad = backward_product(hidden_low, expand)
    norm_grad, regain_grad = normalize_back(second_grad, standard, inverse, regain)
    middle_grad = upstream + norm_grad
    middle_low = middle_grad.astype(BF16)
    context_low = backward_product(middle_low, merger).astype(BF16)
    return (middle_grad, context_low, regain_grad, (middle_low, hidden_low, out_low))


def region_outside(crossed, region_number, region_cotangent, shards_in):
    crossed = lax.ppermute(crossed, SEG, [(0, 1), (1, 0)])
    images = crossed.shape[1]
    model_width = crossed.shape[2]
    gathered = [lax.all_gather(shard, IMG, axis=0, tiled=True) for shard in shards_in]
    full_gain, triple, merger, full_regain, expand, shrink = gathered
    scaling = full_gain.astype(F32)
    regain = full_regain.astype(F32)
    region_in = crossed.astype(F32)
    first_low, standard, inverse, packed = block_head(region_in, scaling, triple)
    local_keys = packed[..., model_width : 2 * model_width]
    local_values = packed[..., 2 * model_width :]
    all_keys, all_values = (
        lax.all_gather(local_keys, IMG, axis=1, tiled=True),
        lax.all_gather(local_values, IMG, axis=1, tiled=True),
    )
    head_shape = all_keys.shape[:-1] + (model_width // HD, HD)
    keyset = all_keys.reshape(head_shape)
    valueset = all_values.reshape(head_shape)
    queries = heads_of(packed, 0)
    first_slot = lax.axis_index(IMG) * images
    own_number = lax.dynamic_slice_in_dim(region_number, first_slot, images, 1)
    allowed = own_number[:, :, None] == region_number[:, None, :]
    context, logsum = attend(queries, keyset, valueset, allowed)
    context = context.reshape(region_in.shape)
    region_result, kept_tail = block_tail(region_in, context, regain, merger, expand, shrink)
    region_output = region_result.astype(BF16)
    upstream = region_cotangent.astype(F32)
    middle_grad, context_low, second_gain_grad, low_rows = tail_back(
        upstream, kept_tail, regain, merger, expand, shrink
    )
    middle_low, hidden_low, out_low = low_rows
    context_heads = context_low.reshape(queries.shape)
    query_grad, key_grad, value_grad = attend_back(
        queries, keyset, valueset, allowed, logsum, context_heads
    )
    key_sum, value_sum = (
        lax.psum_scatter(key_grad.reshape(all_keys.shape), IMG, scatter_dimension=1, tiled=True),
        lax.psum_scatter(
            value_grad.reshape(all_values.shape), IMG, scatter_dimension=1, tiled=True
        ),
    )
    packed_grad = jnp.concatenate(
        [query_grad.reshape(region_in.shape), key_sum, value_sum], axis=-1
    ).astype(BF16)
    norm_grad, first_gain_grad = normalize_back(
        backward_product(packed_grad, triple), standard, inverse, scaling
    )
    input_grad = (middle_grad + norm_grad).astype(BF16)
    second_low = kept_tail[2]
    active_low = kept_tail[4]
    shards = (
        lax.psum_scatter(first_gain_grad, IMG, scatter_dimension=0, tiled=True),
        lax.psum_scatter(
            row_product(first_low, packed_grad), IMG, scatter_dimension=0, tiled=True
        ),
        lax.psum_scatter(row_product(context, middle_low), IMG, scatter_dimension=0, tiled=True),
        lax.psum_scatter(second_gain_grad, IMG, scatter_dimension=0, tiled=True),
        lax.psum_scatter(
            row_product(second_low, hidden_low), IMG, scatter_dimension=0, tiled=True
        ),
        lax.psum_scatter(row_product(active_low, out_low), IMG, scatter_dimension=0, tiled=True),
    )
    totals = tuple(lax.psum(shard.astype(BF16), SEG).astype(F32) for shard in shards)
    return region_output, lax.ppermute(input_grad, SEG, [(0, 1), (1, 0)]), totals


def local(
    n_img,
    patch_tokens,
    class_tokens,
    region_number,
    frozen_gain,
    frozen_triple,
    frozen_merge,
    frozen_regain,
    frozen_expand,
    frozen_shrink,
    gain_first,
    weight_triple,
    weight_merge,
    gain_second,
    weight_expand,
    weight_shrink,
    patch_cotangent,
    region_cotangent,
):
    micros, per, patches, width = patch_tokens.shape
    hidden = frozen_expand.shape[1]
    images = micros * per
    shard, shard_ff = width // n_img, hidden // n_img
    lanes, pairs, keys, heads = 2 * patches, images // 2, n_img * images, width // HD
    inside = keys == patches and shard == PAD - 8 and images == 16 and width == 384

    class_rows = class_tokens.reshape(images, width)
    inputs = dict(
        tokens=patch_tokens.reshape(images, patches, width),
        cotangent=patch_cotangent.reshape(images, patches, width),
        class_tokens=class_rows,
        frozen_gain=frozen_gain,
        frozen_regain=frozen_regain,
        frozen_triple=frozen_triple,
        frozen_merge=frozen_merge,
        frozen_expand=frozen_expand,
        frozen_shrink=frozen_shrink,
    )
    if inside:
        inputs |= dict(
            gain_first=gain_first,
            gain_second=gain_second,
            region_cotangent=region_cotangent.reshape(images, width),
            region_number=region_number,
            weight_triple=weight_triple,
            weight_merge=weight_merge,
            weight_expand=weight_expand,
            weight_shrink=weight_shrink,
        )
    vmem = pl.BlockSpec(memory_space=pltpu.VMEM)
    hbm = pl.BlockSpec(memory_space=pl.ANY)
    streams = 2
    in_specs = [hbm] * streams + [vmem] * (len(inputs) - streams)

    shape = jax.ShapeDtypeStruct
    columns = 4 * width + hidden + 256
    large = dict(
        patch_rows=shape((images, patches, width), BF16),
        first_rows=shape((pairs, width, lanes), BF16),
        grad_rows=shape((pairs, width, lanes), BF16),
        triple_turned=shape((3 * width, width), BF16),
        merge_turned=shape((width, width), BF16),
        expand_turned=shape((hidden, width), BF16),
        shrink_turned=shape((width, hidden), BF16),
    )
    small = dict(
        stat=shape((pairs, 8, lanes), F32),
        class_packed=shape((images, 3 * width), F32),
        class_context=shape((images, width), F32),
        class_middle=shape((images, width), F32),
        class_slope=shape((images, hidden), F32),
        query_map=shape((images, HEADS8, width), F32),
        class_probs=shape((images, HEADS8, patches), F32),
        class_scores=shape((images, HEADS8, patches), F32),
        self_prob=shape((images, HEADS8, 128), F32),
        class_dk=shape((images, HEADS8, width), F32),
        class_dv=shape((images, HEADS8, width), F32),
    )
    if inside:
        small |= dict(
            class_up=shape((images, width), BF16),
            region_out=shape((images, width), BF16),
            grads_out=shape((shard, columns), F32),
            shrink_out=shape((shard_ff, width), F32),
        )
    else:
        small |= dict(class_out=shape((images, width), BF16))
    outputs = large | small
    out_specs = [hbm] * len(large) + [vmem] * len(small)

    v = pltpu.VMEM
    dma = pltpu.SemaphoreType.DMA
    working = dict(
        gainT=v((width, lanes), F32),
        regainT=v((width, lanes), F32),
        qkv=v((3 * width, lanes), BF16),
        ctx=v((width, lanes), BF16),
        probs=v((2 * heads, patches, patches), BF16),
        shares=v((2, HEADS8, patches), F32),
        class_weights=v((2, HEADS8, patches), F32),
        active=v((hidden, lanes), BF16),
        slope=v((hidden, lanes), BF16),
        packed_grad=v((3 * width, lanes), BF16),
        low_grad=v((width, lanes), BF16),
        class_k=v((images, HEADS8, width), F32),
        class_v=v((images, HEADS8, width), F32),
        mixed=v((images, HEADS8, width), F32),
        firstT=v((pairs, width, lanes), BF16),
        input_grad=v((pairs, width, lanes), BF16),
        first_sem=dma((pairs,)),
        grad_sem=dma((pairs,)),
    )
    turned = dict(
        tripleT=v((3 * width, width), BF16),
        mergeT=v((width, width), BF16),
        expandT=v((hidden, width), BF16),
        shrinkT=v((width, hidden), BF16),
    )
    scratch = working | turned | dict(
        tok=v((images, patches, width), BF16),
        cot=v((images, patches, width), BF16),
        class_first=v((images, HEADS8, width), F32),
        self_score=v((images, HEADS8, 128), F32),
        tok_sem=dma((pairs,)),
        cot_sem=dma((pairs,)),
        out_sem=dma((pairs,)),
        turn_sem=dma((len(turned),)),
    )
    if inside:
        deep = PAD * n_img
        scratch |= dict(
            class_out=v((images, width), BF16),
            crossed=v((n_img, images, width), BF16),
            crossed_grad=v((images, width), BF16),
            returned=v((images, width), BF16),
            shard_gains=v((8, 128), F32),
            w_own=v((2, PAD, 4 * width), BF16),
            w_all=v((2, n_img, PAD, 4 * width), BF16),
            s_own=v((2, shard_ff // 2, width), BF16),
            s_all=v((2, n_img, shard_ff // 2, width), BF16),
            region_shrink=v((hidden, width), BF16),
            region_first=v((deep, keys), BF16),
            region_context=v((deep, keys), BF16),
            region_second=v((deep, keys), BF16),
            region_active=v((hidden, keys), BF16),
            region_rows=v((keys, width), F32),
            gain_columns=v((width, 128), F32),
            grads=v((shard, columns), F32),
            grads_in=v((shard, columns), F32),
            grads_shrink=v((shard_ff, width), F32),
            grads_shrink_in=v((shard_ff, width), F32),
            l_weights=dma((2,)),
            l_shrink=dma((2,)),
            l_forward=dma((2,)),
            l_forward_shrink=dma((2,)),
            l_crossed=dma((2,)),
            l_returned=dma((2,)),
            l_grads=dma((2,)),
            l_grads_shrink=dma((2,)),
        )
    sizes = dict(
        n_img=n_img,
        width=width,
        hidden=hidden,
        images=images,
        patches=patches,
        inside=inside,
        early=pairs - LATE,
    )
    limit = dict(vmem_limit_bytes=60 * 1024 * 1024)
    remote = dict(collective_id=0, has_side_effects=True) if inside else {}
    names = list(inputs) + list(outputs) + list(scratch)
    results = pl.pallas_call(
        functools.partial(patch_kernel, SimpleNamespace(names=names, **sizes)),
        out_shape=list(outputs.values()),
        in_specs=in_specs,
        out_specs=out_specs,
        scratch_shapes=list(scratch.values()),
        compiler_params=pltpu.CompilerParams(**limit, **remote),
    )(*inputs.values())
    done = dict(zip(outputs, results, strict=True))

    if not inside:
        class_out = done.pop(list(small)[-1])
        region_output, class_up, grads = region_outside(
            class_out.reshape(class_tokens.shape),
            region_number,
            region_cotangent,
            (gain_first, weight_triple, weight_merge, gain_second, weight_expand, weight_shrink),
        )
        done |= dict(class_up=class_up.reshape(images, width))

    streamed = [done.pop(name) for name in large]
    done = SimpleNamespace(**done)
    tripleT, mergeT, expandT, shrinkT = streamed[-len(turned) :]
    stages = (
        dict(class_packed=done.class_packed, stat=done.stat, tripleT=tripleT),
        dict(mergeT=mergeT, frozen_shrink=frozen_shrink, expandT=expandT),
        dict(
            shrinkT=shrinkT,
            frozen_expand=frozen_expand,
            frozen_merge=frozen_merge,
            frozen_triple=frozen_triple,
            class_dk=done.class_dk,
            class_dv=done.class_dv,
        ),
        dict(class_tokens=class_rows) | vars(done),
    )
    staged, bounds = {}, ()
    for stage in stages:
        staged |= {name: a for name, a in stage.items() if name not in staged}
        bounds += (len(staged),)
    inputs = dict(
        tokens=patch_tokens.reshape(images, patches, width),
        cotangent=patch_cotangent.reshape(images, patches, width),
        patch_rows=streamed[0],
        first_rows=streamed[1],
        grad_rows=streamed[2],
    )
    inputs |= staged
    inputs |= dict(frozen_gain=frozen_gain, frozen_regain=frozen_regain)
    outputs = dict(
        patch_output=shape((images, patches, width), BF16),
        patch_gradient=shape((images, patches, width), BF16),
        class_gradient=shape((images, width), BF16),
    )
    out_specs = [hbm] * 2 + [vmem]
    if inside:
        ready = dict(
            region_output=shape((images, width), BF16),
            first_gradient=shape((1, shard), F32),
            triple_gradient=shape((shard, 3 * width), F32),
            merge_gradient=shape((shard, width), F32),
            second_gradient=shape((1, shard), F32),
            expand_gradient=shape((shard, hidden), F32),
            shrink_gradient=shape((shard_ff, width), F32),
        )
        outputs |= ready
        out_specs += [vmem] * len(ready)
    scratch = working | dict(
        tok=v((2 * LATE, patches, width), BF16),
        cot=v((2 * LATE, patches, width), BF16),
        result=v((images, patches, width), BF16),
        ungainT=v((width, patches), F32),
        low_map=v((images, HEADS8, width), F32),
        class_total=v((images, HEADS8, 128), F32),
        load_sem=dma((len(staged),)),
        ready=v((images - 2 * LATE, patches, width), BF16),
        late_sem=dma((5,)),
        back_sem=dma((pairs,)),
    )
    scratch |= {name + BESIDE: v(a.shape, a.dtype) for name, a in staged.items()}
    names = list(inputs) + list(outputs) + list(scratch)
    sizes |= dict(names=names, staged=list(staged), bounds=bounds)
    results = pl.pallas_call(
        functools.partial(finish_kernel, SimpleNamespace(**sizes)),
        out_shape=list(outputs.values()),
        in_specs=[hbm] * (len(inputs) - 2) + [vmem] * 2,
        out_specs=out_specs,
        scratch_shapes=list(scratch.values()),
        compiler_params=pltpu.CompilerParams(**limit),
    )(*inputs.values())
    done = SimpleNamespace(**dict(zip(outputs, results, strict=True)))
    if inside:
        region_output = done.region_output.reshape(class_tokens.shape)
        grads = (
            done.first_gradient.reshape(shard),
            done.triple_gradient,
            done.merge_gradient,
            done.second_gradient.reshape(shard),
            done.expand_gradient,
            done.shrink_gradient,
        )
    return (
        done.patch_output.reshape(patch_tokens.shape),
        region_output,
        done.patch_gradient.reshape(patch_tokens.shape),
        done.class_gradient.reshape(class_tokens.shape),
        *grads,
    )


def solution(mesh):
    patch, row = P(SEG, IMG, None, None), P(SEG, IMG, None)
    gain, weight, whole = P(IMG), P(IMG, None), P()
    block = (gain, weight, weight, gain, weight, weight)
    placed = (patch, row, P(SEG, None)) + (whole,) * 6 + block + (patch, row)
    return jax.shard_map(
        functools.partial(local, mesh.shape[IMG]),
        mesh=mesh,
        in_specs=placed,
        out_specs=(patch, row, patch, row) + block,
        check_vma=False,
    )
```

```python
import functools
from types import SimpleNamespace

import jax
import jax.numpy as jnp
from jax import lax
from jax.experimental import pallas as pl
from jax.experimental.pallas import tpu as pltpu
from jax.sharding import PartitionSpec as P

SEG = "segment"
IMG = "img"
HD = 64
HEADS8 = 8
EPSILON = 1e-06
LOG2E = 1.4426950408889634
LN2 = 0.6931471805599453
ROOT_HALF = 0.7071067811865476
DENSITY = 0.3989422804014327
LOG2_DENSITY = -1.3257480647361593
F32 = jnp.float32
BF16 = jnp.bfloat16
MESH = pl.DeviceIdType.MESH
NEG = -1e30
PAD = 32
BESIDE = "_"

AT_FORWARD = 5
AT_REGION = 6
LATE = 1


def nn(a, b):
    return lax.dot_general(a, b, (((1,), (0,)), ((), ())), preferred_element_type=F32)


def nt(a, b):
    return lax.dot_general(a, b, (((1,), (1,)), ((), ())), preferred_element_type=F32)


def tn(a, b):
    return lax.dot_general(a, b, (((0,), (0,)), ((), ())), preferred_element_type=F32)


def mean(values, axis):
    return jnp.sum(values, axis=axis, keepdims=True) * (1.0 / values.shape[axis])


def standardize(values, axis):
    centre = mean(values, axis)
    centred = values - centre
    inverse = lax.rsqrt(mean(centred * centred, axis) + EPSILON)
    return centred * inverse, centre, inverse


def norm_back(scaled, standard, inverse, axis):
    return inverse * (
        scaled - mean(scaled, axis) - standard * mean(scaled * standard, axis)
    )


def gelu_pair(hidden):
    upto = 0.5 + 0.5 * lax.erf(hidden * ROOT_HALF)
    bell = jnp.exp2(hidden * hidden * (-0.5 * LOG2E))
    return hidden * upto, upto + hidden * (bell * DENSITY)


def gelu_pair_low(half):
    twice = (1.0 + lax.erf(half * (2.0 * ROOT_HALF))).astype(BF16)
    bell = jnp.exp2(half * half * (-2.0 * LOG2E) + (LOG2_DENSITY + 2.0)).astype(BF16)
    low = half.astype(BF16)
    return low * twice, twice + low * bell


def own_heads(rows, width):
    shape = (rows * HEADS8, width)
    lane = lax.broadcasted_iota(jnp.int32, shape, 1) // HD
    return lane == lax.rem(lax.broadcasted_iota(jnp.int32, shape, 0), HEADS8)


def spread(values):
    rows, width = values.shape
    tall = jnp.broadcast_to(values[:, None, :], (rows, HEADS8, width))
    return jnp.where(own_heads(rows, width), tall.reshape(rows * HEADS8, width), 0.0)


def gather_heads(values):
    tall, width = values.shape
    kept = jnp.where(own_heads(tall // HEADS8, width), values, 0.0)
    return jnp.sum(kept.reshape(tall // HEADS8, HEADS8, width), axis=1)


def column(row, lanes):
    tall = jnp.broadcast_to(row, (128, row.shape[1])).T
    return jnp.concatenate([tall] * (lanes // 128), axis=1)


def pair_copy(source, target, sems, it):
    part = pl.ds(2 * it, 2)
    return pltpu.make_async_copy(source.at[part], target.at[part], sems.at[it])


def one_copy(source, target, sems, it):
    return pltpu.make_async_copy(source.at[it], target.at[it], sems.at[it])


def padded(values, shard, n):
    blank = jnp.zeros((PAD - shard, values.shape[1]), values.dtype)
    parts = []
    for j in range(n):
        parts += [values[shard * j : shard * (j + 1)], blank]
    return jnp.concatenate(parts, axis=0)


def trimmed(values, shard, n):
    return jnp.concatenate([values[PAD * j : PAD * j + shard] for j in range(n)], axis=0)


def project(r, dims, it):
    width = dims.width
    first = r.firstT[it]
    queries = nn(r.tripleT[0:width, :], first) * (LOG2E * HD ** (-0.5))
    r.qkv[0:width, :] = queries.astype(BF16)
    r.qkv[width:, :] = nn(r.tripleT[width:, :], first).astype(BF16)


def patch_pair(r, dims, it, slot, following, ready=lambda stage: None):
    width, hidden, patches = dims.width, dims.hidden, dims.patches
    heads = width // HD
    block_head = own_heads(1, width)
    span = [slice(b * patches, (b + 1) * patches) for b in range(2)]
    qkv, ctx, probs = r.qkv, r.ctx, r.probs
    values = jnp.concatenate([r.tok[2 * slot + b].T for b in range(2)], axis=1).astype(F32)
    order = [(b, h) for h in range(heads) for b in range(2)]
    key_rows = [r.class_k[2 * it + b].astype(BF16) for b in range(2)]
    value_rows = [r.class_v[2 * it + b].astype(BF16) for b in range(2)]
    class_scores = [nn(key_rows[b], qkv[0:width, span[b]]) for b in range(2)]

    def part(which, turn):
        b, h = order[turn]
        return qkv[which * width + HD * h : which * width + HD * (h + 1), span[b]]

    scores, mixes, class_weights, shares = {0: tn(part(1, 0), part(0, 0))}, [], [], []
    for turn, (b, h) in enumerate(order):
        if turn + 1 < len(order):
            scores[turn + 1] = tn(part(1, turn + 1), part(0, turn + 1))
        class_score = class_scores[b][h : h + 1, :]
        top = jnp.maximum(jnp.max(scores[turn], axis=0, keepdims=True), class_score)
        weights = jnp.exp2(scores.pop(turn) - top)
        class_weight = jnp.exp2(class_score - top)
        shares.append(1.0 / (jnp.sum(weights, axis=0, keepdims=True) + class_weight))
        class_weights.append(class_weight)
        probs[b * heads + h] = weights.astype(BF16)
        if turn:
            last = order[turn - 1]
            mixes.append(nn(part(2, turn - 1), probs[last[0] * heads + last[1]]))
    mixes.append(nn(part(2, len(order) - 1), probs[2 * heads - 1]))
    blank = [jnp.zeros((HEADS8 - heads, patches), F32)]
    for b in range(2):
        weights = jnp.concatenate(class_weights[b::2] + blank, axis=0)
        r.class_weights[b] = weights
        r.shares[b] = jnp.concatenate(shares[b::2] + blank, axis=0)
        from_class = tn(value_rows[b], weights.astype(BF16))
        for h in range(heads):
            at = slice(HD * h, HD * (h + 1))
            mix = mixes[2 * h + b] + from_class[at]
            ctx[at, span[b]] = (mix * shares[2 * h + b]).astype(BF16)
    ready(1)
    merged = nn(r.mergeT[...], ctx[...])
    upstream = jnp.concatenate([r.cot[2 * slot + b].T for b in range(2)], axis=1)
    half_upstream = upstream * BF16(0.5)
    chunks = [slice(c, c + width) for c in range(0, hidden, width)]

    def active_grad(at):
        return nn(r.frozen_shrink[at, :], half_upstream).astype(BF16)

    ahead = len(chunks) // 2
    active_grads = [active_grad(at) for at in chunks[:ahead]]
    middle = values + merged
    unit_b, _, inverse_b = standardize(middle, 0)
    second = (unit_b * r.regainT[...]).astype(BF16)
    coming = nn(r.expandT[chunks[0], :], second)
    for k, at in enumerate(chunks):
        current = coming
        if k + 1 < len(chunks):
            coming = nn(r.expandT[chunks[k + 1], :], second)
        if ahead + k < len(chunks):
            active_grads.append(active_grad(chunks[ahead + k]))
        active, slope = gelu_pair_low(current)
        r.active[at, :] = active.astype(BF16)
        r.slope[at, :] = active_grads[k] * slope.astype(BF16)
    ready(2)
    second_grad = nn(r.frozen_expand[...], r.slope[...])
    shrunk = nn(r.shrinkT[...], r.active[...])
    middle_grad = upstream.astype(F32) + norm_back(
        second_grad * r.regainT[...], unit_b, inverse_b, 0
    )
    result = middle + shrunk
    for b in range(2):
        r.tok[2 * slot + b] = result[:, span[b]].astype(BF16).T
    context_grad = nn(r.frozen_merge[...], middle_grad.astype(BF16))
    low_grad, packed_grad = r.low_grad, r.packed_grad
    totals, from_class = [[], []], []
    for b in range(2):
        for h in range(heads):
            at = slice(HD * h, HD * (h + 1))
            low = context_grad[at, span[b]] * r.shares[b][h : h + 1, :]
            totals[b].append(
                jnp.sum(low * ctx[at, span[b]].astype(F32), axis=0, keepdims=True)
            )
            low_grad[at, span[b]] = low.astype(BF16)
        all_low = low_grad[:, span[b]]
        weights = r.class_weights[b]
        class_grad = weights * (
            nn(value_rows[b], all_low) - jnp.concatenate(totals[b] + blank, axis=0)
        )
        class_grad = class_grad.astype(BF16)
        from_class.append(tn(key_rows[b], class_grad))
        dk = nt(class_grad, qkv[0:width, span[b]]) * LN2
        dv = nt(weights.astype(BF16), all_low)
        r.class_dk[2 * it + b] = jnp.where(block_head, dk, 0.0)
        r.class_dv[2 * it + b] = jnp.where(block_head, dv, 0.0)

    def low_part(turn):
        b, h = order[turn]
        return low_grad[HD * h : HD * (h + 1), span[b]]

    def put(which, turn, grad):
        b, h = order[turn]
        rows_at = slice(which * width + HD * h, which * width + HD * (h + 1))
        packed_grad[rows_at, span[b]] = grad.astype(BF16)

    def key_and_query(turn, score_grad):
        b, h = order[turn]
        put(1, turn, nt(part(0, turn), score_grad) * LN2)
        query_grad = nn(part(1, turn), score_grad) + from_class[b][HD * h : HD * (h + 1)]
        put(0, turn, query_grad * HD ** (-0.5))

    grads, score_grads = {0: tn(part(2, 0), low_part(0))}, {}
    for turn, (b, h) in enumerate(order):
        if turn + 1 < len(order):
            grads[turn + 1] = tn(part(2, turn + 1), low_part(turn + 1))
        weights = probs[b * heads + h]
        put(2, turn, nt(low_part(turn), weights))
        score_grads[turn] = weights * (grads.pop(turn) - totals[b][h]).astype(BF16)
        if turn:
            key_and_query(turn - 1, score_grads.pop(turn - 1))
    key_and_query(len(order) - 1, score_grads.pop(len(order) - 1))
    first_grad = nn(r.frozen_triple[...], packed_grad[...])
    if following is not None:
        project(r, dims, following)
    centre, inverse = r.stat[it, 0:1, :], r.stat[it, 1:2, :]
    unit = (values - centre) * inverse
    back = norm_back(first_grad * r.gainT[...], unit, inverse, 0)
    r.input_grad[it] = (middle_grad + back).astype(BF16)


def patch_kernel(dims, *refs):
    r = SimpleNamespace(**dict(zip(dims.names, refs, strict=True)))
    n_img, width, hidden, inside = dims.n_img, dims.width, dims.hidden, dims.inside
    heads = width // HD
    rows, patches = dims.images, dims.patches
    pairs, lanes = rows // 2, 2 * patches
    shard = width // n_img
    shard_ff = hidden // n_img

    if inside:
        seg = lax.axis_index(SEG)
        me = lax.axis_index(IMG)
        barrier = pltpu.get_barrier_semaphore()

        def sibling(src, dst, link):
            return pltpu.make_async_remote_copy(
                src_ref=src,
                dst_ref=dst,
                send_sem=link.at[0],
                recv_sem=link.at[1],
                device_id={SEG: 1 - seg},
                device_id_type=MESH,
            )

        def to_peers(source, target, link):
            def send(step, carry):
                pltpu.make_async_remote_copy(
                    src_ref=source,
                    dst_ref=target,
                    send_sem=link.at[0],
                    recv_sem=link.at[1],
                    device_id={IMG: lax.rem(me + step, n_img)},
                    device_id_type=MESH,
                ).start()
                return carry

            lax.fori_loop(1, n_img, send, 0)
            pltpu.make_async_copy(source, target, link.at[1]).start()

        def to_other_segment(source, target, link):
            def send(step, carry):
                pltpu.make_async_remote_copy(
                    src_ref=source,
                    dst_ref=target,
                    send_sem=link.at[0],
                    recv_sem=link.at[1],
                    device_id={SEG: 1 - seg, IMG: lax.rem(me + step, n_img)},
                    device_id_type=MESH,
                ).start()
                return carry

            lax.fori_loop(0, n_img, send, 0)

        def wait_all(whole, sem):
            pltpu.make_async_copy(whole, whole, sem).wait()

        def greet(step, carry):
            peer = lax.rem(me + step, n_img)
            for other in range(2):
                pl.semaphore_signal(
                    barrier,
                    inc=1,
                    device_id={SEG: lax.rem(seg + other, 2), IMG: peer},
                    device_id_type=MESH,
                )
            return carry

        lax.fori_loop(1, n_img, greet, 0)
        pl.semaphore_signal(barrier, inc=1, device_id={SEG: 1 - seg}, device_id_type=MESH)

    for it in range(pairs):
        pair_copy(r.tokens, r.tok, r.tok_sem, it).start()
    for it in range(dims.early):
        pair_copy(r.cotangent, r.cot, r.cot_sem, it).start()

    gain_row = r.frozen_gain[...].astype(F32).reshape(1, width)
    regain_row = r.frozen_regain[...].astype(F32).reshape(1, width)
    r.tripleT[...] = r.frozen_triple[...].T
    r.mergeT[...] = r.frozen_merge[...].T
    r.expandT[...] = r.frozen_expand[...].T * BF16(0.5)
    r.shrinkT[...] = r.frozen_shrink[...].T
    turns = (
        (r.tripleT, r.triple_turned),
        (r.mergeT, r.merge_turned),
        (r.expandT, r.expand_turned),
        (r.shrinkT, r.shrink_turned),
    )
    for k, (turned, target) in enumerate(turns):
        pltpu.make_async_copy(turned, target, r.turn_sem.at[k]).start()
    r.gainT[...] = column(gain_row, lanes)
    r.regainT[...] = column(regain_row, lanes)

    if inside:
        upstream = r.region_cotangent[...].astype(F32)
        fill = [upstream[8 * k : 8 * k + 8] for k in range(rows // 8)]
        r.shard_gains[...] = jnp.zeros_like(r.shard_gains)
        r.shard_gains[0:1, 0:shard] = r.gain_first[...].astype(F32).reshape(1, shard)
        r.shard_gains[1:2, 0:shard] = r.gain_second[...].astype(F32).reshape(1, shard)
        for k in range(2):
            tall = column(r.shard_gains[k : k + 1, :], 128)
            fill += [tall[at : at + 8] for at in range(0, shard, 8)]
        fill = jnp.concatenate(fill, axis=1)
        triple = r.weight_triple[...].astype(F32)
        merge = r.weight_merge[...].astype(F32)
        expand = r.weight_expand[...].astype(F32)
        first_half = jnp.concatenate([triple, merge], axis=1)
        r.w_own[0] = jnp.concatenate([first_half, fill], axis=0).astype(BF16)
        r.w_own[1] = jnp.concatenate([expand, fill], axis=0).astype(BF16)
        for k in range(2):
            r.s_own[k] = r.weight_shrink[k * shard_ff // 2 : (k + 1) * shard_ff // 2, :]

    class_in = r.class_tokens[...].astype(F32)
    class_unit, _, _ = standardize(class_in, 1)
    class_first = (class_unit * gain_row).astype(BF16)
    class_packed = nn(class_first, r.frozen_triple[...]).astype(BF16).astype(F32)
    r.class_packed[...] = class_packed
    tall_q = spread(class_packed[:, 0:width])
    tall_k = spread(class_packed[:, width : 2 * width])
    tall_v = spread(class_packed[:, 2 * width :])
    r.class_k[...] = tall_k.reshape(rows, HEADS8, width)
    r.class_v[...] = tall_v.reshape(rows, HEADS8, width)
    query_map = nt(tall_q.astype(BF16), r.frozen_triple[:, width : 2 * width])
    query_map = query_map * (LOG2E * HD ** (-0.5))
    r.query_map[...] = query_map.reshape(rows, HEADS8, width)
    self_score = jnp.sum(tall_q * tall_k, axis=1, keepdims=True) * (LOG2E * HD ** (-0.5))
    r.self_score[...] = jnp.broadcast_to(self_score, (rows * HEADS8, 128)).reshape(
        rows, HEADS8, 128
    )
    r.class_first[...] = jnp.broadcast_to(
        class_first.astype(F32)[:, None, :], (rows, HEADS8, width)
    )

    def class_norm(it):
        pair_copy(r.tokens, r.tok, r.tok_sem, it).wait()
        values = jnp.concatenate([r.tok[2 * it + b].T for b in range(2)], axis=1).astype(F32)
        unit, centre, inverse = standardize(values, 0)
        first = (unit * r.gainT[...]).astype(BF16)
        r.firstT[it] = first
        r.stat[it, 0:1, :] = centre
        r.stat[it, 1:2, :] = inverse
        return first

    def class_forward(step, carry):
        turns = [2 * step, 2 * step + 1]
        firsts = [class_norm(it) for it in turns]
        scores = []
        for it, first in zip(turns, firsts):
            maps = jnp.concatenate([r.query_map[2 * it + b] for b in range(2)], axis=0)
            scores.append(nn(maps.astype(BF16), first))
        spread_out = []
        for it, first, score in zip(turns, firsts, scores):
            for b in range(2):
                part = score[b * HEADS8 : (b + 1) * HEADS8, b * patches : (b + 1) * patches]
                r.class_scores[2 * it + b] = part
                alone = r.self_score[2 * it + b][:, 0:1]
                top = jnp.maximum(jnp.max(part, axis=1, keepdims=True), alone)
                weights = jnp.exp2(part - top)
                weight_alone = jnp.exp2(alone - top)
                share = 1.0 / (jnp.sum(weights, axis=1, keepdims=True) + weight_alone)
                weights = weights * share
                weight_alone = weight_alone * share
                r.class_probs[2 * it + b] = weights
                r.self_prob[2 * it + b] = jnp.broadcast_to(weight_alone, (HEADS8, 128))
                span = first[:, b * patches : (b + 1) * patches]
                spread_out.append((2 * it + b, weights, weight_alone, span))
        for image, weights, weight_alone, span in spread_out:
            mixed = nt(weights.astype(BF16), span)
            r.mixed[image] = mixed + weight_alone * r.class_first[image]
        return carry

    lax.fori_loop(0, pairs // 2, class_forward, 0)
    if inside:
        pl.semaphore_wait(barrier, 2 * n_img - 1)
        to_peers(r.w_own.at[seg], r.w_all.at[seg, me], r.l_weights)
        to_peers(r.s_own.at[seg], r.s_all.at[seg, me], r.l_shrink)

    mixed = r.mixed[...].reshape(rows * HEADS8, width).astype(BF16)
    class_context = gather_heads(nn(mixed, r.frozen_triple[:, 2 * width :])).astype(BF16)
    class_middle = class_in + nn(class_context, r.frozen_merge[...])
    class_unit_b, _, _ = standardize(class_middle, 1)
    class_second = (class_unit_b * regain_row).astype(BF16)
    class_active, class_slope = gelu_pair(nn(class_second, r.frozen_expand[...]))
    class_out = class_middle + nn(class_active.astype(BF16), r.frozen_shrink[...])
    r.class_context[...] = class_context.astype(F32)
    r.class_middle[...] = class_middle
    r.class_slope[...] = class_slope
    r.class_out[...] = class_out.astype(BF16)
    if inside:
        to_other_segment(r.class_out, r.crossed.at[me], r.l_crossed)

    def region():
        keys = n_img * rows
        wait_all(r.crossed, r.l_crossed.at[1])
        sibling(r.w_all.at[seg], r.w_all.at[seg], r.l_forward).wait()
        sibling(r.s_all.at[seg], r.s_all.at[seg], r.l_forward_shrink).wait()
        half = shard_ff // 2
        for j in range(n_img):
            for k in range(2):
                down = shard_ff * j + half * k
                r.region_shrink[down : down + half, :] = r.s_all[k, j]
        deep = PAD * n_img
        w_triple = r.w_all[0, :, :, 0 : 3 * width].reshape(deep, 3 * width)
        w_merge = r.w_all[0, :, :, 3 * width :].reshape(deep, width)
        w_expand = r.w_all[1].reshape(deep, hidden)
        ups, wide = [], [[], []]
        for j in range(n_img):
            fill = r.w_all[seg, j].astype(F32)[shard:PAD]
            ups += [fill[:, width * k : width * (k + 1)] for k in range(rows // 8)]
            for k in range(2):
                first_at = width * (rows // 8) + 128 * (shard // 8) * k
                for at in range(first_at, first_at + 128 * (shard // 8), 128):
                    wide[k].append(fill[:, at : at + 128])
        wide = [jnp.concatenate(w, axis=0) for w in wide]
        gain, regain = (jnp.concatenate([g] * (keys // 128), axis=1) for g in wide)
        upstream = jnp.concatenate(ups, axis=0).T.astype(BF16)

        slots = r.region_number.shape[1]
        per = slots // n_img
        micros = rows // per
        numbers = r.region_number[...].astype(F32)
        numbers = jnp.concatenate([numbers, jnp.zeros((8 - micros, slots), F32)], axis=0)
        at = lax.broadcasted_iota(jnp.int32, (slots, keys), 1)
        slot = lax.broadcasted_iota(jnp.int32, (slots, keys), 0)
        chosen = slot == per * (at // rows) + lax.rem(at, per)
        numbers = nn(numbers.astype(BF16), jnp.where(chosen, 1.0, 0.0).astype(BF16))
        at = lax.rem(lax.broadcasted_iota(jnp.int32, (1, keys), 1), rows) // per
        code = jnp.zeros((1, keys), F32)
        for m in range(micros):
            code = jnp.where(at == m, numbers[m : m + 1, :] * micros + m, code)
        code_down = jnp.broadcast_to(code, (128, keys)).T
        code_down = jnp.concatenate([code_down] * (keys // 128), axis=1)
        bias = jnp.where(code_down == code, 0.0, NEG)

        qkv, probs, ctx = r.qkv, r.probs, r.ctx
        values = r.crossed[...].reshape(keys, width).T.astype(F32)
        unit, _, inverse = standardize(values, 0)
        r.region_first[...] = padded(unit * gain, shard, n_img).astype(BF16)
        packed = tn(w_triple, r.region_first[...])
        qkv[0:width, 0:keys] = (packed[0:width] * (LOG2E * HD ** (-0.5))).astype(BF16)
        qkv[width:, 0:keys] = packed[width:].astype(BF16)

        def part(which, h):
            return qkv[which * width + HD * h : which * width + HD * (h + 1), 0:keys]

        mixes, scores = [], [tn(part(1, 0), part(0, 0))]
        for h in range(heads):
            if h + 1 < heads:
                scores.append(tn(part(1, h + 1), part(0, h + 1)))
            biased = scores[h] + bias
            weights = jnp.exp2(biased - jnp.max(biased, axis=0, keepdims=True))
            r.shares[0, h : h + 1, :] = 1.0 / jnp.sum(weights, axis=0, keepdims=True)
            probs[h] = weights.astype(BF16)
            if h:
                mixes.append(nn(part(2, h - 1), probs[h - 1]) * r.shares[0, h - 1 : h, :])
        mixes.append(nn(part(2, heads - 1), probs[heads - 1]) * r.shares[0, heads - 1 : heads, :])
        context = jnp.concatenate(mixes, axis=0)
        r.region_context[...] = padded(context, shard, n_img).astype(BF16)
        middle = values + tn(w_merge, r.region_context[...])
        unit_b, _, inverse_b = standardize(middle, 0)
        r.region_second[...] = padded(unit_b * regain, shard, n_img).astype(BF16)
        for c in range(0, hidden, width):
            at = slice(c, c + width)
            active, slope = gelu_pair(tn(w_expand[:, at], r.region_second[...]))
            r.region_active[at, :] = active.astype(BF16)
            r.slope[at, 0:keys] = slope.astype(BF16)
        result = middle + tn(r.region_shrink[...], r.region_active[...])
        mine = pl.ds(pl.multiple_of(me * rows, rows), rows)
        r.region_rows[...] = result.T
        r.region_out[...] = r.region_rows[mine, :].astype(BF16)

        for c in range(0, hidden, width):
            at = slice(c, c + width)
            active_grad = nn(r.region_shrink[at, :], upstream)
            r.active[at, 0:keys] = (active_grad * r.slope[at, 0:keys].astype(F32)).astype(BF16)
        hidden_low = r.active[:, 0:keys]
        second_grad = trimmed(nn(w_expand, hidden_low), shard, n_img)
        middle_grad = upstream.astype(F32) + norm_back(second_grad * regain, unit_b, inverse_b, 0)
        middle_low = middle_grad.astype(BF16)
        context_grad = trimmed(nn(w_merge, middle_low), shard, n_img)
        packed_grad = r.packed_grad
        lows, totals = [], []
        for h in range(heads):
            at = slice(HD * h, HD * (h + 1))
            low = context_grad[at] * r.shares[0, h : h + 1, :]
            totals.append(jnp.sum(low * context[at], axis=0, keepdims=True))
            lows.append(low.astype(BF16))

        def put(which, h, grad):
            packed_grad[which * width + HD * h : which * width + HD * (h + 1), 0:keys] = (
                grad.astype(BF16)
            )

        def key_and_query(h, score_grad):
            put(1, h, nt(part(0, h), score_grad) * LN2)
            put(0, h, nn(part(1, h), score_grad) * HD ** (-0.5))

        grads, score_grads = [tn(part(2, 0), lows[0])], []
        for h in range(heads):
            if h + 1 < heads:
                grads.append(tn(part(2, h + 1), lows[h + 1]))
            put(2, h, nt(lows[h], probs[h]))
            score_grad = probs[h].astype(F32) * (grads[h] - totals[h])
            score_grads.append(score_grad.astype(BF16))
            if h:
                key_and_query(h - 1, score_grads[h - 1])
        key_and_query(heads - 1, score_grads[heads - 1])
        first_grad = trimmed(nn(w_triple, packed_grad[:, 0:keys]), shard, n_img)
        back = norm_back(first_grad * gain, unit, inverse, 0)
        r.region_rows[...] = (middle_grad + back).T
        r.crossed_grad[...] = r.region_rows[mine, :].astype(BF16)
        sibling(r.crossed_grad, r.returned, r.l_returned).start()

        mine = pl.ds(pl.multiple_of(me * PAD, PAD), PAD)
        grads = r.grads
        grads[:, 0 : 3 * width] = nt(r.region_first[mine, :], packed_grad[:, 0:keys])[0:shard]
        grads[:, 3 * width : 4 * width] = nt(r.region_context[mine, :], middle_low)[0:shard]
        grads[:, 4 * width : 4 * width + hidden] = nt(r.region_second[mine, :], hidden_low)[0:shard]
        mine = pl.ds(pl.multiple_of(me * shard_ff, shard_ff), shard_ff)
        r.grads_shrink[...] = nt(r.region_active[mine, :], upstream)
        mine = pl.ds(pl.multiple_of(me * shard, shard), shard)
        for k, (grad, standard) in enumerate(((first_grad, unit), (second_grad, unit_b))):
            total = jnp.sum(grad * standard, axis=1, keepdims=True)
            r.gain_columns[...] = jnp.broadcast_to(total, (width, 128))
            at = 4 * width + hidden + 128 * k
            grads[:, at : at + 128] = r.gain_columns[mine, :]
        sibling(grads, r.grads_in, r.l_grads).start()
        sibling(r.grads_shrink, r.grads_shrink_in, r.l_grads_shrink).start()

    def one_pair(it, carry):
        pair_copy(r.cotangent, r.cot, r.cot_sem, it).wait()
        patch_pair(r, dims, it, it, jnp.minimum(it + 1, pairs - 1))
        pair_copy(r.tok, r.patch_rows, r.out_sem, it).start()
        one_copy(r.input_grad, r.grad_rows, r.grad_sem, it).start()

        if inside:

            @pl.when(it == AT_FORWARD)
            def _():
                wait_all(r.w_all.at[seg], r.l_weights.at[1])
                wait_all(r.s_all.at[seg], r.l_shrink.at[1])
                sibling(r.w_all.at[seg], r.w_all.at[seg], r.l_forward).start()
                sibling(r.s_all.at[seg], r.s_all.at[seg], r.l_forward_shrink).start()

            pl.when(it == AT_REGION)(region)
        return carry

    for it in range(pairs):
        one_copy(r.firstT, r.first_rows, r.first_sem, it).start()
    project(r, dims, 0)
    lax.fori_loop(0, dims.early, one_pair, 0)

    if inside:
        sibling(r.crossed_grad, r.returned, r.l_returned).wait()
        sibling(r.grads, r.grads_in, r.l_grads).wait()
        sibling(r.grads_shrink, r.grads_shrink_in, r.l_grads_shrink).wait()
        r.class_up[...] = r.returned[...]
        r.grads_out[...] = r.grads[...] + r.grads_in[...]
        r.shrink_out[...] = r.grads_shrink[...] + r.grads_shrink_in[...]
        peers = pl.ds(0, n_img - 1)
        wait_all(r.w_all.at[0, peers], r.l_weights.at[0])
        wait_all(r.s_all.at[0, peers], r.l_shrink.at[0])
        wait_all(r.crossed, r.l_crossed.at[0])
    for it in range(pairs):
        one_copy(r.firstT, r.first_rows, r.first_sem, it).wait()
    for it in range(dims.early):
        pair_copy(r.tok, r.patch_rows, r.out_sem, it).wait()
        one_copy(r.input_grad, r.grad_rows, r.grad_sem, it).wait()
    for k, (turned, target) in enumerate(turns):
        pltpu.make_async_copy(turned, target, r.turn_sem.at[k]).wait()


def finish_kernel(dims, *refs):
    r = SimpleNamespace(**dict(zip(dims.names, refs, strict=True)))
    width, hidden = dims.width, dims.hidden
    rows, patches, early = dims.images, dims.patches, dims.early
    pairs, lanes = rows // 2, 2 * patches
    late = pairs - early

    loads = []
    for k, name in enumerate(dims.staged):
        load = pltpu.make_async_copy(getattr(r, name), getattr(r, name + BESIDE), r.load_sem.at[k])
        setattr(r, name, getattr(r, name + BESIDE))
        loads.append(load)
    last = pl.ds(2 * early, 2 * late)
    tok_in = pltpu.make_async_copy(r.tokens.at[last], r.tok, r.late_sem.at[0])
    cot_in = pltpu.make_async_copy(r.cotangent.at[last], r.cot, r.late_sem.at[1])
    ready = pl.ds(0, 2 * early)
    rows_in = pltpu.make_async_copy(r.patch_rows.at[ready], r.ready, r.late_sem.at[2])
    rows_out = pltpu.make_async_copy(r.ready, r.patch_output.at[ready], r.late_sem.at[4])
    firsts = [one_copy(r.first_rows, r.firstT, r.first_sem, it) for it in range(pairs)]
    earlier = [one_copy(r.grad_rows, r.input_grad, r.grad_sem, it) for it in range(early)]
    bounds = (0,) + dims.bounds
    stages = [loads[a:b] for a, b in zip(bounds, bounds[1:])]
    stages[0] = firsts[early:] + [tok_in] + stages[0]
    stages[1] = [cot_in] + stages[1]
    stages[3] = stages[3] + [rows_in] + firsts[:early] + earlier

    def ask(*wanted):
        for stage in wanted:
            for load in stages[stage]:
                load.start()

    def ready(stage):
        for load in stages[stage]:
            load.wait()
        if stage == 0:
            ask(1, 2)
        if stage == 1:
            ask(3)

    ask(0)
    ready(0)
    gain_row = r.frozen_gain[...].astype(F32).reshape(1, width)
    regain_row = r.frozen_regain[...].astype(F32).reshape(1, width)
    r.gainT[...] = column(gain_row, lanes)
    r.regainT[...] = column(regain_row, lanes)
    packed = r.class_packed[...]
    tall_k = spread(packed[:, width : 2 * width])
    tall_v = spread(packed[:, 2 * width :])
    r.class_k[...] = tall_k.reshape(rows, HEADS8, width)
    r.class_v[...] = tall_v.reshape(rows, HEADS8, width)
    project(r, dims, early)
    for it in range(early, pairs):
        following = it + 1 if it + 1 < pairs else None
        wait = ready if it == early else lambda stage: None
        patch_pair(r, dims, it, it - early, following, wait)
    ready(3)
    rows_out.start()
    out = pltpu.make_async_copy(r.tok, r.patch_output.at[last], r.late_sem.at[3])
    out.start()

    upstream = r.class_up[...]
    middle = r.class_middle[...]
    unit, _, inverse = standardize(middle, 1)
    hidden_low = (nt(upstream, r.frozen_shrink[...]) * r.class_slope[...]).astype(BF16)
    second_grad = nt(hidden_low, r.frozen_expand[...])
    middle_grad = upstream.astype(F32) + norm_back(second_grad * regain_row, unit, inverse, 1)
    low = nt(middle_grad.astype(BF16), r.frozen_merge[...]).astype(BF16).astype(F32)
    tall_low = spread(low)
    low_map = nt(tall_low.astype(BF16), r.frozen_triple[:, 2 * width :])
    r.low_map[...] = low_map.reshape(rows, HEADS8, width)
    total = jnp.sum(spread(low * r.class_context[...]), axis=1, keepdims=True)
    r.class_total[...] = jnp.broadcast_to(total, (rows * HEADS8, 128)).reshape(rows, HEADS8, 128)
    r.ungainT[...] = 1.0 / r.gainT[:, 0:patches]

    def correct(step, carry):
        turns = [2 * step, 2 * step + 1]
        grads = []
        for it in turns:
            maps = jnp.concatenate([r.low_map[2 * it + b] for b in range(2)], axis=0)
            grads.append(nn(maps.astype(BF16), r.firstT[it]))
        small = []
        for it, grad in zip(turns, grads):
            for b in range(2):
                image = 2 * it + b
                span = slice(b * patches, (b + 1) * patches)
                part = grad[b * HEADS8 : (b + 1) * HEADS8, span]
                weights = r.class_probs[image]
                score_grad = weights * (part - r.class_total[image][:, 0:1])
                toward = jnp.concatenate([r.query_map[image], r.low_map[image]], axis=0) * gain_row
                left = (toward - mean(toward, 1)).astype(BF16)
                right = jnp.concatenate([score_grad * LN2, weights], axis=0)
                right = right * r.stat[it, 1:2, span]
                scores = jnp.concatenate([r.class_scores[image], part], axis=0)
                along = jnp.sum(right * scores, axis=0, keepdims=True) * (1.0 / width)
                small.append((it, image, span, score_grad, left, right.astype(BF16), along))
        products = [tn(left, right) for _, _, _, _, left, right, _ in small]
        for product, (it, image, span, score_grad, _, _, along) in zip(products, small):
            first = r.firstT[it, :, span]
            r.mixed[image] = nt(score_grad.astype(BF16), first)
            back = product - first.astype(F32) * (r.ungainT[...] * along)
            result = r.input_grad[it, :, span].astype(F32) + back
            r.result[image] = result.astype(BF16).T
        for it in turns:
            pair_copy(r.result, r.patch_gradient, r.back_sem, it).start()
        return carry

    lax.fori_loop(0, pairs // 2, correct, 0)

    self_prob = r.self_prob[...].reshape(rows * HEADS8, 128)[:, 0:1]
    tall_q = spread(packed[:, 0:width])
    self_grad = self_prob * (jnp.sum(tall_low * tall_v, axis=1, keepdims=True) - total)
    unit, _, inverse = standardize(r.class_tokens[...].astype(F32), 1)
    first = (unit * gain_row).astype(BF16).astype(F32)
    tall_first = jnp.broadcast_to(first[:, None, :], (rows, HEADS8, width))
    mixed = r.mixed[...].reshape(rows * HEADS8, width)
    mixed = mixed + self_grad * tall_first.reshape(rows * HEADS8, width)
    triple = r.frozen_triple
    query_grad = gather_heads(nn(mixed.astype(BF16), triple[:, width : 2 * width]))
    key_grad = r.class_dk[...] + (tall_q * (self_grad * HD ** (-0.5))).reshape(
        rows, HEADS8, width
    )
    value_grad = r.class_dv[...] + (tall_low * self_prob).reshape(rows, HEADS8, width)
    packed_grad = jnp.concatenate(
        [query_grad * HD ** (-0.5), jnp.sum(key_grad, axis=1), jnp.sum(value_grad, axis=1)],
        axis=1,
    ).astype(BF16)
    first_grad = nt(packed_grad, triple[...])
    back = norm_back(first_grad * gain_row, unit, inverse, 1)
    r.class_gradient[...] = (middle_grad + back).astype(BF16)
    if dims.inside:
        wide = width * 4 + hidden
        r.region_output[...] = r.region_out[...]
        r.triple_gradient[...] = r.grads_out[:, 0 : 3 * width]
        r.merge_gradient[...] = r.grads_out[:, 3 * width : 4 * width]
        r.expand_gradient[...] = r.grads_out[:, 4 * width : wide]
        r.shrink_gradient[...] = r.shrink_out[...]
        shard = r.grads_out.shape[0]
        blank = jnp.zeros((128 - shard, 128), F32)
        for k, target in enumerate((r.first_gradient, r.second_gradient)):
            columns = r.grads_out[:, wide + 128 * k : wide + 128 * (k + 1)]
            columns = jnp.concatenate([columns, blank], axis=0).T
            target[...] = columns[0:1, 0:shard]
    rows_out.wait()
    out.wait()
    for it in range(pairs):
        pair_copy(r.result, r.patch_gradient, r.back_sem, it).wait()


def normalize(values, scaling):
    centred = values - jnp.mean(values, axis=-1, keepdims=True)
    inverse = lax.rsqrt(jnp.mean(centred * centred, axis=-1, keepdims=True) + EPSILON)
    standard = centred * inverse
    return (standard * scaling, standard, inverse)


def normalize_back(upstream, standard, inverse, scaling):
    scaled = upstream * scaling
    centred = scaled - jnp.mean(scaled, axis=-1, keepdims=True)
    centred = centred - standard * jnp.mean(scaled * standard, axis=-1, keepdims=True)
    gain_grad = jnp.sum((upstream * standard).reshape(-1, upstream.shape[-1]), axis=0)
    return (centred * inverse, gain_grad)


def gelu_slope(hidden):
    return (
        0.5 * (1.0 + lax.erf(hidden * 0.7071067811865476))
        + hidden * jnp.exp(-0.5 * hidden * hidden) * 0.3989422804014327
    )


def forward_product(operand, weight):
    return lax.dot_general(
        operand, weight, (((operand.ndim - 1,), (0,)), ((), ())), preferred_element_type=F32
    )


def backward_product(upstream, weight):
    return lax.dot_general(
        upstream,
        weight,
        (((upstream.ndim - 1,), (1,)), ((), ())),
        preferred_element_type=F32,
    )


def row_product(operand, cotangent):
    left_rows = operand.reshape(-1, operand.shape[-1])
    right_rows = cotangent.reshape(-1, cotangent.shape[-1])
    return lax.dot_general(
        left_rows, right_rows, (((0,), (0,)), ((), ())), preferred_element_type=F32
    )


def heads_of(packed, portion):
    section_width = packed.shape[-1] // 3
    section = packed[..., portion * section_width : (portion + 1) * section_width]
    return section.reshape(packed.shape[:-1] + (section_width // HD, HD))


def raw_scores(queries, keyset, allowed):
    scores = jnp.einsum(
        "bqhd,bkhd->bhqk", queries, keyset, preferred_element_type=F32
    ) * HD ** (-0.5)
    if allowed is None:
        return scores
    return jnp.where(allowed[:, None], scores, -1e30)


def attend(queries, keyset, valueset, allowed):
    scores = raw_scores(queries, keyset, allowed)
    highest = jnp.max(scores, axis=-1, keepdims=True)
    logsum = highest + jnp.log(jnp.sum(jnp.exp(scores - highest), axis=-1, keepdims=True))
    weighting = jnp.exp(scores - logsum).astype(BF16)
    context = jnp.einsum("bhqk,bkhd->bqhd", weighting, valueset, preferred_element_type=F32)
    return (context.astype(BF16), logsum)


def score_terms(queries, keyset, valueset, allowed, logsum, context_grad):
    scores = raw_scores(queries, keyset, allowed)
    weighting = jnp.exp(scores - logsum)
    weight_grad = jnp.einsum(
        "bqhd,bkhd->bhqk", context_grad, valueset, preferred_element_type=F32
    )
    row_total = jnp.sum(weighting * weight_grad, axis=-1, keepdims=True)
    score_grad = (weighting * (weight_grad - row_total)).astype(BF16)
    return (weighting, score_grad, row_total)


def attend_back(queries, keyset, valueset, allowed, logsum, context_grad):
    weighting, score_grad, row_total = score_terms(
        queries, keyset, valueset, allowed, logsum, context_grad
    )
    value_grad = jnp.einsum(
        "bhqk,bqhd->bkhd",
        weighting.astype(BF16),
        context_grad,
        preferred_element_type=F32,
    )
    query_grad = jnp.einsum(
        "bhqk,bkhd->bqhd", score_grad, keyset, preferred_element_type=F32
    ) * HD ** (-0.5)
    key_grad = jnp.einsum(
        "bhqk,bqhd->bkhd", score_grad, queries, preferred_element_type=F32
    ) * HD ** (-0.5)
    return (query_grad, key_grad, value_grad)


def block_head(inputs, scaling, triple):
    normed, standard, inverse = normalize(inputs, scaling)
    first_low = normed.astype(BF16)
    packed = forward_product(first_low, triple).astype(BF16)
    return (first_low, standard, inverse, packed)


def block_tail(inputs, context, regain, merger, expand, shrink):
    middle = inputs + forward_product(context, merger)
    normed, standard, inverse = normalize(middle, regain)
    second = normed.astype(BF16)
    hidden = forward_product(second, expand)
    active = jax.nn.gelu(hidden, approximate=False).astype(BF16)
    result = middle + forward_product(active, shrink)
    return (result, (standard, inverse, second, hidden, active))


def tail_back(upstream, kept_tail, regain, merger, expand, shrink):
    standard, inverse, second, hidden, active = kept_tail
    out_low = upstream.astype(BF16)
    active_grad = backward_product(out_low, shrink)
    hidden_low = (active_grad * gelu_slope(hidden)).astype(BF16)
    second_grad = backward_product(hidden_low, expand)
    norm_grad, regain_grad = normalize_back(second_grad, standard, inverse, regain)
    middle_grad = upstream + norm_grad
    middle_low = middle_grad.astype(BF16)
    context_low = backward_product(middle_low, merger).astype(BF16)
    return (middle_grad, context_low, regain_grad, (middle_low, hidden_low, out_low))


def region_outside(crossed, region_number, region_cotangent, shards_in):
    crossed = lax.ppermute(crossed, SEG, [(0, 1), (1, 0)])
    images = crossed.shape[1]
    model_width = crossed.shape[2]
    gathered = [lax.all_gather(shard, IMG, axis=0, tiled=True) for shard in shards_in]
    full_gain, triple, merger, full_regain, expand, shrink = gathered
    scaling = full_gain.astype(F32)
    regain = full_regain.astype(F32)
    region_in = crossed.astype(F32)
    first_low, standard, inverse, packed = block_head(region_in, scaling, triple)
    local_keys = packed[..., model_width : 2 * model_width]
    local_values = packed[..., 2 * model_width :]
    all_keys, all_values = (
        lax.all_gather(local_keys, IMG, axis=1, tiled=True),
        lax.all_gather(local_values, IMG, axis=1, tiled=True),
    )
    head_shape = all_keys.shape[:-1] + (model_width // HD, HD)
    keyset = all_keys.reshape(head_shape)
    valueset = all_values.reshape(head_shape)
    queries = heads_of(packed, 0)
    first_slot = lax.axis_index(IMG) * images
    own_number = lax.dynamic_slice_in_dim(region_number, first_slot, images, 1)
    allowed = own_number[:, :, None] == region_number[:, None, :]
    context, logsum = attend(queries, keyset, valueset, allowed)
    context = context.reshape(region_in.shape)
    region_result, kept_tail = block_tail(region_in, context, regain, merger, expand, shrink)
    region_output = region_result.astype(BF16)
    upstream = region_cotangent.astype(F32)
    middle_grad, context_low, second_gain_grad, low_rows = tail_back(
        upstream, kept_tail, regain, merger, expand, shrink
    )
    middle_low, hidden_low, out_low = low_rows
    context_heads = context_low.reshape(queries.shape)
    query_grad, key_grad, value_grad = attend_back(
        queries, keyset, valueset, allowed, logsum, context_heads
    )
    key_sum, value_sum = (
        lax.psum_scatter(key_grad.reshape(all_keys.shape), IMG, scatter_dimension=1, tiled=True),
        lax.psum_scatter(
            value_grad.reshape(all_values.shape), IMG, scatter_dimension=1, tiled=True
        ),
    )
    packed_grad = jnp.concatenate(
        [query_grad.reshape(region_in.shape), key_sum, value_sum], axis=-1
    ).astype(BF16)
    norm_grad, first_gain_grad = normalize_back(
        backward_product(packed_grad, triple), standard, inverse, scaling
    )
    input_grad = (middle_grad + norm_grad).astype(BF16)
    second_low = kept_tail[2]
    active_low = kept_tail[4]
    shards = (
        lax.psum_scatter(first_gain_grad, IMG, scatter_dimension=0, tiled=True),
        lax.psum_scatter(
            row_product(first_low, packed_grad), IMG, scatter_dimension=0, tiled=True
        ),
        lax.psum_scatter(row_product(context, middle_low), IMG, scatter_dimension=0, tiled=True),
        lax.psum_scatter(second_gain_grad, IMG, scatter_dimension=0, tiled=True),
        lax.psum_scatter(
            row_product(second_low, hidden_low), IMG, scatter_dimension=0, tiled=True
        ),
        lax.psum_scatter(row_product(active_low, out_low), IMG, scatter_dimension=0, tiled=True),
    )
    totals = tuple(lax.psum(shard.astype(BF16), SEG).astype(F32) for shard in shards)
    return region_output, lax.ppermute(input_grad, SEG, [(0, 1), (1, 0)]), totals


def local(
    n_img,
    patch_tokens,
    class_tokens,
    region_number,
    frozen_gain,
    frozen_triple,
    frozen_merge,
    frozen_regain,
    frozen_expand,
    frozen_shrink,
    gain_first,
    weight_triple,
    weight_merge,
    gain_second,
    weight_expand,
    weight_shrink,
    patch_cotangent,
    region_cotangent,
):
    micros, per, patches, width = patch_tokens.shape
    hidden = frozen_expand.shape[1]
    images = micros * per
    shard, shard_ff = width // n_img, hidden // n_img
    lanes, pairs, keys, heads = 2 * patches, images // 2, n_img * images, width // HD
    inside = keys == patches and shard == PAD - 8 and images == 16 and width == 384

    class_rows = class_tokens.reshape(images, width)
    inputs = dict(
        tokens=patch_tokens.reshape(images, patches, width),
        cotangent=patch_cotangent.reshape(images, patches, width),
        class_tokens=class_rows,
        frozen_gain=frozen_gain,
        frozen_regain=frozen_regain,
        frozen_triple=frozen_triple,
        frozen_merge=frozen_merge,
        frozen_expand=frozen_expand,
        frozen_shrink=frozen_shrink,
    )
    if inside:
        inputs |= dict(
            gain_first=gain_first,
            gain_second=gain_second,
            region_cotangent=region_cotangent.reshape(images, width),
            region_number=region_number,
            weight_triple=weight_triple,
            weight_merge=weight_merge,
            weight_expand=weight_expand,
            weight_shrink=weight_shrink,
        )
    vmem = pl.BlockSpec(memory_space=pltpu.VMEM)
    hbm = pl.BlockSpec(memory_space=pl.ANY)
    streams = 2
    in_specs = [hbm] * streams + [vmem] * (len(inputs) - streams)

    shape = jax.ShapeDtypeStruct
    columns = 4 * width + hidden + 256
    large = dict(
        patch_rows=shape((images, patches, width), BF16),
        first_rows=shape((pairs, width, lanes), BF16),
        grad_rows=shape((pairs, width, lanes), BF16),
        triple_turned=shape((3 * width, width), BF16),
        merge_turned=shape((width, width), BF16),
        expand_turned=shape((hidden, width), BF16),
        shrink_turned=shape((width, hidden), BF16),
    )
    small = dict(
        stat=shape((pairs, 8, lanes), F32),
        class_packed=shape((images, 3 * width), F32),
        class_context=shape((images, width), F32),
        class_middle=shape((images, width), F32),
        class_slope=shape((images, hidden), F32),
        query_map=shape((images, HEADS8, width), F32),
        class_probs=shape((images, HEADS8, patches), F32),
        class_scores=shape((images, HEADS8, patches), F32),
        self_prob=shape((images, HEADS8, 128), F32),
        class_dk=shape((images, HEADS8, width), F32),
        class_dv=shape((images, HEADS8, width), F32),
    )
    if inside:
        small |= dict(
            class_up=shape((images, width), BF16),
            region_out=shape((images, width), BF16),
            grads_out=shape((shard, columns), F32),
            shrink_out=shape((shard_ff, width), F32),
        )
    else:
        small |= dict(class_out=shape((images, width), BF16))
    outputs = large | small
    out_specs = [hbm] * len(large) + [vmem] * len(small)

    v = pltpu.VMEM
    dma = pltpu.SemaphoreType.DMA
    working = dict(
        gainT=v((width, lanes), F32),
        regainT=v((width, lanes), F32),
        qkv=v((3 * width, lanes), BF16),
        ctx=v((width, lanes), BF16),
        probs=v((2 * heads, patches, patches), BF16),
        shares=v((2, HEADS8, patches), F32),
        class_weights=v((2, HEADS8, patches), F32),
        active=v((hidden, lanes), BF16),
        slope=v((hidden, lanes), BF16),
        packed_grad=v((3 * width, lanes), BF16),
        low_grad=v((width, lanes), BF16),
        class_k=v((images, HEADS8, width), F32),
        class_v=v((images, HEADS8, width), F32),
        mixed=v((images, HEADS8, width), F32),
        firstT=v((pairs, width, lanes), BF16),
        input_grad=v((pairs, width, lanes), BF16),
        first_sem=dma((pairs,)),
        grad_sem=dma((pairs,)),
    )
    turned = dict(
        tripleT=v((3 * width, width), BF16),
        mergeT=v((width, width), BF16),
        expandT=v((hidden, width), BF16),
        shrinkT=v((width, hidden), BF16),
    )
    scratch = working | turned | dict(
        tok=v((images, patches, width), BF16),
        cot=v((images, patches, width), BF16),
        class_first=v((images, HEADS8, width), F32),
        self_score=v((images, HEADS8, 128), F32),
        tok_sem=dma((pairs,)),
        cot_sem=dma((pairs,)),
        out_sem=dma((pairs,)),
        turn_sem=dma((len(turned),)),
    )
    if inside:
        deep = PAD * n_img
        scratch |= dict(
            class_out=v((images, width), BF16),
            crossed=v((n_img, images, width), BF16),
            crossed_grad=v((images, width), BF16),
            returned=v((images, width), BF16),
            shard_gains=v((8, 128), F32),
            w_own=v((2, PAD, 4 * width), BF16),
            w_all=v((2, n_img, PAD, 4 * width), BF16),
            s_own=v((2, shard_ff // 2, width), BF16),
            s_all=v((2, n_img, shard_ff // 2, width), BF16),
            region_shrink=v((hidden, width), BF16),
            region_first=v((deep, keys), BF16),
            region_context=v((deep, keys), BF16),
            region_second=v((deep, keys), BF16),
            region_active=v((hidden, keys), BF16),
            region_rows=v((keys, width), F32),
            gain_columns=v((width, 128), F32),
            grads=v((shard, columns), F32),
            grads_in=v((shard, columns), F32),
            grads_shrink=v((shard_ff, width), F32),
            grads_shrink_in=v((shard_ff, width), F32),
            l_weights=dma((2,)),
            l_shrink=dma((2,)),
            l_forward=dma((2,)),
            l_forward_shrink=dma((2,)),
            l_crossed=dma((2,)),
            l_returned=dma((2,)),
            l_grads=dma((2,)),
            l_grads_shrink=dma((2,)),
        )
    sizes = dict(
        n_img=n_img,
        width=width,
        hidden=hidden,
        images=images,
        patches=patches,
        inside=inside,
        early=pairs - LATE,
    )
    limit = dict(vmem_limit_bytes=60 * 1024 * 1024)
    remote = dict(collective_id=0, has_side_effects=True) if inside else {}
    names = list(inputs) + list(outputs) + list(scratch)
    results = pl.pallas_call(
        functools.partial(patch_kernel, SimpleNamespace(names=names, **sizes)),
        out_shape=list(outputs.values()),
        in_specs=in_specs,
        out_specs=out_specs,
        scratch_shapes=list(scratch.values()),
        compiler_params=pltpu.CompilerParams(**limit, **remote),
    )(*inputs.values())
    done = dict(zip(outputs, results, strict=True))

    if not inside:
        class_out = done.pop(list(small)[-1])
        region_output, class_up, grads = region_outside(
            class_out.reshape(class_tokens.shape),
            region_number,
            region_cotangent,
            (gain_first, weight_triple, weight_merge, gain_second, weight_expand, weight_shrink),
        )
        done |= dict(class_up=class_up.reshape(images, width))

    streamed = [done.pop(name) for name in large]
    done = SimpleNamespace(**done)
    tripleT, mergeT, expandT, shrinkT = streamed[-len(turned) :]
    stages = (
        dict(class_packed=done.class_packed, stat=done.stat, tripleT=tripleT),
        dict(mergeT=mergeT, frozen_shrink=frozen_shrink, expandT=expandT),
        dict(
            shrinkT=shrinkT,
            frozen_expand=frozen_expand,
            frozen_merge=frozen_merge,
            frozen_triple=frozen_triple,
            class_dk=done.class_dk,
            class_dv=done.class_dv,
        ),
        dict(class_tokens=class_rows) | vars(done),
    )
    staged, bounds = {}, ()
    for stage in stages:
        staged |= {name: a for name, a in stage.items() if name not in staged}
        bounds += (len(staged),)
    inputs = dict(
        tokens=patch_tokens.reshape(images, patches, width),
        cotangent=patch_cotangent.reshape(images, patches, width),
        patch_rows=streamed[0],
        first_rows=streamed[1],
        grad_rows=streamed[2],
    )
    inputs |= staged
    inputs |= dict(frozen_gain=frozen_gain, frozen_regain=frozen_regain)
    outputs = dict(
        patch_output=shape((images, patches, width), BF16),
        patch_gradient=shape((images, patches, width), BF16),
        class_gradient=shape((images, width), BF16),
    )
    out_specs = [hbm] * 2 + [vmem]
    if inside:
        ready = dict(
            region_output=shape((images, width), BF16),
            first_gradient=shape((1, shard), F32),
            triple_gradient=shape((shard, 3 * width), F32),
            merge_gradient=shape((shard, width), F32),
            second_gradient=shape((1, shard), F32),
            expand_gradient=shape((shard, hidden), F32),
            shrink_gradient=shape((shard_ff, width), F32),
        )
        outputs |= ready
        out_specs += [vmem] * len(ready)
    scratch = working | dict(
        tok=v((2 * LATE, patches, width), BF16),
        cot=v((2 * LATE, patches, width), BF16),
        result=v((images, patches, width), BF16),
        ungainT=v((width, patches), F32),
        low_map=v((images, HEADS8, width), F32),
        class_total=v((images, HEADS8, 128), F32),
        load_sem=dma((len(staged),)),
        ready=v((images - 2 * LATE, patches, width), BF16),
        late_sem=dma((5,)),
        back_sem=dma((pairs,)),
    )
    scratch |= {name + BESIDE: v(a.shape, a.dtype) for name, a in staged.items()}
    names = list(inputs) + list(outputs) + list(scratch)
    sizes |= dict(names=names, staged=list(staged), bounds=bounds)
    results = pl.pallas_call(
        functools.partial(finish_kernel, SimpleNamespace(**sizes)),
        out_shape=list(outputs.values()),
        in_specs=[hbm] * (len(inputs) - 2) + [vmem] * 2,
        out_specs=out_specs,
        scratch_shapes=list(scratch.values()),
        compiler_params=pltpu.CompilerParams(**limit),
    )(*inputs.values())
    done = SimpleNamespace(**dict(zip(outputs, results, strict=True)))
    if inside:
        region_output = done.region_output.reshape(class_tokens.shape)
        grads = (
            done.first_gradient.reshape(shard),
            done.triple_gradient,
            done.merge_gradient,
            done.second_gradient.reshape(shard),
            done.expand_gradient,
            done.shrink_gradient,
        )
    return (
        done.patch_output.reshape(patch_tokens.shape),
        region_output,
        done.patch_gradient.reshape(patch_tokens.shape),
        done.class_gradient.reshape(class_tokens.shape),
        *grads,
    )


def solution(mesh):
    patch, row = P(SEG, IMG, None, None), P(SEG, IMG, None)
    gain, weight, whole = P(IMG), P(IMG, None), P()
    block = (gain, weight, weight, gain, weight, weight)
    placed = (patch, row, P(SEG, None)) + (whole,) * 6 + block + (patch, row)
    return jax.shard_map(
        functools.partial(local, mesh.shape[IMG]),
        mesh=mesh,
        in_specs=placed,
        out_specs=(patch, row, patch, row) + block,
        check_vma=False,
    )
```

```python
import functools
from types import SimpleNamespace

import jax
import jax.numpy as jnp
from jax import lax
from jax.experimental import pallas as pl
from jax.experimental.pallas import tpu as pltpu
from jax.sharding import PartitionSpec as P

SEG = "segment"
IMG = "img"
HD = 64
HEADS8 = 8
EPSILON = 1e-06
LOG2E = 1.4426950408889634
LN2 = 0.6931471805599453
ROOT_HALF = 0.7071067811865476
DENSITY = 0.3989422804014327
LOG2_DENSITY = -1.3257480647361593
F32 = jnp.float32
BF16 = jnp.bfloat16
MESH = pl.DeviceIdType.MESH
NEG = -1e30
PAD = 32
BESIDE = "_"

AT_FORWARD = 5
AT_REGION = 6
LATE = 1


def nn(a, b):
    return lax.dot_general(a, b, (((1,), (0,)), ((), ())), preferred_element_type=F32)


def nt(a, b):
    return lax.dot_general(a, b, (((1,), (1,)), ((), ())), preferred_element_type=F32)


def tn(a, b):
    return lax.dot_general(a, b, (((0,), (0,)), ((), ())), preferred_element_type=F32)


def mean(values, axis):
    return jnp.sum(values, axis=axis, keepdims=True) * (1.0 / values.shape[axis])


def standardize(values, axis):
    centre = mean(values, axis)
    centred = values - centre
    inverse = lax.rsqrt(mean(centred * centred, axis) + EPSILON)
    return centred * inverse, centre, inverse


def norm_back(scaled, standard, inverse, axis):
    return inverse * (
        scaled - mean(scaled, axis) - standard * mean(scaled * standard, axis)
    )


def gelu_pair(hidden):
    upto = 0.5 + 0.5 * lax.erf(hidden * ROOT_HALF)
    bell = jnp.exp2(hidden * hidden * (-0.5 * LOG2E))
    return hidden * upto, upto + hidden * (bell * DENSITY)


def gelu_pair_low(half):
    twice = (1.0 + lax.erf(half * (2.0 * ROOT_HALF))).astype(BF16)
    bell = jnp.exp2(half * half * (-2.0 * LOG2E) + (LOG2_DENSITY + 2.0)).astype(BF16)
    low = half.astype(BF16)
    return low * twice, twice + low * bell


def own_heads(rows, width):
    shape = (rows * HEADS8, width)
    lane = lax.broadcasted_iota(jnp.int32, shape, 1) // HD
    return lane == lax.rem(lax.broadcasted_iota(jnp.int32, shape, 0), HEADS8)


def spread(values):
    rows, width = values.shape
    tall = jnp.broadcast_to(values[:, None, :], (rows, HEADS8, width))
    return jnp.where(own_heads(rows, width), tall.reshape(rows * HEADS8, width), 0.0)


def gather_heads(values):
    tall, width = values.shape
    kept = jnp.where(own_heads(tall // HEADS8, width), values, 0.0)
    return jnp.sum(kept.reshape(tall // HEADS8, HEADS8, width), axis=1)


def column(row, lanes):
    tall = jnp.broadcast_to(row, (128, row.shape[1])).T
    return jnp.concatenate([tall] * (lanes // 128), axis=1)


def pair_copy(source, target, sems, it):
    part = pl.ds(2 * it, 2)
    return pltpu.make_async_copy(source.at[part], target.at[part], sems.at[it])


def one_copy(source, target, sems, it):
    return pltpu.make_async_copy(source.at[it], target.at[it], sems.at[it])


def padded(values, shard, n):
    blank = jnp.zeros((PAD - shard, values.shape[1]), values.dtype)
    parts = []
    for j in range(n):
        parts += [values[shard * j : shard * (j + 1)], blank]
    return jnp.concatenate(parts, axis=0)


def trimmed(values, shard, n):
    return jnp.concatenate([values[PAD * j : PAD * j + shard] for j in range(n)], axis=0)


def project(r, dims, it):
    width = dims.width
    first = r.firstT[it]
    queries = nn(r.tripleT[0:width, :], first) * (LOG2E * HD ** (-0.5))
    r.qkv[0:width, :] = queries.astype(BF16)
    r.qkv[width:, :] = nn(r.tripleT[width:, :], first).astype(BF16)


def patch_pair(r, dims, it, slot, following, ready=lambda stage: None):
    width, hidden, patches = dims.width, dims.hidden, dims.patches
    heads = width // HD
    block_head = own_heads(1, width)
    span = [slice(b * patches, (b + 1) * patches) for b in range(2)]
    qkv, ctx, probs = r.qkv, r.ctx, r.probs
    values = jnp.concatenate([r.tok[2 * slot + b].T for b in range(2)], axis=1).astype(F32)
    order = [(b, h) for h in range(heads) for b in range(2)]
    key_rows = [r.class_k[2 * it + b].astype(BF16) for b in range(2)]
    value_rows = [r.class_v[2 * it + b].astype(BF16) for b in range(2)]
    class_scores = [nn(key_rows[b], qkv[0:width, span[b]]) for b in range(2)]

    def part(which, turn):
        b, h = order[turn]
        return qkv[which * width + HD * h : which * width + HD * (h + 1), span[b]]

    scores, mixes, class_weights, shares = {0: tn(part(1, 0), part(0, 0))}, [], [], []
    for turn, (b, h) in enumerate(order):
        if turn + 1 < len(order):
            scores[turn + 1] = tn(part(1, turn + 1), part(0, turn + 1))
        class_score = class_scores[b][h : h + 1, :]
        top = jnp.maximum(jnp.max(scores[turn], axis=0, keepdims=True), class_score)
        weights = jnp.exp2(scores.pop(turn) - top)
        class_weight = jnp.exp2(class_score - top)
        shares.append(1.0 / (jnp.sum(weights, axis=0, keepdims=True) + class_weight))
        class_weights.append(class_weight)
        probs[b * heads + h] = weights.astype(BF16)
        if turn:
            last = order[turn - 1]
            mixes.append(nn(part(2, turn - 1), probs[last[0] * heads + last[1]]))
    mixes.append(nn(part(2, len(order) - 1), probs[2 * heads - 1]))
    blank = [jnp.zeros((HEADS8 - heads, patches), F32)]
    for b in range(2):
        weights = jnp.concatenate(class_weights[b::2] + blank, axis=0)
        r.class_weights[b] = weights
        r.shares[b] = jnp.concatenate(shares[b::2] + blank, axis=0)
        from_class = tn(value_rows[b], weights.astype(BF16))
        for h in range(heads):
            at = slice(HD * h, HD * (h + 1))
            mix = mixes[2 * h + b] + from_class[at]
            ctx[at, span[b]] = (mix * shares[2 * h + b]).astype(BF16)
    ready(1)
    merged = nn(r.mergeT[...], ctx[...])
    upstream = jnp.concatenate([r.cot[2 * slot + b].T for b in range(2)], axis=1)
    half_upstream = upstream * BF16(0.5)
    third = hidden // 3
    chunks = [slice(c, c + third) for c in range(0, hidden, third)]

    def active_grad(at):
        return nn(r.frozen_shrink[at, :], half_upstream).astype(BF16)

    ahead = len(chunks) // 2
    active_grads = [active_grad(at) for at in chunks[:ahead]]
    middle = values + merged
    unit_b, _, inverse_b = standardize(middle, 0)
    second = (unit_b * r.regainT[...]).astype(BF16)
    coming = nn(r.expandT[chunks[0], :], second)
    for k, at in enumerate(chunks):
        current = coming
        if k + 1 < len(chunks):
            coming = nn(r.expandT[chunks[k + 1], :], second)
        if ahead + k < len(chunks):
            active_grads.append(active_grad(chunks[ahead + k]))
        active, slope = gelu_pair_low(current)
        r.active[at, :] = active.astype(BF16)
        r.slope[at, :] = active_grads[k] * slope.astype(BF16)
    ready(2)
    second_grad = nn(r.frozen_expand[...], r.slope[...])
    shrunk = nn(r.shrinkT[...], r.active[...])
    middle_grad = upstream.astype(F32) + norm_back(
        second_grad * r.regainT[...], unit_b, inverse_b, 0
    )
    result = middle + shrunk
    for b in range(2):
        r.tok[2 * slot + b] = result[:, span[b]].astype(BF16).T
    context_grad = nn(r.frozen_merge[...], middle_grad.astype(BF16))
    low_grad, packed_grad = r.low_grad, r.packed_grad
    totals, from_class = [[], []], []
    for b in range(2):
        for h in range(heads):
            at = slice(HD * h, HD * (h + 1))
            low = context_grad[at, span[b]] * r.shares[b][h : h + 1, :]
            totals[b].append(
                jnp.sum(low * ctx[at, span[b]].astype(F32), axis=0, keepdims=True)
            )
            low_grad[at, span[b]] = low.astype(BF16)
        all_low = low_grad[:, span[b]]
        weights = r.class_weights[b]
        class_grad = weights * (
            nn(value_rows[b], all_low) - jnp.concatenate(totals[b] + blank, axis=0)
        )
        class_grad = class_grad.astype(BF16)
        from_class.append(tn(key_rows[b], class_grad))
        dk = nt(class_grad, qkv[0:width, span[b]]) * LN2
        dv = nt(weights.astype(BF16), all_low)
        r.class_dk[2 * it + b] = jnp.where(block_head, dk, 0.0)
        r.class_dv[2 * it + b] = jnp.where(block_head, dv, 0.0)

    def low_part(turn):
        b, h = order[turn]
        return low_grad[HD * h : HD * (h + 1), span[b]]

    def put(which, turn, grad):
        b, h = order[turn]
        rows_at = slice(which * width + HD * h, which * width + HD * (h + 1))
        packed_grad[rows_at, span[b]] = grad.astype(BF16)

    def key_and_query(turn, score_grad):
        b, h = order[turn]
        put(1, turn, nt(part(0, turn), score_grad) * LN2)
        query_grad = nn(part(1, turn), score_grad) + from_class[b][HD * h : HD * (h + 1)]
        put(0, turn, query_grad * HD ** (-0.5))

    grads, score_grads = {0: tn(part(2, 0), low_part(0))}, {}
    for turn, (b, h) in enumerate(order):
        if turn + 1 < len(order):
            grads[turn + 1] = tn(part(2, turn + 1), low_part(turn + 1))
        weights = probs[b * heads + h]
        put(2, turn, nt(low_part(turn), weights))
        score_grads[turn] = weights * (grads.pop(turn) - totals[b][h]).astype(BF16)
        if turn:
            key_and_query(turn - 1, score_grads.pop(turn - 1))
    key_and_query(len(order) - 1, score_grads.pop(len(order) - 1))
    first_grad = nn(r.frozen_triple[...], packed_grad[...])
    if following is not None:
        project(r, dims, following)
    centre, inverse = r.stat[it, 0:1, :], r.stat[it, 1:2, :]
    unit = (values - centre) * inverse
    back = norm_back(first_grad * r.gainT[...], unit, inverse, 0)
    r.input_grad[it] = (middle_grad + back).astype(BF16)


def patch_kernel(dims, *refs):
    r = SimpleNamespace(**dict(zip(dims.names, refs, strict=True)))
    n_img, width, hidden, inside = dims.n_img, dims.width, dims.hidden, dims.inside
    heads = width // HD
    rows, patches = dims.images, dims.patches
    pairs, lanes = rows // 2, 2 * patches
    shard = width // n_img
    shard_ff = hidden // n_img

    if inside:
        seg = lax.axis_index(SEG)
        me = lax.axis_index(IMG)
        barrier = pltpu.get_barrier_semaphore()

        def sibling(src, dst, link):
            return pltpu.make_async_remote_copy(
                src_ref=src,
                dst_ref=dst,
                send_sem=link.at[0],
                recv_sem=link.at[1],
                device_id={SEG: 1 - seg},
                device_id_type=MESH,
            )

        def to_peers(source, target, link):
            def send(step, carry):
                pltpu.make_async_remote_copy(
                    src_ref=source,
                    dst_ref=target,
                    send_sem=link.at[0],
                    recv_sem=link.at[1],
                    device_id={IMG: lax.rem(me + step, n_img)},
                    device_id_type=MESH,
                ).start()
                return carry

            lax.fori_loop(1, n_img, send, 0)
            pltpu.make_async_copy(source, target, link.at[1]).start()

        def to_other_segment(source, target, link):
            def send(step, carry):
                pltpu.make_async_remote_copy(
                    src_ref=source,
                    dst_ref=target,
                    send_sem=link.at[0],
                    recv_sem=link.at[1],
                    device_id={SEG: 1 - seg, IMG: lax.rem(me + step, n_img)},
                    device_id_type=MESH,
                ).start()
                return carry

            lax.fori_loop(0, n_img, send, 0)

        def wait_all(whole, sem):
            pltpu.make_async_copy(whole, whole, sem).wait()

        def greet(step, carry):
            peer = lax.rem(me + step, n_img)
            for other in range(2):
                pl.semaphore_signal(
                    barrier,
                    inc=1,
                    device_id={SEG: lax.rem(seg + other, 2), IMG: peer},
                    device_id_type=MESH,
                )
            return carry

        lax.fori_loop(1, n_img, greet, 0)
        pl.semaphore_signal(barrier, inc=1, device_id={SEG: 1 - seg}, device_id_type=MESH)

    for it in range(pairs):
        pair_copy(r.tokens, r.tok, r.tok_sem, it).start()
    for it in range(dims.early):
        pair_copy(r.cotangent, r.cot, r.cot_sem, it).start()

    gain_row = r.frozen_gain[...].astype(F32).reshape(1, width)
    regain_row = r.frozen_regain[...].astype(F32).reshape(1, width)
    r.tripleT[...] = r.frozen_triple[...].T
    r.mergeT[...] = r.frozen_merge[...].T
    r.expandT[...] = r.frozen_expand[...].T * BF16(0.5)
    r.shrinkT[...] = r.frozen_shrink[...].T
    turns = (
        (r.tripleT, r.triple_turned),
        (r.mergeT, r.merge_turned),
        (r.expandT, r.expand_turned),
        (r.shrinkT, r.shrink_turned),
    )
    for k, (turned, target) in enumerate(turns):
        pltpu.make_async_copy(turned, target, r.turn_sem.at[k]).start()
    r.gainT[...] = column(gain_row, lanes)
    r.regainT[...] = column(regain_row, lanes)

    if inside:
        upstream = r.region_cotangent[...].astype(F32)
        fill = [upstream[8 * k : 8 * k + 8] for k in range(rows // 8)]
        r.shard_gains[...] = jnp.zeros_like(r.shard_gains)
        r.shard_gains[0:1, 0:shard] = r.gain_first[...].astype(F32).reshape(1, shard)
        r.shard_gains[1:2, 0:shard] = r.gain_second[...].astype(F32).reshape(1, shard)
        for k in range(2):
            tall = column(r.shard_gains[k : k + 1, :], 128)
            fill += [tall[at : at + 8] for at in range(0, shard, 8)]
        fill = jnp.concatenate(fill, axis=1)
        triple = r.weight_triple[...].astype(F32)
        merge = r.weight_merge[...].astype(F32)
        expand = r.weight_expand[...].astype(F32)
        first_half = jnp.concatenate([triple, merge], axis=1)
        r.w_own[0] = jnp.concatenate([first_half, fill], axis=0).astype(BF16)
        r.w_own[1] = jnp.concatenate([expand, fill], axis=0).astype(BF16)
        for k in range(2):
            r.s_own[k] = r.weight_shrink[k * shard_ff // 2 : (k + 1) * shard_ff // 2, :]

    class_in = r.class_tokens[...].astype(F32)
    class_unit, _, _ = standardize(class_in, 1)
    class_first = (class_unit * gain_row).astype(BF16)
    class_packed = nn(class_first, r.frozen_triple[...]).astype(BF16).astype(F32)
    r.class_packed[...] = class_packed
    tall_q = spread(class_packed[:, 0:width])
    tall_k = spread(class_packed[:, width : 2 * width])
    tall_v = spread(class_packed[:, 2 * width :])
    r.class_k[...] = tall_k.reshape(rows, HEADS8, width)
    r.class_v[...] = tall_v.reshape(rows, HEADS8, width)
    query_map = nt(tall_q.astype(BF16), r.frozen_triple[:, width : 2 * width])
    query_map = query_map * (LOG2E * HD ** (-0.5))
    r.query_map[...] = query_map.reshape(rows, HEADS8, width)
    self_score = jnp.sum(tall_q * tall_k, axis=1, keepdims=True) * (LOG2E * HD ** (-0.5))
    r.self_score[...] = jnp.broadcast_to(self_score, (rows * HEADS8, 128)).reshape(
        rows, HEADS8, 128
    )
    r.class_first[...] = jnp.broadcast_to(
        class_first.astype(F32)[:, None, :], (rows, HEADS8, width)
    )

    def class_norm(it):
        pair_copy(r.tokens, r.tok, r.tok_sem, it).wait()
        values = jnp.concatenate([r.tok[2 * it + b].T for b in range(2)], axis=1).astype(F32)
        unit, centre, inverse = standardize(values, 0)
        first = (unit * r.gainT[...]).astype(BF16)
        r.firstT[it] = first
        r.stat[it, 0:1, :] = centre
        r.stat[it, 1:2, :] = inverse
        return first

    def class_forward(step, carry):
        turns = [2 * step, 2 * step + 1]
        firsts = [class_norm(it) for it in turns]
        scores = []
        for it, first in zip(turns, firsts):
            maps = jnp.concatenate([r.query_map[2 * it + b] for b in range(2)], axis=0)
            scores.append(nn(maps.astype(BF16), first))
        spread_out = []
        for it, first, score in zip(turns, firsts, scores):
            for b in range(2):
                part = score[b * HEADS8 : (b + 1) * HEADS8, b * patches : (b + 1) * patches]
                r.class_scores[2 * it + b] = part
                alone = r.self_score[2 * it + b][:, 0:1]
                top = jnp.maximum(jnp.max(part, axis=1, keepdims=True), alone)
                weights = jnp.exp2(part - top)
                weight_alone = jnp.exp2(alone - top)
                share = 1.0 / (jnp.sum(weights, axis=1, keepdims=True) + weight_alone)
                weights = weights * share
                weight_alone = weight_alone * share
                r.class_probs[2 * it + b] = weights
                r.self_prob[2 * it + b] = jnp.broadcast_to(weight_alone, (HEADS8, 128))
                span = first[:, b * patches : (b + 1) * patches]
                spread_out.append((2 * it + b, weights, weight_alone, span))
        for image, weights, weight_alone, span in spread_out:
            mixed = nt(weights.astype(BF16), span)
            r.mixed[image] = mixed + weight_alone * r.class_first[image]
        return carry

    lax.fori_loop(0, pairs // 2, class_forward, 0)
    if inside:
        pl.semaphore_wait(barrier, 2 * n_img - 1)
        to_peers(r.w_own.at[seg], r.w_all.at[seg, me], r.l_weights)
        to_peers(r.s_own.at[seg], r.s_all.at[seg, me], r.l_shrink)

    mixed = r.mixed[...].reshape(rows * HEADS8, width).astype(BF16)
    class_context = gather_heads(nn(mixed, r.frozen_triple[:, 2 * width :])).astype(BF16)
    class_middle = class_in + nn(class_context, r.frozen_merge[...])
    class_unit_b, _, _ = standardize(class_middle, 1)
    class_second = (class_unit_b * regain_row).astype(BF16)
    class_active, class_slope = gelu_pair(nn(class_second, r.frozen_expand[...]))
    class_out = class_middle + nn(class_active.astype(BF16), r.frozen_shrink[...])
    r.class_context[...] = class_context.astype(F32)
    r.class_middle[...] = class_middle
    r.class_slope[...] = class_slope
    r.class_out[...] = class_out.astype(BF16)
    if inside:
        to_other_segment(r.class_out, r.crossed.at[me], r.l_crossed)

    def region():
        keys = n_img * rows
        wait_all(r.crossed, r.l_crossed.at[1])
        sibling(r.w_all.at[seg], r.w_all.at[seg], r.l_forward).wait()
        sibling(r.s_all.at[seg], r.s_all.at[seg], r.l_forward_shrink).wait()
        half = shard_ff // 2
        for j in range(n_img):
            for k in range(2):
                down = shard_ff * j + half * k
                r.region_shrink[down : down + half, :] = r.s_all[k, j]
        deep = PAD * n_img
        w_triple = r.w_all[0, :, :, 0 : 3 * width].reshape(deep, 3 * width)
        w_merge = r.w_all[0, :, :, 3 * width :].reshape(deep, width)
        w_expand = r.w_all[1].reshape(deep, hidden)
        ups, wide = [], [[], []]
        for j in range(n_img):
            fill = r.w_all[seg, j].astype(F32)[shard:PAD]
            ups += [fill[:, width * k : width * (k + 1)] for k in range(rows // 8)]
            for k in range(2):
                first_at = width * (rows // 8) + 128 * (shard // 8) * k
                for at in range(first_at, first_at + 128 * (shard // 8), 128):
                    wide[k].append(fill[:, at : at + 128])
        wide = [jnp.concatenate(w, axis=0) for w in wide]
        gain, regain = (jnp.concatenate([g] * (keys // 128), axis=1) for g in wide)
        upstream = jnp.concatenate(ups, axis=0).T.astype(BF16)

        slots = r.region_number.shape[1]
        per = slots // n_img
        micros = rows // per
        numbers = r.region_number[...].astype(F32)
        numbers = jnp.concatenate([numbers, jnp.zeros((8 - micros, slots), F32)], axis=0)
        at = lax.broadcasted_iota(jnp.int32, (slots, keys), 1)
        slot = lax.broadcasted_iota(jnp.int32, (slots, keys), 0)
        chosen = slot == per * (at // rows) + lax.rem(at, per)
        numbers = nn(numbers.astype(BF16), jnp.where(chosen, 1.0, 0.0).astype(BF16))
        at = lax.rem(lax.broadcasted_iota(jnp.int32, (1, keys), 1), rows) // per
        code = jnp.zeros((1, keys), F32)
        for m in range(micros):
            code = jnp.where(at == m, numbers[m : m + 1, :] * micros + m, code)
        code_down = jnp.broadcast_to(code, (128, keys)).T
        code_down = jnp.concatenate([code_down] * (keys // 128), axis=1)
        bias = jnp.where(code_down == code, 0.0, NEG)

        qkv, probs, ctx = r.qkv, r.probs, r.ctx
        values = r.crossed[...].reshape(keys, width).T.astype(F32)
        unit, _, inverse = standardize(values, 0)
        r.region_first[...] = padded(unit * gain, shard, n_img).astype(BF16)
        packed = tn(w_triple, r.region_first[...])
        qkv[0:width, 0:keys] = (packed[0:width] * (LOG2E * HD ** (-0.5))).astype(BF16)
        qkv[width:, 0:keys] = packed[width:].astype(BF16)

        def part(which, h):
            return qkv[which * width + HD * h : which * width + HD * (h + 1), 0:keys]

        mixes, scores = [], [tn(part(1, 0), part(0, 0))]
        for h in range(heads):
            if h + 1 < heads:
                scores.append(tn(part(1, h + 1), part(0, h + 1)))
            biased = scores[h] + bias
            weights = jnp.exp2(biased - jnp.max(biased, axis=0, keepdims=True))
            r.shares[0, h : h + 1, :] = 1.0 / jnp.sum(weights, axis=0, keepdims=True)
            probs[h] = weights.astype(BF16)
            if h:
                mixes.append(nn(part(2, h - 1), probs[h - 1]) * r.shares[0, h - 1 : h, :])
        mixes.append(nn(part(2, heads - 1), probs[heads - 1]) * r.shares[0, heads - 1 : heads, :])
        context = jnp.concatenate(mixes, axis=0)
        r.region_context[...] = padded(context, shard, n_img).astype(BF16)
        middle = values + tn(w_merge, r.region_context[...])
        unit_b, _, inverse_b = standardize(middle, 0)
        r.region_second[...] = padded(unit_b * regain, shard, n_img).astype(BF16)
        for c in range(0, hidden, width):
            at = slice(c, c + width)
            active, slope = gelu_pair(tn(w_expand[:, at], r.region_second[...]))
            r.region_active[at, :] = active.astype(BF16)
            r.slope[at, 0:keys] = slope.astype(BF16)
        result = middle + tn(r.region_shrink[...], r.region_active[...])
        mine = pl.ds(pl.multiple_of(me * rows, rows), rows)
        r.region_rows[...] = result.T
        r.region_out[...] = r.region_rows[mine, :].astype(BF16)

        for c in range(0, hidden, width):
            at = slice(c, c + width)
            active_grad = nn(r.region_shrink[at, :], upstream)
            r.active[at, 0:keys] = (active_grad * r.slope[at, 0:keys].astype(F32)).astype(BF16)
        hidden_low = r.active[:, 0:keys]
        second_grad = trimmed(nn(w_expand, hidden_low), shard, n_img)
        middle_grad = upstream.astype(F32) + norm_back(second_grad * regain, unit_b, inverse_b, 0)
        middle_low = middle_grad.astype(BF16)
        context_grad = trimmed(nn(w_merge, middle_low), shard, n_img)
        packed_grad = r.packed_grad
        lows, totals = [], []
        for h in range(heads):
            at = slice(HD * h, HD * (h + 1))
            low = context_grad[at] * r.shares[0, h : h + 1, :]
            totals.append(jnp.sum(low * context[at], axis=0, keepdims=True))
            lows.append(low.astype(BF16))

        def put(which, h, grad):
            packed_grad[which * width + HD * h : which * width + HD * (h + 1), 0:keys] = (
                grad.astype(BF16)
            )

        def key_and_query(h, score_grad):
            put(1, h, nt(part(0, h), score_grad) * LN2)
            put(0, h, nn(part(1, h), score_grad) * HD ** (-0.5))

        grads, score_grads = [tn(part(2, 0), lows[0])], []
        for h in range(heads):
            if h + 1 < heads:
                grads.append(tn(part(2, h + 1), lows[h + 1]))
            put(2, h, nt(lows[h], probs[h]))
            score_grad = probs[h].astype(F32) * (grads[h] - totals[h])
            score_grads.append(score_grad.astype(BF16))
            if h:
                key_and_query(h - 1, score_grads[h - 1])
        key_and_query(heads - 1, score_grads[heads - 1])
        first_grad = trimmed(nn(w_triple, packed_grad[:, 0:keys]), shard, n_img)
        back = norm_back(first_grad * gain, unit, inverse, 0)
        r.region_rows[...] = (middle_grad + back).T
        r.crossed_grad[...] = r.region_rows[mine, :].astype(BF16)
        sibling(r.crossed_grad, r.returned, r.l_returned).start()

        mine = pl.ds(pl.multiple_of(me * PAD, PAD), PAD)
        grads = r.grads
        grads[:, 0 : 3 * width] = nt(r.region_first[mine, :], packed_grad[:, 0:keys])[0:shard]
        grads[:, 3 * width : 4 * width] = nt(r.region_context[mine, :], middle_low)[0:shard]
        grads[:, 4 * width : 4 * width + hidden] = nt(r.region_second[mine, :], hidden_low)[0:shard]
        mine = pl.ds(pl.multiple_of(me * shard_ff, shard_ff), shard_ff)
        r.grads_shrink[...] = nt(r.region_active[mine, :], upstream)
        mine = pl.ds(pl.multiple_of(me * shard, shard), shard)
        for k, (grad, standard) in enumerate(((first_grad, unit), (second_grad, unit_b))):
            total = jnp.sum(grad * standard, axis=1, keepdims=True)
            r.gain_columns[...] = jnp.broadcast_to(total, (width, 128))
            at = 4 * width + hidden + 128 * k
            grads[:, at : at + 128] = r.gain_columns[mine, :]
        sibling(grads, r.grads_in, r.l_grads).start()
        sibling(r.grads_shrink, r.grads_shrink_in, r.l_grads_shrink).start()

    def one_pair(it, carry):
        pair_copy(r.cotangent, r.cot, r.cot_sem, it).wait()
        patch_pair(r, dims, it, it, jnp.minimum(it + 1, pairs - 1))
        pair_copy(r.tok, r.patch_rows, r.out_sem, it).start()
        one_copy(r.input_grad, r.grad_rows, r.grad_sem, it).start()

        if inside:

            @pl.when(it == AT_FORWARD)
            def _():
                wait_all(r.w_all.at[seg], r.l_weights.at[1])
                wait_all(r.s_all.at[seg], r.l_shrink.at[1])
                sibling(r.w_all.at[seg], r.w_all.at[seg], r.l_forward).start()
                sibling(r.s_all.at[seg], r.s_all.at[seg], r.l_forward_shrink).start()

            pl.when(it == AT_REGION)(region)
        return carry

    for it in range(pairs):
        one_copy(r.firstT, r.first_rows, r.first_sem, it).start()
    project(r, dims, 0)
    lax.fori_loop(0, dims.early, one_pair, 0)

    if inside:
        sibling(r.crossed_grad, r.returned, r.l_returned).wait()
        sibling(r.grads, r.grads_in, r.l_grads).wait()
        sibling(r.grads_shrink, r.grads_shrink_in, r.l_grads_shrink).wait()
        r.class_up[...] = r.returned[...]
        r.grads_out[...] = r.grads[...] + r.grads_in[...]
        r.shrink_out[...] = r.grads_shrink[...] + r.grads_shrink_in[...]
        peers = pl.ds(0, n_img - 1)
        wait_all(r.w_all.at[0, peers], r.l_weights.at[0])
        wait_all(r.s_all.at[0, peers], r.l_shrink.at[0])
        wait_all(r.crossed, r.l_crossed.at[0])
    for it in range(pairs):
        one_copy(r.firstT, r.first_rows, r.first_sem, it).wait()
    for it in range(dims.early):
        pair_copy(r.tok, r.patch_rows, r.out_sem, it).wait()
        one_copy(r.input_grad, r.grad_rows, r.grad_sem, it).wait()
    for k, (turned, target) in enumerate(turns):
        pltpu.make_async_copy(turned, target, r.turn_sem.at[k]).wait()


def finish_kernel(dims, *refs):
    r = SimpleNamespace(**dict(zip(dims.names, refs, strict=True)))
    width, hidden = dims.width, dims.hidden
    rows, patches, early = dims.images, dims.patches, dims.early
    pairs, lanes = rows // 2, 2 * patches
    late = pairs - early

    loads = []
    for k, name in enumerate(dims.staged):
        load = pltpu.make_async_copy(getattr(r, name), getattr(r, name + BESIDE), r.load_sem.at[k])
        setattr(r, name, getattr(r, name + BESIDE))
        loads.append(load)
    last = pl.ds(2 * early, 2 * late)
    tok_in = pltpu.make_async_copy(r.tokens.at[last], r.tok, r.late_sem.at[0])
    cot_in = pltpu.make_async_copy(r.cotangent.at[last], r.cot, r.late_sem.at[1])
    ready = pl.ds(0, 2 * early)
    rows_in = pltpu.make_async_copy(r.patch_rows.at[ready], r.ready, r.late_sem.at[2])
    rows_out = pltpu.make_async_copy(r.ready, r.patch_output.at[ready], r.late_sem.at[4])
    firsts = [one_copy(r.first_rows, r.firstT, r.first_sem, it) for it in range(pairs)]
    earlier = [one_copy(r.grad_rows, r.input_grad, r.grad_sem, it) for it in range(early)]
    bounds = (0,) + dims.bounds
    stages = [loads[a:b] for a, b in zip(bounds, bounds[1:])]
    stages[0] = firsts[early:] + [tok_in] + stages[0]
    stages[1] = [cot_in] + stages[1]
    stages[3] = stages[3] + [rows_in] + firsts[:early] + earlier

    def ask(*wanted):
        for stage in wanted:
            for load in stages[stage]:
                load.start()

    def ready(stage):
        for load in stages[stage]:
            load.wait()
        if stage == 0:
            ask(1, 2)
        if stage == 1:
            ask(3)

    ask(0)
    ready(0)
    gain_row = r.frozen_gain[...].astype(F32).reshape(1, width)
    regain_row = r.frozen_regain[...].astype(F32).reshape(1, width)
    r.gainT[...] = column(gain_row, lanes)
    r.regainT[...] = column(regain_row, lanes)
    packed = r.class_packed[...]
    tall_k = spread(packed[:, width : 2 * width])
    tall_v = spread(packed[:, 2 * width :])
    r.class_k[...] = tall_k.reshape(rows, HEADS8, width)
    r.class_v[...] = tall_v.reshape(rows, HEADS8, width)
    project(r, dims, early)
    for it in range(early, pairs):
        following = it + 1 if it + 1 < pairs else None
        wait = ready if it == early else lambda stage: None
        patch_pair(r, dims, it, it - early, following, wait)
    ready(3)
    rows_out.start()
    out = pltpu.make_async_copy(r.tok, r.patch_output.at[last], r.late_sem.at[3])
    out.start()

    upstream = r.class_up[...]
    middle = r.class_middle[...]
    unit, _, inverse = standardize(middle, 1)
    hidden_low = (nt(upstream, r.frozen_shrink[...]) * r.class_slope[...]).astype(BF16)
    second_grad = nt(hidden_low, r.frozen_expand[...])
    middle_grad = upstream.astype(F32) + norm_back(second_grad * regain_row, unit, inverse, 1)
    low = nt(middle_grad.astype(BF16), r.frozen_merge[...]).astype(BF16).astype(F32)
    tall_low = spread(low)
    low_map = nt(tall_low.astype(BF16), r.frozen_triple[:, 2 * width :])
    r.low_map[...] = low_map.reshape(rows, HEADS8, width)
    total = jnp.sum(spread(low * r.class_context[...]), axis=1, keepdims=True)
    r.class_total[...] = jnp.broadcast_to(total, (rows * HEADS8, 128)).reshape(rows, HEADS8, 128)
    r.ungainT[...] = 1.0 / r.gainT[:, 0:patches]

    def correct(step, carry):
        turns = [2 * step, 2 * step + 1]
        grads = []
        for it in turns:
            maps = jnp.concatenate([r.low_map[2 * it + b] for b in range(2)], axis=0)
            grads.append(nn(maps.astype(BF16), r.firstT[it]))
        small = []
        for it, grad in zip(turns, grads):
            for b in range(2):
                image = 2 * it + b
                span = slice(b * patches, (b + 1) * patches)
                part = grad[b * HEADS8 : (b + 1) * HEADS8, span]
                weights = r.class_probs[image]
                score_grad = weights * (part - r.class_total[image][:, 0:1])
                toward = jnp.concatenate([r.query_map[image], r.low_map[image]], axis=0) * gain_row
                left = (toward - mean(toward, 1)).astype(BF16)
                right = jnp.concatenate([score_grad * LN2, weights], axis=0)
                right = right * r.stat[it, 1:2, span]
                scores = jnp.concatenate([r.class_scores[image], part], axis=0)
                along = jnp.sum(right * scores, axis=0, keepdims=True) * (1.0 / width)
                small.append((it, image, span, score_grad, left, right.astype(BF16), along))
        products = [tn(left, right) for _, _, _, _, left, right, _ in small]
        for product, (it, image, span, score_grad, _, _, along) in zip(products, small):
            first = r.firstT[it, :, span]
            r.mixed[image] = nt(score_grad.astype(BF16), first)
            back = product - first.astype(F32) * (r.ungainT[...] * along)
            result = r.input_grad[it, :, span].astype(F32) + back
            r.result[image] = result.astype(BF16).T
        for it in turns:
            pair_copy(r.result, r.patch_gradient, r.back_sem, it).start()
        return carry

    lax.fori_loop(0, pairs // 2, correct, 0)

    self_prob = r.self_prob[...].reshape(rows * HEADS8, 128)[:, 0:1]
    tall_q = spread(packed[:, 0:width])
    self_grad = self_prob * (jnp.sum(tall_low * tall_v, axis=1, keepdims=True) - total)
    unit, _, inverse = standardize(r.class_tokens[...].astype(F32), 1)
    first = (unit * gain_row).astype(BF16).astype(F32)
    tall_first = jnp.broadcast_to(first[:, None, :], (rows, HEADS8, width))
    mixed = r.mixed[...].reshape(rows * HEADS8, width)
    mixed = mixed + self_grad * tall_first.reshape(rows * HEADS8, width)
    triple = r.frozen_triple
    query_grad = gather_heads(nn(mixed.astype(BF16), triple[:, width : 2 * width]))
    key_grad = r.class_dk[...] + (tall_q * (self_grad * HD ** (-0.5))).reshape(
        rows, HEADS8, width
    )
    value_grad = r.class_dv[...] + (tall_low * self_prob).reshape(rows, HEADS8, width)
    packed_grad = jnp.concatenate(
        [query_grad * HD ** (-0.5), jnp.sum(key_grad, axis=1), jnp.sum(value_grad, axis=1)],
        axis=1,
    ).astype(BF16)
    first_grad = nt(packed_grad, triple[...])
    back = norm_back(first_grad * gain_row, unit, inverse, 1)
    r.class_gradient[...] = (middle_grad + back).astype(BF16)
    if dims.inside:
        wide = width * 4 + hidden
        r.region_output[...] = r.region_out[...]
        r.triple_gradient[...] = r.grads_out[:, 0 : 3 * width]
        r.merge_gradient[...] = r.grads_out[:, 3 * width : 4 * width]
        r.expand_gradient[...] = r.grads_out[:, 4 * width : wide]
        r.shrink_gradient[...] = r.shrink_out[...]
        shard = r.grads_out.shape[0]
        blank = jnp.zeros((128 - shard, 128), F32)
        for k, target in enumerate((r.first_gradient, r.second_gradient)):
            columns = r.grads_out[:, wide + 128 * k : wide + 128 * (k + 1)]
            columns = jnp.concatenate([columns, blank], axis=0).T
            target[...] = columns[0:1, 0:shard]
    rows_out.wait()
    out.wait()
    for it in range(pairs):
        pair_copy(r.result, r.patch_gradient, r.back_sem, it).wait()


def normalize(values, scaling):
    centred = values - jnp.mean(values, axis=-1, keepdims=True)
    inverse = lax.rsqrt(jnp.mean(centred * centred, axis=-1, keepdims=True) + EPSILON)
    standard = centred * inverse
    return (standard * scaling, standard, inverse)


def normalize_back(upstream, standard, inverse, scaling):
    scaled = upstream * scaling
    centred = scaled - jnp.mean(scaled, axis=-1, keepdims=True)
    centred = centred - standard * jnp.mean(scaled * standard, axis=-1, keepdims=True)
    gain_grad = jnp.sum((upstream * standard).reshape(-1, upstream.shape[-1]), axis=0)
    return (centred * inverse, gain_grad)


def gelu_slope(hidden):
    return (
        0.5 * (1.0 + lax.erf(hidden * 0.7071067811865476))
        + hidden * jnp.exp(-0.5 * hidden * hidden) * 0.3989422804014327
    )


def forward_product(operand, weight):
    return lax.dot_general(
        operand, weight, (((operand.ndim - 1,), (0,)), ((), ())), preferred_element_type=F32
    )


def backward_product(upstream, weight):
    return lax.dot_general(
        upstream,
        weight,
        (((upstream.ndim - 1,), (1,)), ((), ())),
        preferred_element_type=F32,
    )


def row_product(operand, cotangent):
    left_rows = operand.reshape(-1, operand.shape[-1])
    right_rows = cotangent.reshape(-1, cotangent.shape[-1])
    return lax.dot_general(
        left_rows, right_rows, (((0,), (0,)), ((), ())), preferred_element_type=F32
    )


def heads_of(packed, portion):
    section_width = packed.shape[-1] // 3
    section = packed[..., portion * section_width : (portion + 1) * section_width]
    return section.reshape(packed.shape[:-1] + (section_width // HD, HD))


def raw_scores(queries, keyset, allowed):
    scores = jnp.einsum(
        "bqhd,bkhd->bhqk", queries, keyset, preferred_element_type=F32
    ) * HD ** (-0.5)
    if allowed is None:
        return scores
    return jnp.where(allowed[:, None], scores, -1e30)


def attend(queries, keyset, valueset, allowed):
    scores = raw_scores(queries, keyset, allowed)
    highest = jnp.max(scores, axis=-1, keepdims=True)
    logsum = highest + jnp.log(jnp.sum(jnp.exp(scores - highest), axis=-1, keepdims=True))
    weighting = jnp.exp(scores - logsum).astype(BF16)
    context = jnp.einsum("bhqk,bkhd->bqhd", weighting, valueset, preferred_element_type=F32)
    return (context.astype(BF16), logsum)


def score_terms(queries, keyset, valueset, allowed, logsum, context_grad):
    scores = raw_scores(queries, keyset, allowed)
    weighting = jnp.exp(scores - logsum)
    weight_grad = jnp.einsum(
        "bqhd,bkhd->bhqk", context_grad, valueset, preferred_element_type=F32
    )
    row_total = jnp.sum(weighting * weight_grad, axis=-1, keepdims=True)
    score_grad = (weighting * (weight_grad - row_total)).astype(BF16)
    return (weighting, score_grad, row_total)


def attend_back(queries, keyset, valueset, allowed, logsum, context_grad):
    weighting, score_grad, row_total = score_terms(
        queries, keyset, valueset, allowed, logsum, context_grad
    )
    value_grad = jnp.einsum(
        "bhqk,bqhd->bkhd",
        weighting.astype(BF16),
        context_grad,
        preferred_element_type=F32,
    )
    query_grad = jnp.einsum(
        "bhqk,bkhd->bqhd", score_grad, keyset, preferred_element_type=F32
    ) * HD ** (-0.5)
    key_grad = jnp.einsum(
        "bhqk,bqhd->bkhd", score_grad, queries, preferred_element_type=F32
    ) * HD ** (-0.5)
    return (query_grad, key_grad, value_grad)


def block_head(inputs, scaling, triple):
    normed, standard, inverse = normalize(inputs, scaling)
    first_low = normed.astype(BF16)
    packed = forward_product(first_low, triple).astype(BF16)
    return (first_low, standard, inverse, packed)


def block_tail(inputs, context, regain, merger, expand, shrink):
    middle = inputs + forward_product(context, merger)
    normed, standard, inverse = normalize(middle, regain)
    second = normed.astype(BF16)
    hidden = forward_product(second, expand)
    active = jax.nn.gelu(hidden, approximate=False).astype(BF16)
    result = middle + forward_product(active, shrink)
    return (result, (standard, inverse, second, hidden, active))


def tail_back(upstream, kept_tail, regain, merger, expand, shrink):
    standard, inverse, second, hidden, active = kept_tail
    out_low = upstream.astype(BF16)
    active_grad = backward_product(out_low, shrink)
    hidden_low = (active_grad * gelu_slope(hidden)).astype(BF16)
    second_grad = backward_product(hidden_low, expand)
    norm_grad, regain_grad = normalize_back(second_grad, standard, inverse, regain)
    middle_grad = upstream + norm_grad
    middle_low = middle_grad.astype(BF16)
    context_low = backward_product(middle_low, merger).astype(BF16)
    return (middle_grad, context_low, regain_grad, (middle_low, hidden_low, out_low))


def region_outside(crossed, region_number, region_cotangent, shards_in):
    crossed = lax.ppermute(crossed, SEG, [(0, 1), (1, 0)])
    images = crossed.shape[1]
    model_width = crossed.shape[2]
    gathered = [lax.all_gather(shard, IMG, axis=0, tiled=True) for shard in shards_in]
    full_gain, triple, merger, full_regain, expand, shrink = gathered
    scaling = full_gain.astype(F32)
    regain = full_regain.astype(F32)
    region_in = crossed.astype(F32)
    first_low, standard, inverse, packed = block_head(region_in, scaling, triple)
    local_keys = packed[..., model_width : 2 * model_width]
    local_values = packed[..., 2 * model_width :]
    all_keys, all_values = (
        lax.all_gather(local_keys, IMG, axis=1, tiled=True),
        lax.all_gather(local_values, IMG, axis=1, tiled=True),
    )
    head_shape = all_keys.shape[:-1] + (model_width // HD, HD)
    keyset = all_keys.reshape(head_shape)
    valueset = all_values.reshape(head_shape)
    queries = heads_of(packed, 0)
    first_slot = lax.axis_index(IMG) * images
    own_number = lax.dynamic_slice_in_dim(region_number, first_slot, images, 1)
    allowed = own_number[:, :, None] == region_number[:, None, :]
    context, logsum = attend(queries, keyset, valueset, allowed)
    context = context.reshape(region_in.shape)
    region_result, kept_tail = block_tail(region_in, context, regain, merger, expand, shrink)
    region_output = region_result.astype(BF16)
    upstream = region_cotangent.astype(F32)
    middle_grad, context_low, second_gain_grad, low_rows = tail_back(
        upstream, kept_tail, regain, merger, expand, shrink
    )
    middle_low, hidden_low, out_low = low_rows
    context_heads = context_low.reshape(queries.shape)
    query_grad, key_grad, value_grad = attend_back(
        queries, keyset, valueset, allowed, logsum, context_heads
    )
    key_sum, value_sum = (
        lax.psum_scatter(key_grad.reshape(all_keys.shape), IMG, scatter_dimension=1, tiled=True),
        lax.psum_scatter(
            value_grad.reshape(all_values.shape), IMG, scatter_dimension=1, tiled=True
        ),
    )
    packed_grad = jnp.concatenate(
        [query_grad.reshape(region_in.shape), key_sum, value_sum], axis=-1
    ).astype(BF16)
    norm_grad, first_gain_grad = normalize_back(
        backward_product(packed_grad, triple), standard, inverse, scaling
    )
    input_grad = (middle_grad + norm_grad).astype(BF16)
    second_low = kept_tail[2]
    active_low = kept_tail[4]
    shards = (
        lax.psum_scatter(first_gain_grad, IMG, scatter_dimension=0, tiled=True),
        lax.psum_scatter(
            row_product(first_low, packed_grad), IMG, scatter_dimension=0, tiled=True
        ),
        lax.psum_scatter(row_product(context, middle_low), IMG, scatter_dimension=0, tiled=True),
        lax.psum_scatter(second_gain_grad, IMG, scatter_dimension=0, tiled=True),
        lax.psum_scatter(
            row_product(second_low, hidden_low), IMG, scatter_dimension=0, tiled=True
        ),
        lax.psum_scatter(row_product(active_low, out_low), IMG, scatter_dimension=0, tiled=True),
    )
    totals = tuple(lax.psum(shard.astype(BF16), SEG).astype(F32) for shard in shards)
    return region_output, lax.ppermute(input_grad, SEG, [(0, 1), (1, 0)]), totals


def local(
    n_img,
    patch_tokens,
    class_tokens,
    region_number,
    frozen_gain,
    frozen_triple,
    frozen_merge,
    frozen_regain,
    frozen_expand,
    frozen_shrink,
    gain_first,
    weight_triple,
    weight_merge,
    gain_second,
    weight_expand,
    weight_shrink,
    patch_cotangent,
    region_cotangent,
):
    micros, per, patches, width = patch_tokens.shape
    hidden = frozen_expand.shape[1]
    images = micros * per
    shard, shard_ff = width // n_img, hidden // n_img
    lanes, pairs, keys, heads = 2 * patches, images // 2, n_img * images, width // HD
    inside = keys == patches and shard == PAD - 8 and images == 16 and width == 384

    class_rows = class_tokens.reshape(images, width)
    inputs = dict(
        tokens=patch_tokens.reshape(images, patches, width),
        cotangent=patch_cotangent.reshape(images, patches, width),
        class_tokens=class_rows,
        frozen_gain=frozen_gain,
        frozen_regain=frozen_regain,
        frozen_triple=frozen_triple,
        frozen_merge=frozen_merge,
        frozen_expand=frozen_expand,
        frozen_shrink=frozen_shrink,
    )
    if inside:
        inputs |= dict(
            gain_first=gain_first,
            gain_second=gain_second,
            region_cotangent=region_cotangent.reshape(images, width),
            region_number=region_number,
            weight_triple=weight_triple,
            weight_merge=weight_merge,
            weight_expand=weight_expand,
            weight_shrink=weight_shrink,
        )
    vmem = pl.BlockSpec(memory_space=pltpu.VMEM)
    hbm = pl.BlockSpec(memory_space=pl.ANY)
    streams = 2
    in_specs = [hbm] * streams + [vmem] * (len(inputs) - streams)

    shape = jax.ShapeDtypeStruct
    columns = 4 * width + hidden + 256
    large = dict(
        patch_rows=shape((images, patches, width), BF16),
        first_rows=shape((pairs, width, lanes), BF16),
        grad_rows=shape((pairs, width, lanes), BF16),
        triple_turned=shape((3 * width, width), BF16),
        merge_turned=shape((width, width), BF16),
        expand_turned=shape((hidden, width), BF16),
        shrink_turned=shape((width, hidden), BF16),
    )
    small = dict(
        stat=shape((pairs, 8, lanes), F32),
        class_packed=shape((images, 3 * width), F32),
        class_context=shape((images, width), F32),
        class_middle=shape((images, width), F32),
        class_slope=shape((images, hidden), F32),
        query_map=shape((images, HEADS8, width), F32),
        class_probs=shape((images, HEADS8, patches), F32),
        class_scores=shape((images, HEADS8, patches), F32),
        self_prob=shape((images, HEADS8, 128), F32),
        class_dk=shape((images, HEADS8, width), F32),
        class_dv=shape((images, HEADS8, width), F32),
    )
    if inside:
        small |= dict(
            class_up=shape((images, width), BF16),
            region_out=shape((images, width), BF16),
            grads_out=shape((shard, columns), F32),
            shrink_out=shape((shard_ff, width), F32),
        )
    else:
        small |= dict(class_out=shape((images, width), BF16))
    outputs = large | small
    out_specs = [hbm] * len(large) + [vmem] * len(small)

    v = pltpu.VMEM
    dma = pltpu.SemaphoreType.DMA
    working = dict(
        gainT=v((width, lanes), F32),
        regainT=v((width, lanes), F32),
        qkv=v((3 * width, lanes), BF16),
        ctx=v((width, lanes), BF16),
        probs=v((2 * heads, patches, patches), BF16),
        shares=v((2, HEADS8, patches), F32),
        class_weights=v((2, HEADS8, patches), F32),
        active=v((hidden, lanes), BF16),
        slope=v((hidden, lanes), BF16),
        packed_grad=v((3 * width, lanes), BF16),
        low_grad=v((width, lanes), BF16),
        class_k=v((images, HEADS8, width), F32),
        class_v=v((images, HEADS8, width), F32),
        mixed=v((images, HEADS8, width), F32),
        firstT=v((pairs, width, lanes), BF16),
        input_grad=v((pairs, width, lanes), BF16),
        first_sem=dma((pairs,)),
        grad_sem=dma((pairs,)),
    )
    turned = dict(
        tripleT=v((3 * width, width), BF16),
        mergeT=v((width, width), BF16),
        expandT=v((hidden, width), BF16),
        shrinkT=v((width, hidden), BF16),
    )
    scratch = working | turned | dict(
        tok=v((images, patches, width), BF16),
        cot=v((images, patches, width), BF16),
        class_first=v((images, HEADS8, width), F32),
        self_score=v((images, HEADS8, 128), F32),
        tok_sem=dma((pairs,)),
        cot_sem=dma((pairs,)),
        out_sem=dma((pairs,)),
        turn_sem=dma((len(turned),)),
    )
    if inside:
        deep = PAD * n_img
        scratch |= dict(
            class_out=v((images, width), BF16),
            crossed=v((n_img, images, width), BF16),
            crossed_grad=v((images, width), BF16),
            returned=v((images, width), BF16),
            shard_gains=v((8, 128), F32),
            w_own=v((2, PAD, 4 * width), BF16),
            w_all=v((2, n_img, PAD, 4 * width), BF16),
            s_own=v((2, shard_ff // 2, width), BF16),
            s_all=v((2, n_img, shard_ff // 2, width), BF16),
            region_shrink=v((hidden, width), BF16),
            region_first=v((deep, keys), BF16),
            region_context=v((deep, keys), BF16),
            region_second=v((deep, keys), BF16),
            region_active=v((hidden, keys), BF16),
            region_rows=v((keys, width), F32),
            gain_columns=v((width, 128), F32),
            grads=v((shard, columns), F32),
            grads_in=v((shard, columns), F32),
            grads_shrink=v((shard_ff, width), F32),
            grads_shrink_in=v((shard_ff, width), F32),
            l_weights=dma((2,)),
            l_shrink=dma((2,)),
            l_forward=dma((2,)),
            l_forward_shrink=dma((2,)),
            l_crossed=dma((2,)),
            l_returned=dma((2,)),
            l_grads=dma((2,)),
            l_grads_shrink=dma((2,)),
        )
    sizes = dict(
        n_img=n_img,
        width=width,
        hidden=hidden,
        images=images,
        patches=patches,
        inside=inside,
        early=pairs - LATE,
    )
    limit = dict(vmem_limit_bytes=60 * 1024 * 1024)
    remote = dict(collective_id=0, has_side_effects=True) if inside else {}
    names = list(inputs) + list(outputs) + list(scratch)
    results = pl.pallas_call(
        functools.partial(patch_kernel, SimpleNamespace(names=names, **sizes)),
        out_shape=list(outputs.values()),
        in_specs=in_specs,
        out_specs=out_specs,
        scratch_shapes=list(scratch.values()),
        compiler_params=pltpu.CompilerParams(**limit, **remote),
    )(*inputs.values())
    done = dict(zip(outputs, results, strict=True))

    if not inside:
        class_out = done.pop(list(small)[-1])
        region_output, class_up, grads = region_outside(
            class_out.reshape(class_tokens.shape),
            region_number,
            region_cotangent,
            (gain_first, weight_triple, weight_merge, gain_second, weight_expand, weight_shrink),
        )
        done |= dict(class_up=class_up.reshape(images, width))

    streamed = [done.pop(name) for name in large]
    done = SimpleNamespace(**done)
    tripleT, mergeT, expandT, shrinkT = streamed[-len(turned) :]
    stages = (
        dict(class_packed=done.class_packed, stat=done.stat, tripleT=tripleT),
        dict(mergeT=mergeT, frozen_shrink=frozen_shrink, expandT=expandT),
        dict(
            shrinkT=shrinkT,
            frozen_expand=frozen_expand,
            frozen_merge=frozen_merge,
            frozen_triple=frozen_triple,
            class_dk=done.class_dk,
            class_dv=done.class_dv,
        ),
        dict(class_tokens=class_rows) | vars(done),
    )
    staged, bounds = {}, ()
    for stage in stages:
        staged |= {name: a for name, a in stage.items() if name not in staged}
        bounds += (len(staged),)
    inputs = dict(
        tokens=patch_tokens.reshape(images, patches, width),
        cotangent=patch_cotangent.reshape(images, patches, width),
        patch_rows=streamed[0],
        first_rows=streamed[1],
        grad_rows=streamed[2],
    )
    inputs |= staged
    inputs |= dict(frozen_gain=frozen_gain, frozen_regain=frozen_regain)
    outputs = dict(
        patch_output=shape((images, patches, width), BF16),
        patch_gradient=shape((images, patches, width), BF16),
        class_gradient=shape((images, width), BF16),
    )
    out_specs = [hbm] * 2 + [vmem]
    if inside:
        ready = dict(
            region_output=shape((images, width), BF16),
            first_gradient=shape((1, shard), F32),
            triple_gradient=shape((shard, 3 * width), F32),
            merge_gradient=shape((shard, width), F32),
            second_gradient=shape((1, shard), F32),
            expand_gradient=shape((shard, hidden), F32),
            shrink_gradient=shape((shard_ff, width), F32),
        )
        outputs |= ready
        out_specs += [vmem] * len(ready)
    scratch = working | dict(
        tok=v((2 * LATE, patches, width), BF16),
        cot=v((2 * LATE, patches, width), BF16),
        result=v((images, patches, width), BF16),
        ungainT=v((width, patches), F32),
        low_map=v((images, HEADS8, width), F32),
        class_total=v((images, HEADS8, 128), F32),
        load_sem=dma((len(staged),)),
        ready=v((images - 2 * LATE, patches, width), BF16),
        late_sem=dma((5,)),
        back_sem=dma((pairs,)),
    )
    scratch |= {name + BESIDE: v(a.shape, a.dtype) for name, a in staged.items()}
    names = list(inputs) + list(outputs) + list(scratch)
    sizes |= dict(names=names, staged=list(staged), bounds=bounds)
    results = pl.pallas_call(
        functools.partial(finish_kernel, SimpleNamespace(**sizes)),
        out_shape=list(outputs.values()),
        in_specs=[hbm] * (len(inputs) - 2) + [vmem] * 2,
        out_specs=out_specs,
        scratch_shapes=list(scratch.values()),
        compiler_params=pltpu.CompilerParams(**limit),
    )(*inputs.values())
    done = SimpleNamespace(**dict(zip(outputs, results, strict=True)))
    if inside:
        region_output = done.region_output.reshape(class_tokens.shape)
        grads = (
            done.first_gradient.reshape(shard),
            done.triple_gradient,
            done.merge_gradient,
            done.second_gradient.reshape(shard),
            done.expand_gradient,
            done.shrink_gradient,
        )
    return (
        done.patch_output.reshape(patch_tokens.shape),
        region_output,
        done.patch_gradient.reshape(patch_tokens.shape),
        done.class_gradient.reshape(class_tokens.shape),
        *grads,
    )


def solution(mesh):
    patch, row = P(SEG, IMG, None, None), P(SEG, IMG, None)
    gain, weight, whole = P(IMG), P(IMG, None), P()
    block = (gain, weight, weight, gain, weight, weight)
    placed = (patch, row, P(SEG, None)) + (whole,) * 6 + block + (patch, row)
    return jax.shard_map(
        functools.partial(local, mesh.shape[IMG]),
        mesh=mesh,
        in_specs=placed,
        out_specs=(patch, row, patch, row) + block,
        check_vma=False,
    )
```

```python
import functools
from types import SimpleNamespace

import jax
import jax.numpy as jnp
from jax import lax
from jax.experimental import pallas as pl
from jax.experimental.pallas import tpu as pltpu
from jax.sharding import PartitionSpec as P

SEG = "segment"
IMG = "img"
HD = 64
HEADS8 = 8
EPSILON = 1e-06
LOG2E = 1.4426950408889634
LN2 = 0.6931471805599453
ROOT_HALF = 0.7071067811865476
DENSITY = 0.3989422804014327
LOG2_DENSITY = -1.3257480647361593
F32 = jnp.float32
BF16 = jnp.bfloat16
MESH = pl.DeviceIdType.MESH
NEG = -1e30
PAD = 32
BESIDE = "_"

AT_FORWARD = 5
AT_REGION = 6
LATE = 1


def nn(a, b):
    return lax.dot_general(a, b, (((1,), (0,)), ((), ())), preferred_element_type=F32)


def nt(a, b):
    return lax.dot_general(a, b, (((1,), (1,)), ((), ())), preferred_element_type=F32)


def tn(a, b):
    return lax.dot_general(a, b, (((0,), (0,)), ((), ())), preferred_element_type=F32)


def mean(values, axis):
    return jnp.sum(values, axis=axis, keepdims=True) * (1.0 / values.shape[axis])


def standardize(values, axis):
    centre = mean(values, axis)
    centred = values - centre
    inverse = lax.rsqrt(mean(centred * centred, axis) + EPSILON)
    return centred * inverse, centre, inverse


def norm_back(scaled, standard, inverse, axis):
    return inverse * (
        scaled - mean(scaled, axis) - standard * mean(scaled * standard, axis)
    )


def gelu_pair(hidden):
    upto = 0.5 + 0.5 * lax.erf(hidden * ROOT_HALF)
    bell = jnp.exp2(hidden * hidden * (-0.5 * LOG2E))
    return hidden * upto, upto + hidden * (bell * DENSITY)


def gelu_pair_low(half):
    twice = (1.0 + lax.erf(half * (2.0 * ROOT_HALF))).astype(BF16)
    bell = jnp.exp2(half * half * (-2.0 * LOG2E) + (LOG2_DENSITY + 2.0)).astype(BF16)
    low = half.astype(BF16)
    return low * twice, twice + low * bell


def own_heads(rows, width):
    shape = (rows * HEADS8, width)
    lane = lax.broadcasted_iota(jnp.int32, shape, 1) // HD
    return lane == lax.rem(lax.broadcasted_iota(jnp.int32, shape, 0), HEADS8)


def spread(values):
    rows, width = values.shape
    tall = jnp.broadcast_to(values[:, None, :], (rows, HEADS8, width))
    return jnp.where(own_heads(rows, width), tall.reshape(rows * HEADS8, width), 0.0)


def gather_heads(values):
    tall, width = values.shape
    kept = jnp.where(own_heads(tall // HEADS8, width), values, 0.0)
    return jnp.sum(kept.reshape(tall // HEADS8, HEADS8, width), axis=1)


def column(row, lanes):
    tall = jnp.broadcast_to(row, (128, row.shape[1])).T
    return jnp.concatenate([tall] * (lanes // 128), axis=1)


def pair_copy(source, target, sems, it):
    part = pl.ds(2 * it, 2)
    return pltpu.make_async_copy(source.at[part], target.at[part], sems.at[it])


def one_copy(source, target, sems, it):
    return pltpu.make_async_copy(source.at[it], target.at[it], sems.at[it])


def padded(values, shard, n):
    blank = jnp.zeros((PAD - shard, values.shape[1]), values.dtype)
    parts = []
    for j in range(n):
        parts += [values[shard * j : shard * (j + 1)], blank]
    return jnp.concatenate(parts, axis=0)


def trimmed(values, shard, n):
    return jnp.concatenate([values[PAD * j : PAD * j + shard] for j in range(n)], axis=0)


def project(r, dims, it):
    width = dims.width
    first = r.firstT[it]
    queries = nn(r.tripleT[0:width, :], first) * (LOG2E * HD ** (-0.5))
    r.qkv[0:width, :] = queries.astype(BF16)
    r.qkv[width:, :] = nn(r.tripleT[width:, :], first).astype(BF16)


def patch_pair(r, dims, it, slot, following, ready=lambda stage: None):
    width, hidden, patches = dims.width, dims.hidden, dims.patches
    heads = width // HD
    block_head = own_heads(1, width)
    span = [slice(b * patches, (b + 1) * patches) for b in range(2)]
    qkv, ctx, probs = r.qkv, r.ctx, r.probs
    values = jnp.concatenate([r.tok[2 * slot + b].T for b in range(2)], axis=1).astype(F32)
    order = [(b, h) for h in range(heads) for b in range(2)]
    key_rows = [r.class_k[2 * it + b].astype(BF16) for b in range(2)]
    value_rows = [r.class_v[2 * it + b].astype(BF16) for b in range(2)]
    class_scores = [nn(key_rows[b], qkv[0:width, span[b]]) for b in range(2)]

    def part(which, turn):
        b, h = order[turn]
        return qkv[which * width + HD * h : which * width + HD * (h + 1), span[b]]

    scores, mixes, class_weights, shares = {0: tn(part(1, 0), part(0, 0))}, [], [], []
    for turn, (b, h) in enumerate(order):
        if turn + 1 < len(order):
            scores[turn + 1] = tn(part(1, turn + 1), part(0, turn + 1))
        class_score = class_scores[b][h : h + 1, :]
        top = jnp.maximum(jnp.max(scores[turn], axis=0, keepdims=True), class_score)
        weights = jnp.exp2(scores.pop(turn) - top)
        class_weight = jnp.exp2(class_score - top)
        shares.append(1.0 / (jnp.sum(weights, axis=0, keepdims=True) + class_weight))
        class_weights.append(class_weight)
        probs[b * heads + h] = weights.astype(BF16)
        if turn:
            last = order[turn - 1]
            mixes.append(nn(part(2, turn - 1), probs[last[0] * heads + last[1]]))
    mixes.append(nn(part(2, len(order) - 1), probs[2 * heads - 1]))
    blank = [jnp.zeros((HEADS8 - heads, patches), F32)]
    for b in range(2):
        weights = jnp.concatenate(class_weights[b::2] + blank, axis=0)
        r.class_weights[b] = weights
        r.shares[b] = jnp.concatenate(shares[b::2] + blank, axis=0)
        from_class = tn(value_rows[b], weights.astype(BF16))
        for h in range(heads):
            at = slice(HD * h, HD * (h + 1))
            mix = mixes[2 * h + b] + from_class[at]
            ctx[at, span[b]] = (mix * shares[2 * h + b]).astype(BF16)
    ready(1)
    merged = nn(r.mergeT[...], ctx[...])
    upstream = jnp.concatenate([r.cot[2 * slot + b].T for b in range(2)], axis=1)
    half_upstream = upstream * BF16(0.5)
    third = hidden // 3
    chunks = [slice(c, c + third) for c in range(0, hidden, third)]

    def active_grad(at):
        return nn(r.frozen_shrink[at, :], half_upstream).astype(BF16)

    ahead = len(chunks) // 2
    active_grads = [active_grad(at) for at in chunks[:ahead]]
    middle = values + merged
    unit_b, _, inverse_b = standardize(middle, 0)
    second = (unit_b * r.regainT[...]).astype(BF16)
    coming = nn(r.expandT[chunks[0], :], second)
    for k, at in enumerate(chunks):
        current = coming
        if k + 1 < len(chunks):
            coming = nn(r.expandT[chunks[k + 1], :], second)
        if ahead + k < len(chunks):
            active_grads.append(active_grad(chunks[ahead + k]))
        active, slope = gelu_pair_low(current)
        r.active[at, :] = active.astype(BF16)
        r.slope[at, :] = active_grads[k] * slope.astype(BF16)
    ready(2)
    second_grad = nn(r.frozen_expand[...], r.slope[...])
    shrunk = nn(r.shrinkT[...], r.active[...])
    middle_grad = upstream.astype(F32) + norm_back(
        second_grad * r.regainT[...], unit_b, inverse_b, 0
    )
    result = middle + shrunk
    for b in range(2):
        r.tok[2 * slot + b] = result[:, span[b]].astype(BF16).T
    context_grad = nn(r.frozen_merge[...], middle_grad.astype(BF16))
    low_grad, packed_grad = r.low_grad, r.packed_grad
    totals, from_class = [[], []], []
    for b in range(2):
        for h in range(heads):
            at = slice(HD * h, HD * (h + 1))
            low = context_grad[at, span[b]] * r.shares[b][h : h + 1, :]
            totals[b].append(
                jnp.sum(low * ctx[at, span[b]].astype(F32), axis=0, keepdims=True)
            )
            low_grad[at, span[b]] = low.astype(BF16)
        all_low = low_grad[:, span[b]]
        weights = r.class_weights[b]
        class_grad = weights * (
            nn(value_rows[b], all_low) - jnp.concatenate(totals[b] + blank, axis=0)
        )
        class_grad = class_grad.astype(BF16)
        from_class.append(tn(key_rows[b], class_grad))
        dk = nt(class_grad, qkv[0:width, span[b]]) * LN2
        dv = nt(weights.astype(BF16), all_low)
        r.class_dk[2 * it + b] = jnp.where(block_head, dk, 0.0)
        r.class_dv[2 * it + b] = jnp.where(block_head, dv, 0.0)

    def low_part(turn):
        b, h = order[turn]
        return low_grad[HD * h : HD * (h + 1), span[b]]

    def put(which, turn, grad):
        b, h = order[turn]
        rows_at = slice(which * width + HD * h, which * width + HD * (h + 1))
        packed_grad[rows_at, span[b]] = grad.astype(BF16)

    def key_and_query(turn, score_grad):
        b, h = order[turn]
        put(1, turn, nt(part(0, turn), score_grad) * LN2)
        query_grad = nn(part(1, turn), score_grad) + from_class[b][HD * h : HD * (h + 1)]
        put(0, turn, query_grad * HD ** (-0.5))

    grads, score_grads = {0: tn(part(2, 0), low_part(0))}, {}
    for turn, (b, h) in enumerate(order):
        if turn + 1 < len(order):
            grads[turn + 1] = tn(part(2, turn + 1), low_part(turn + 1))
        weights = probs[b * heads + h]
        put(2, turn, nt(low_part(turn), weights))
        score_grads[turn] = weights * (grads.pop(turn) - totals[b][h]).astype(BF16)
        if turn:
            key_and_query(turn - 1, score_grads.pop(turn - 1))
    key_and_query(len(order) - 1, score_grads.pop(len(order) - 1))
    first_grad = nn(r.frozen_triple[...], packed_grad[...])
    if following is not None:
        project(r, dims, following)
    centre, inverse = r.stat[it, 0:1, :], r.stat[it, 1:2, :]
    unit = (values - centre) * inverse
    back = norm_back(first_grad * r.gainT[...], unit, inverse, 0)
    r.input_grad[it] = (middle_grad + back).astype(BF16)


def patch_kernel(dims, *refs):
    r = SimpleNamespace(**dict(zip(dims.names, refs, strict=True)))
    n_img, width, hidden, inside = dims.n_img, dims.width, dims.hidden, dims.inside
    heads = width // HD
    rows, patches = dims.images, dims.patches
    pairs, lanes = rows // 2, 2 * patches
    shard = width // n_img
    shard_ff = hidden // n_img

    if inside:
        seg = lax.axis_index(SEG)
        me = lax.axis_index(IMG)
        barrier = pltpu.get_barrier_semaphore()

        def sibling(src, dst, link):
            return pltpu.make_async_remote_copy(
                src_ref=src,
                dst_ref=dst,
                send_sem=link.at[0],
                recv_sem=link.at[1],
                device_id={SEG: 1 - seg},
                device_id_type=MESH,
            )

        def to_peers(source, target, link):
            def send(step, carry):
                pltpu.make_async_remote_copy(
                    src_ref=source,
                    dst_ref=target,
                    send_sem=link.at[0],
                    recv_sem=link.at[1],
                    device_id={IMG: lax.rem(me + step, n_img)},
                    device_id_type=MESH,
                ).start()
                return carry

            lax.fori_loop(1, n_img, send, 0)
            pltpu.make_async_copy(source, target, link.at[1]).start()

        def to_other_segment(source, target, link):
            def send(step, carry):
                pltpu.make_async_remote_copy(
                    src_ref=source,
                    dst_ref=target,
                    send_sem=link.at[0],
                    recv_sem=link.at[1],
                    device_id={SEG: 1 - seg, IMG: lax.rem(me + step, n_img)},
                    device_id_type=MESH,
                ).start()
                return carry

            lax.fori_loop(0, n_img, send, 0)

        def wait_all(whole, sem):
            pltpu.make_async_copy(whole, whole, sem).wait()

        def greet(step, carry):
            peer = lax.rem(me + step, n_img)
            for other in range(2):
                pl.semaphore_signal(
                    barrier,
                    inc=1,
                    device_id={SEG: lax.rem(seg + other, 2), IMG: peer},
                    device_id_type=MESH,
                )
            return carry

        lax.fori_loop(1, n_img, greet, 0)
        pl.semaphore_signal(barrier, inc=1, device_id={SEG: 1 - seg}, device_id_type=MESH)

    for it in range(pairs):
        pair_copy(r.tokens, r.tok, r.tok_sem, it).start()
    for it in range(dims.early):
        pair_copy(r.cotangent, r.cot, r.cot_sem, it).start()

    gain_row = r.frozen_gain[...].astype(F32).reshape(1, width)
    regain_row = r.frozen_regain[...].astype(F32).reshape(1, width)
    r.tripleT[...] = r.frozen_triple[...].T
    r.mergeT[...] = r.frozen_merge[...].T
    r.expandT[...] = r.frozen_expand[...].T * BF16(0.5)
    r.shrinkT[...] = r.frozen_shrink[...].T
    turns = (
        (r.tripleT, r.triple_turned),
        (r.mergeT, r.merge_turned),
        (r.expandT, r.expand_turned),
        (r.shrinkT, r.shrink_turned),
    )
    for k, (turned, target) in enumerate(turns):
        pltpu.make_async_copy(turned, target, r.turn_sem.at[k]).start()
    r.gainT[...] = column(gain_row, lanes)
    r.regainT[...] = column(regain_row, lanes)

    if inside:
        upstream = r.region_cotangent[...].astype(F32)
        fill = [upstream[8 * k : 8 * k + 8] for k in range(rows // 8)]
        r.shard_gains[...] = jnp.zeros_like(r.shard_gains)
        r.shard_gains[0:1, 0:shard] = r.gain_first[...].astype(F32).reshape(1, shard)
        r.shard_gains[1:2, 0:shard] = r.gain_second[...].astype(F32).reshape(1, shard)
        for k in range(2):
            tall = column(r.shard_gains[k : k + 1, :], 128)
            fill += [tall[at : at + 8] for at in range(0, shard, 8)]
        fill = jnp.concatenate(fill, axis=1)
        triple = r.weight_triple[...].astype(F32)
        merge = r.weight_merge[...].astype(F32)
        expand = r.weight_expand[...].astype(F32)
        first_half = jnp.concatenate([triple, merge], axis=1)
        r.w_own[0] = jnp.concatenate([first_half, fill], axis=0).astype(BF16)
        r.w_own[1] = jnp.concatenate([expand, fill], axis=0).astype(BF16)
        for k in range(2):
            r.s_own[k] = r.weight_shrink[k * shard_ff // 2 : (k + 1) * shard_ff // 2, :]

    class_in = r.class_tokens[...].astype(F32)
    class_unit, _, _ = standardize(class_in, 1)
    class_first = (class_unit * gain_row).astype(BF16)
    class_packed = nn(class_first, r.frozen_triple[...]).astype(BF16).astype(F32)
    r.class_packed[...] = class_packed
    tall_q = spread(class_packed[:, 0:width])
    tall_k = spread(class_packed[:, width : 2 * width])
    tall_v = spread(class_packed[:, 2 * width :])
    r.class_k[...] = tall_k.reshape(rows, HEADS8, width)
    r.class_v[...] = tall_v.reshape(rows, HEADS8, width)
    query_map = nt(tall_q.astype(BF16), r.frozen_triple[:, width : 2 * width])
    query_map = query_map * (LOG2E * HD ** (-0.5))
    r.query_map[...] = query_map.reshape(rows, HEADS8, width)
    self_score = jnp.sum(tall_q * tall_k, axis=1, keepdims=True) * (LOG2E * HD ** (-0.5))
    r.self_score[...] = jnp.broadcast_to(self_score, (rows * HEADS8, 128)).reshape(
        rows, HEADS8, 128
    )
    r.class_first[...] = jnp.broadcast_to(
        class_first.astype(F32)[:, None, :], (rows, HEADS8, width)
    )

    def class_norm(it):
        pair_copy(r.tokens, r.tok, r.tok_sem, it).wait()
        values = jnp.concatenate([r.tok[2 * it + b].T for b in range(2)], axis=1).astype(F32)
        unit, centre, inverse = standardize(values, 0)
        first = (unit * r.gainT[...]).astype(BF16)
        r.firstT[it] = first
        r.stat[it, 0:1, :] = centre
        r.stat[it, 1:2, :] = inverse
        return first

    def class_forward(step, carry):
        turns = [4 * step + k for k in range(4)]
        firsts = [class_norm(it) for it in turns]
        scores = []
        for it, first in zip(turns, firsts):
            maps = jnp.concatenate([r.query_map[2 * it + b] for b in range(2)], axis=0)
            scores.append(nn(maps.astype(BF16), first))
        spread_out = []
        for it, first, score in zip(turns, firsts, scores):
            for b in range(2):
                part = score[b * HEADS8 : (b + 1) * HEADS8, b * patches : (b + 1) * patches]
                r.class_scores[2 * it + b] = part
                alone = r.self_score[2 * it + b][:, 0:1]
                top = jnp.maximum(jnp.max(part, axis=1, keepdims=True), alone)
                weights = jnp.exp2(part - top)
                weight_alone = jnp.exp2(alone - top)
                share = 1.0 / (jnp.sum(weights, axis=1, keepdims=True) + weight_alone)
                weights = weights * share
                weight_alone = weight_alone * share
                r.class_probs[2 * it + b] = weights
                r.self_prob[2 * it + b] = jnp.broadcast_to(weight_alone, (HEADS8, 128))
                span = first[:, b * patches : (b + 1) * patches]
                spread_out.append((2 * it + b, weights, weight_alone, span))
        for image, weights, weight_alone, span in spread_out:
            mixed = nt(weights.astype(BF16), span)
            r.mixed[image] = mixed + weight_alone * r.class_first[image]
        return carry

    lax.fori_loop(0, pairs // 4, class_forward, 0)
    if inside:
        pl.semaphore_wait(barrier, 2 * n_img - 1)
        to_peers(r.w_own.at[seg], r.w_all.at[seg, me], r.l_weights)
        to_peers(r.s_own.at[seg], r.s_all.at[seg, me], r.l_shrink)

    mixed = r.mixed[...].reshape(rows * HEADS8, width).astype(BF16)
    class_context = gather_heads(nn(mixed, r.frozen_triple[:, 2 * width :])).astype(BF16)
    class_middle = class_in + nn(class_context, r.frozen_merge[...])
    class_unit_b, _, _ = standardize(class_middle, 1)
    class_second = (class_unit_b * regain_row).astype(BF16)
    class_active, class_slope = gelu_pair(nn(class_second, r.frozen_expand[...]))
    class_out = class_middle + nn(class_active.astype(BF16), r.frozen_shrink[...])
    r.class_context[...] = class_context.astype(F32)
    r.class_middle[...] = class_middle
    r.class_slope[...] = class_slope
    r.class_out[...] = class_out.astype(BF16)
    if inside:
        to_other_segment(r.class_out, r.crossed.at[me], r.l_crossed)

    def region():
        keys = n_img * rows
        wait_all(r.crossed, r.l_crossed.at[1])
        sibling(r.w_all.at[seg], r.w_all.at[seg], r.l_forward).wait()
        sibling(r.s_all.at[seg], r.s_all.at[seg], r.l_forward_shrink).wait()
        half = shard_ff // 2
        for j in range(n_img):
            for k in range(2):
                down = shard_ff * j + half * k
                r.region_shrink[down : down + half, :] = r.s_all[k, j]
        deep = PAD * n_img
        w_triple = r.w_all[0, :, :, 0 : 3 * width].reshape(deep, 3 * width)
        w_merge = r.w_all[0, :, :, 3 * width :].reshape(deep, width)
        w_expand = r.w_all[1].reshape(deep, hidden)
        ups, wide = [], [[], []]
        for j in range(n_img):
            fill = r.w_all[seg, j].astype(F32)[shard:PAD]
            ups += [fill[:, width * k : width * (k + 1)] for k in range(rows // 8)]
            for k in range(2):
                first_at = width * (rows // 8) + 128 * (shard // 8) * k
                for at in range(first_at, first_at + 128 * (shard // 8), 128):
                    wide[k].append(fill[:, at : at + 128])
        wide = [jnp.concatenate(w, axis=0) for w in wide]
        gain, regain = (jnp.concatenate([g] * (keys // 128), axis=1) for g in wide)
        upstream = jnp.concatenate(ups, axis=0).T.astype(BF16)

        slots = r.region_number.shape[1]
        per = slots // n_img
        micros = rows // per
        numbers = r.region_number[...].astype(F32)
        numbers = jnp.concatenate([numbers, jnp.zeros((8 - micros, slots), F32)], axis=0)
        at = lax.broadcasted_iota(jnp.int32, (slots, keys), 1)
        slot = lax.broadcasted_iota(jnp.int32, (slots, keys), 0)
        chosen = slot == per * (at // rows) + lax.rem(at, per)
        numbers = nn(numbers.astype(BF16), jnp.where(chosen, 1.0, 0.0).astype(BF16))
        at = lax.rem(lax.broadcasted_iota(jnp.int32, (1, keys), 1), rows) // per
        code = jnp.zeros((1, keys), F32)
        for m in range(micros):
            code = jnp.where(at == m, numbers[m : m + 1, :] * micros + m, code)
        code_down = jnp.broadcast_to(code, (128, keys)).T
        code_down = jnp.concatenate([code_down] * (keys // 128), axis=1)
        bias = jnp.where(code_down == code, 0.0, NEG)

        qkv, probs, ctx = r.qkv, r.probs, r.ctx
        values = r.crossed[...].reshape(keys, width).T.astype(F32)
        unit, _, inverse = standardize(values, 0)
        r.region_first[...] = padded(unit * gain, shard, n_img).astype(BF16)
        packed = tn(w_triple, r.region_first[...])
        qkv[0:width, 0:keys] = (packed[0:width] * (LOG2E * HD ** (-0.5))).astype(BF16)
        qkv[width:, 0:keys] = packed[width:].astype(BF16)

        def part(which, h):
            return qkv[which * width + HD * h : which * width + HD * (h + 1), 0:keys]

        mixes, scores = [], [tn(part(1, 0), part(0, 0))]
        for h in range(heads):
            if h + 1 < heads:
                scores.append(tn(part(1, h + 1), part(0, h + 1)))
            biased = scores[h] + bias
            weights = jnp.exp2(biased - jnp.max(biased, axis=0, keepdims=True))
            r.shares[0, h : h + 1, :] = 1.0 / jnp.sum(weights, axis=0, keepdims=True)
            probs[h] = weights.astype(BF16)
            if h:
                mixes.append(nn(part(2, h - 1), probs[h - 1]) * r.shares[0, h - 1 : h, :])
        mixes.append(nn(part(2, heads - 1), probs[heads - 1]) * r.shares[0, heads - 1 : heads, :])
        context = jnp.concatenate(mixes, axis=0)
        r.region_context[...] = padded(context, shard, n_img).astype(BF16)
        middle = values + tn(w_merge, r.region_context[...])
        unit_b, _, inverse_b = standardize(middle, 0)
        r.region_second[...] = padded(unit_b * regain, shard, n_img).astype(BF16)
        for c in range(0, hidden, width):
            at = slice(c, c + width)
            active, slope = gelu_pair(tn(w_expand[:, at], r.region_second[...]))
            r.region_active[at, :] = active.astype(BF16)
            r.slope[at, 0:keys] = slope.astype(BF16)
        result = middle + tn(r.region_shrink[...], r.region_active[...])
        mine = pl.ds(pl.multiple_of(me * rows, rows), rows)
        r.region_rows[...] = result.T
        r.region_out[...] = r.region_rows[mine, :].astype(BF16)

        for c in range(0, hidden, width):
            at = slice(c, c + width)
            active_grad = nn(r.region_shrink[at, :], upstream)
            r.active[at, 0:keys] = (active_grad * r.slope[at, 0:keys].astype(F32)).astype(BF16)
        hidden_low = r.active[:, 0:keys]
        second_grad = trimmed(nn(w_expand, hidden_low), shard, n_img)
        middle_grad = upstream.astype(F32) + norm_back(second_grad * regain, unit_b, inverse_b, 0)
        middle_low = middle_grad.astype(BF16)
        context_grad = trimmed(nn(w_merge, middle_low), shard, n_img)
        packed_grad = r.packed_grad
        lows, totals = [], []
        for h in range(heads):
            at = slice(HD * h, HD * (h + 1))
            low = context_grad[at] * r.shares[0, h : h + 1, :]
            totals.append(jnp.sum(low * context[at], axis=0, keepdims=True))
            lows.append(low.astype(BF16))

        def put(which, h, grad):
            packed_grad[which * width + HD * h : which * width + HD * (h + 1), 0:keys] = (
                grad.astype(BF16)
            )

        def key_and_query(h, score_grad):
            put(1, h, nt(part(0, h), score_grad) * LN2)
            put(0, h, nn(part(1, h), score_grad) * HD ** (-0.5))

        grads, score_grads = [tn(part(2, 0), lows[0])], []
        for h in range(heads):
            if h + 1 < heads:
                grads.append(tn(part(2, h + 1), lows[h + 1]))
            put(2, h, nt(lows[h], probs[h]))
            score_grad = probs[h].astype(F32) * (grads[h] - totals[h])
            score_grads.append(score_grad.astype(BF16))
            if h:
                key_and_query(h - 1, score_grads[h - 1])
        key_and_query(heads - 1, score_grads[heads - 1])
        first_grad = trimmed(nn(w_triple, packed_grad[:, 0:keys]), shard, n_img)
        back = norm_back(first_grad * gain, unit, inverse, 0)
        r.region_rows[...] = (middle_grad + back).T
        r.crossed_grad[...] = r.region_rows[mine, :].astype(BF16)
        sibling(r.crossed_grad, r.returned, r.l_returned).start()

        mine = pl.ds(pl.multiple_of(me * PAD, PAD), PAD)
        grads = r.grads
        grads[:, 0 : 3 * width] = nt(r.region_first[mine, :], packed_grad[:, 0:keys])[0:shard]
        grads[:, 3 * width : 4 * width] = nt(r.region_context[mine, :], middle_low)[0:shard]
        grads[:, 4 * width : 4 * width + hidden] = nt(r.region_second[mine, :], hidden_low)[0:shard]
        mine = pl.ds(pl.multiple_of(me * shard_ff, shard_ff), shard_ff)
        r.grads_shrink[...] = nt(r.region_active[mine, :], upstream)
        mine = pl.ds(pl.multiple_of(me * shard, shard), shard)
        for k, (grad, standard) in enumerate(((first_grad, unit), (second_grad, unit_b))):
            total = jnp.sum(grad * standard, axis=1, keepdims=True)
            r.gain_columns[...] = jnp.broadcast_to(total, (width, 128))
            at = 4 * width + hidden + 128 * k
            grads[:, at : at + 128] = r.gain_columns[mine, :]
        sibling(grads, r.grads_in, r.l_grads).start()
        sibling(r.grads_shrink, r.grads_shrink_in, r.l_grads_shrink).start()

    def one_pair(it, carry):
        pair_copy(r.cotangent, r.cot, r.cot_sem, it).wait()
        patch_pair(r, dims, it, it, jnp.minimum(it + 1, pairs - 1))
        pair_copy(r.tok, r.patch_rows, r.out_sem, it).start()
        one_copy(r.input_grad, r.grad_rows, r.grad_sem, it).start()

        if inside:

            @pl.when(it == AT_FORWARD)
            def _():
                wait_all(r.w_all.at[seg], r.l_weights.at[1])
                wait_all(r.s_all.at[seg], r.l_shrink.at[1])
                sibling(r.w_all.at[seg], r.w_all.at[seg], r.l_forward).start()
                sibling(r.s_all.at[seg], r.s_all.at[seg], r.l_forward_shrink).start()

            pl.when(it == AT_REGION)(region)
        return carry

    for it in range(pairs):
        one_copy(r.firstT, r.first_rows, r.first_sem, it).start()
    project(r, dims, 0)
    lax.fori_loop(0, dims.early, one_pair, 0)

    if inside:
        sibling(r.crossed_grad, r.returned, r.l_returned).wait()
        sibling(r.grads, r.grads_in, r.l_grads).wait()
        sibling(r.grads_shrink, r.grads_shrink_in, r.l_grads_shrink).wait()
        r.class_up[...] = r.returned[...]
        r.grads_out[...] = r.grads[...] + r.grads_in[...]
        r.shrink_out[...] = r.grads_shrink[...] + r.grads_shrink_in[...]
        peers = pl.ds(0, n_img - 1)
        wait_all(r.w_all.at[0, peers], r.l_weights.at[0])
        wait_all(r.s_all.at[0, peers], r.l_shrink.at[0])
        wait_all(r.crossed, r.l_crossed.at[0])
    for it in range(pairs):
        one_copy(r.firstT, r.first_rows, r.first_sem, it).wait()
    for it in range(dims.early):
        pair_copy(r.tok, r.patch_rows, r.out_sem, it).wait()
        one_copy(r.input_grad, r.grad_rows, r.grad_sem, it).wait()
    for k, (turned, target) in enumerate(turns):
        pltpu.make_async_copy(turned, target, r.turn_sem.at[k]).wait()


def finish_kernel(dims, *refs):
    r = SimpleNamespace(**dict(zip(dims.names, refs, strict=True)))
    width, hidden = dims.width, dims.hidden
    rows, patches, early = dims.images, dims.patches, dims.early
    pairs, lanes = rows // 2, 2 * patches
    late = pairs - early

    loads = []
    for k, name in enumerate(dims.staged):
        load = pltpu.make_async_copy(getattr(r, name), getattr(r, name + BESIDE), r.load_sem.at[k])
        setattr(r, name, getattr(r, name + BESIDE))
        loads.append(load)
    last = pl.ds(2 * early, 2 * late)
    tok_in = pltpu.make_async_copy(r.tokens.at[last], r.tok, r.late_sem.at[0])
    cot_in = pltpu.make_async_copy(r.cotangent.at[last], r.cot, r.late_sem.at[1])
    ready = pl.ds(0, 2 * early)
    rows_in = pltpu.make_async_copy(r.patch_rows.at[ready], r.ready, r.late_sem.at[2])
    rows_out = pltpu.make_async_copy(r.ready, r.patch_output.at[ready], r.late_sem.at[4])
    firsts = [one_copy(r.first_rows, r.firstT, r.first_sem, it) for it in range(pairs)]
    earlier = [one_copy(r.grad_rows, r.input_grad, r.grad_sem, it) for it in range(early)]
    bounds = (0,) + dims.bounds
    stages = [loads[a:b] for a, b in zip(bounds, bounds[1:])]
    stages[0] = firsts[early:] + [tok_in] + stages[0]
    stages[1] = [cot_in] + stages[1]
    stages[3] = stages[3] + [rows_in] + firsts[:early] + earlier

    def ask(*wanted):
        for stage in wanted:
            for load in stages[stage]:
                load.start()

    def ready(stage):
        for load in stages[stage]:
            load.wait()
        if stage == 0:
            ask(1, 2)
        if stage == 1:
            ask(3)

    ask(0)
    ready(0)
    gain_row = r.frozen_gain[...].astype(F32).reshape(1, width)
    regain_row = r.frozen_regain[...].astype(F32).reshape(1, width)
    r.gainT[...] = column(gain_row, lanes)
    r.regainT[...] = column(regain_row, lanes)
    packed = r.class_packed[...]
    tall_k = spread(packed[:, width : 2 * width])
    tall_v = spread(packed[:, 2 * width :])
    r.class_k[...] = tall_k.reshape(rows, HEADS8, width)
    r.class_v[...] = tall_v.reshape(rows, HEADS8, width)
    project(r, dims, early)
    for it in range(early, pairs):
        following = it + 1 if it + 1 < pairs else None
        wait = ready if it == early else lambda stage: None
        patch_pair(r, dims, it, it - early, following, wait)
    ready(3)
    rows_out.start()
    out = pltpu.make_async_copy(r.tok, r.patch_output.at[last], r.late_sem.at[3])
    out.start()

    upstream = r.class_up[...]
    middle = r.class_middle[...]
    unit, _, inverse = standardize(middle, 1)
    hidden_low = (nt(upstream, r.frozen_shrink[...]) * r.class_slope[...]).astype(BF16)
    second_grad = nt(hidden_low, r.frozen_expand[...])
    middle_grad = upstream.astype(F32) + norm_back(second_grad * regain_row, unit, inverse, 1)
    low = nt(middle_grad.astype(BF16), r.frozen_merge[...]).astype(BF16).astype(F32)
    tall_low = spread(low)
    low_map = nt(tall_low.astype(BF16), r.frozen_triple[:, 2 * width :])
    r.low_map[...] = low_map.reshape(rows, HEADS8, width)
    total = jnp.sum(spread(low * r.class_context[...]), axis=1, keepdims=True)
    r.class_total[...] = jnp.broadcast_to(total, (rows * HEADS8, 128)).reshape(rows, HEADS8, 128)
    r.ungainT[...] = 1.0 / r.gainT[:, 0:patches]

    def correct(step, carry):
        turns = [4 * step + k for k in range(4)]
        grads = []
        for it in turns:
            maps = jnp.concatenate([r.low_map[2 * it + b] for b in range(2)], axis=0)
            grads.append(nn(maps.astype(BF16), r.firstT[it]))
        small = []
        for it, grad in zip(turns, grads):
            for b in range(2):
                image = 2 * it + b
                span = slice(b * patches, (b + 1) * patches)
                part = grad[b * HEADS8 : (b + 1) * HEADS8, span]
                weights = r.class_probs[image]
                score_grad = weights * (part - r.class_total[image][:, 0:1])
                toward = jnp.concatenate([r.query_map[image], r.low_map[image]], axis=0) * gain_row
                left = (toward - mean(toward, 1)).astype(BF16)
                right = jnp.concatenate([score_grad * LN2, weights], axis=0)
                right = right * r.stat[it, 1:2, span]
                scores = jnp.concatenate([r.class_scores[image], part], axis=0)
                along = jnp.sum(right * scores, axis=0, keepdims=True) * (1.0 / width)
                small.append((it, image, span, score_grad, left, right.astype(BF16), along))
        products = [tn(left, right) for _, _, _, _, left, right, _ in small]
        for product, (it, image, span, score_grad, _, _, along) in zip(products, small):
            first = r.firstT[it, :, span]
            r.mixed[image] = nt(score_grad.astype(BF16), first)
            back = product - first.astype(F32) * (r.ungainT[...] * along)
            result = r.input_grad[it, :, span].astype(F32) + back
            r.result[image] = result.astype(BF16).T
        for it in turns:
            pair_copy(r.result, r.patch_gradient, r.back_sem, it).start()
        return carry

    lax.fori_loop(0, pairs // 4, correct, 0)

    self_prob = r.self_prob[...].reshape(rows * HEADS8, 128)[:, 0:1]
    tall_q = spread(packed[:, 0:width])
    self_grad = self_prob * (jnp.sum(tall_low * tall_v, axis=1, keepdims=True) - total)
    unit, _, inverse = standardize(r.class_tokens[...].astype(F32), 1)
    first = (unit * gain_row).astype(BF16).astype(F32)
    tall_first = jnp.broadcast_to(first[:, None, :], (rows, HEADS8, width))
    mixed = r.mixed[...].reshape(rows * HEADS8, width)
    mixed = mixed + self_grad * tall_first.reshape(rows * HEADS8, width)
    triple = r.frozen_triple
    query_grad = gather_heads(nn(mixed.astype(BF16), triple[:, width : 2 * width]))
    key_grad = r.class_dk[...] + (tall_q * (self_grad * HD ** (-0.5))).reshape(
        rows, HEADS8, width
    )
    value_grad = r.class_dv[...] + (tall_low * self_prob).reshape(rows, HEADS8, width)
    packed_grad = jnp.concatenate(
        [query_grad * HD ** (-0.5), jnp.sum(key_grad, axis=1), jnp.sum(value_grad, axis=1)],
        axis=1,
    ).astype(BF16)
    first_grad = nt(packed_grad, triple[...])
    back = norm_back(first_grad * gain_row, unit, inverse, 1)
    r.class_gradient[...] = (middle_grad + back).astype(BF16)
    if dims.inside:
        wide = width * 4 + hidden
        r.region_output[...] = r.region_out[...]
        r.triple_gradient[...] = r.grads_out[:, 0 : 3 * width]
        r.merge_gradient[...] = r.grads_out[:, 3 * width : 4 * width]
        r.expand_gradient[...] = r.grads_out[:, 4 * width : wide]
        r.shrink_gradient[...] = r.shrink_out[...]
        shard = r.grads_out.shape[0]
        blank = jnp.zeros((128 - shard, 128), F32)
        for k, target in enumerate((r.first_gradient, r.second_gradient)):
            columns = r.grads_out[:, wide + 128 * k : wide + 128 * (k + 1)]
            columns = jnp.concatenate([columns, blank], axis=0).T
            target[...] = columns[0:1, 0:shard]
    rows_out.wait()
    out.wait()
    for it in range(pairs):
        pair_copy(r.result, r.patch_gradient, r.back_sem, it).wait()


def normalize(values, scaling):
    centred = values - jnp.mean(values, axis=-1, keepdims=True)
    inverse = lax.rsqrt(jnp.mean(centred * centred, axis=-1, keepdims=True) + EPSILON)
    standard = centred * inverse
    return (standard * scaling, standard, inverse)


def normalize_back(upstream, standard, inverse, scaling):
    scaled = upstream * scaling
    centred = scaled - jnp.mean(scaled, axis=-1, keepdims=True)
    centred = centred - standard * jnp.mean(scaled * standard, axis=-1, keepdims=True)
    gain_grad = jnp.sum((upstream * standard).reshape(-1, upstream.shape[-1]), axis=0)
    return (centred * inverse, gain_grad)


def gelu_slope(hidden):
    return (
        0.5 * (1.0 + lax.erf(hidden * 0.7071067811865476))
        + hidden * jnp.exp(-0.5 * hidden * hidden) * 0.3989422804014327
    )


def forward_product(operand, weight):
    return lax.dot_general(
        operand, weight, (((operand.ndim - 1,), (0,)), ((), ())), preferred_element_type=F32
    )


def backward_product(upstream, weight):
    return lax.dot_general(
        upstream,
        weight,
        (((upstream.ndim - 1,), (1,)), ((), ())),
        preferred_element_type=F32,
    )


def row_product(operand, cotangent):
    left_rows = operand.reshape(-1, operand.shape[-1])
    right_rows = cotangent.reshape(-1, cotangent.shape[-1])
    return lax.dot_general(
        left_rows, right_rows, (((0,), (0,)), ((), ())), preferred_element_type=F32
    )


def heads_of(packed, portion):
    section_width = packed.shape[-1] // 3
    section = packed[..., portion * section_width : (portion + 1) * section_width]
    return section.reshape(packed.shape[:-1] + (section_width // HD, HD))


def raw_scores(queries, keyset, allowed):
    scores = jnp.einsum(
        "bqhd,bkhd->bhqk", queries, keyset, preferred_element_type=F32
    ) * HD ** (-0.5)
    if allowed is None:
        return scores
    return jnp.where(allowed[:, None], scores, -1e30)


def attend(queries, keyset, valueset, allowed):
    scores = raw_scores(queries, keyset, allowed)
    highest = jnp.max(scores, axis=-1, keepdims=True)
    logsum = highest + jnp.log(jnp.sum(jnp.exp(scores - highest), axis=-1, keepdims=True))
    weighting = jnp.exp(scores - logsum).astype(BF16)
    context = jnp.einsum("bhqk,bkhd->bqhd", weighting, valueset, preferred_element_type=F32)
    return (context.astype(BF16), logsum)


def score_terms(queries, keyset, valueset, allowed, logsum, context_grad):
    scores = raw_scores(queries, keyset, allowed)
    weighting = jnp.exp(scores - logsum)
    weight_grad = jnp.einsum(
        "bqhd,bkhd->bhqk", context_grad, valueset, preferred_element_type=F32
    )
    row_total = jnp.sum(weighting * weight_grad, axis=-1, keepdims=True)
    score_grad = (weighting * (weight_grad - row_total)).astype(BF16)
    return (weighting, score_grad, row_total)


def attend_back(queries, keyset, valueset, allowed, logsum, context_grad):
    weighting, score_grad, row_total = score_terms(
        queries, keyset, valueset, allowed, logsum, context_grad
    )
    value_grad = jnp.einsum(
        "bhqk,bqhd->bkhd",
        weighting.astype(BF16),
        context_grad,
        preferred_element_type=F32,
    )
    query_grad = jnp.einsum(
        "bhqk,bkhd->bqhd", score_grad, keyset, preferred_element_type=F32
    ) * HD ** (-0.5)
    key_grad = jnp.einsum(
        "bhqk,bqhd->bkhd", score_grad, queries, preferred_element_type=F32
    ) * HD ** (-0.5)
    return (query_grad, key_grad, value_grad)


def block_head(inputs, scaling, triple):
    normed, standard, inverse = normalize(inputs, scaling)
    first_low = normed.astype(BF16)
    packed = forward_product(first_low, triple).astype(BF16)
    return (first_low, standard, inverse, packed)


def block_tail(inputs, context, regain, merger, expand, shrink):
    middle = inputs + forward_product(context, merger)
    normed, standard, inverse = normalize(middle, regain)
    second = normed.astype(BF16)
    hidden = forward_product(second, expand)
    active = jax.nn.gelu(hidden, approximate=False).astype(BF16)
    result = middle + forward_product(active, shrink)
    return (result, (standard, inverse, second, hidden, active))


def tail_back(upstream, kept_tail, regain, merger, expand, shrink):
    standard, inverse, second, hidden, active = kept_tail
    out_low = upstream.astype(BF16)
    active_grad = backward_product(out_low, shrink)
    hidden_low = (active_grad * gelu_slope(hidden)).astype(BF16)
    second_grad = backward_product(hidden_low, expand)
    norm_grad, regain_grad = normalize_back(second_grad, standard, inverse, regain)
    middle_grad = upstream + norm_grad
    middle_low = middle_grad.astype(BF16)
    context_low = backward_product(middle_low, merger).astype(BF16)
    return (middle_grad, context_low, regain_grad, (middle_low, hidden_low, out_low))


def region_outside(crossed, region_number, region_cotangent, shards_in):
    crossed = lax.ppermute(crossed, SEG, [(0, 1), (1, 0)])
    images = crossed.shape[1]
    model_width = crossed.shape[2]
    gathered = [lax.all_gather(shard, IMG, axis=0, tiled=True) for shard in shards_in]
    full_gain, triple, merger, full_regain, expand, shrink = gathered
    scaling = full_gain.astype(F32)
    regain = full_regain.astype(F32)
    region_in = crossed.astype(F32)
    first_low, standard, inverse, packed = block_head(region_in, scaling, triple)
    local_keys = packed[..., model_width : 2 * model_width]
    local_values = packed[..., 2 * model_width :]
    all_keys, all_values = (
        lax.all_gather(local_keys, IMG, axis=1, tiled=True),
        lax.all_gather(local_values, IMG, axis=1, tiled=True),
    )
    head_shape = all_keys.shape[:-1] + (model_width // HD, HD)
    keyset = all_keys.reshape(head_shape)
    valueset = all_values.reshape(head_shape)
    queries = heads_of(packed, 0)
    first_slot = lax.axis_index(IMG) * images
    own_number = lax.dynamic_slice_in_dim(region_number, first_slot, images, 1)
    allowed = own_number[:, :, None] == region_number[:, None, :]
    context, logsum = attend(queries, keyset, valueset, allowed)
    context = context.reshape(region_in.shape)
    region_result, kept_tail = block_tail(region_in, context, regain, merger, expand, shrink)
    region_output = region_result.astype(BF16)
    upstream = region_cotangent.astype(F32)
    middle_grad, context_low, second_gain_grad, low_rows = tail_back(
        upstream, kept_tail, regain, merger, expand, shrink
    )
    middle_low, hidden_low, out_low = low_rows
    context_heads = context_low.reshape(queries.shape)
    query_grad, key_grad, value_grad = attend_back(
        queries, keyset, valueset, allowed, logsum, context_heads
    )
    key_sum, value_sum = (
        lax.psum_scatter(key_grad.reshape(all_keys.shape), IMG, scatter_dimension=1, tiled=True),
        lax.psum_scatter(
            value_grad.reshape(all_values.shape), IMG, scatter_dimension=1, tiled=True
        ),
    )
    packed_grad = jnp.concatenate(
        [query_grad.reshape(region_in.shape), key_sum, value_sum], axis=-1
    ).astype(BF16)
    norm_grad, first_gain_grad = normalize_back(
        backward_product(packed_grad, triple), standard, inverse, scaling
    )
    input_grad = (middle_grad + norm_grad).astype(BF16)
    second_low = kept_tail[2]
    active_low = kept_tail[4]
    shards = (
        lax.psum_scatter(first_gain_grad, IMG, scatter_dimension=0, tiled=True),
        lax.psum_scatter(
            row_product(first_low, packed_grad), IMG, scatter_dimension=0, tiled=True
        ),
        lax.psum_scatter(row_product(context, middle_low), IMG, scatter_dimension=0, tiled=True),
        lax.psum_scatter(second_gain_grad, IMG, scatter_dimension=0, tiled=True),
        lax.psum_scatter(
            row_product(second_low, hidden_low), IMG, scatter_dimension=0, tiled=True
        ),
        lax.psum_scatter(row_product(active_low, out_low), IMG, scatter_dimension=0, tiled=True),
    )
    totals = tuple(lax.psum(shard.astype(BF16), SEG).astype(F32) for shard in shards)
    return region_output, lax.ppermute(input_grad, SEG, [(0, 1), (1, 0)]), totals


def local(
    n_img,
    patch_tokens,
    class_tokens,
    region_number,
    frozen_gain,
    frozen_triple,
    frozen_merge,
    frozen_regain,
    frozen_expand,
    frozen_shrink,
    gain_first,
    weight_triple,
    weight_merge,
    gain_second,
    weight_expand,
    weight_shrink,
    patch_cotangent,
    region_cotangent,
):
    micros, per, patches, width = patch_tokens.shape
    hidden = frozen_expand.shape[1]
    images = micros * per
    shard, shard_ff = width // n_img, hidden // n_img
    lanes, pairs, keys, heads = 2 * patches, images // 2, n_img * images, width // HD
    inside = keys == patches and shard == PAD - 8 and images == 16 and width == 384

    class_rows = class_tokens.reshape(images, width)
    inputs = dict(
        tokens=patch_tokens.reshape(images, patches, width),
        cotangent=patch_cotangent.reshape(images, patches, width),
        class_tokens=class_rows,
        frozen_gain=frozen_gain,
        frozen_regain=frozen_regain,
        frozen_triple=frozen_triple,
        frozen_merge=frozen_merge,
        frozen_expand=frozen_expand,
        frozen_shrink=frozen_shrink,
    )
    if inside:
        inputs |= dict(
            gain_first=gain_first,
            gain_second=gain_second,
            region_cotangent=region_cotangent.reshape(images, width),
            region_number=region_number,
            weight_triple=weight_triple,
            weight_merge=weight_merge,
            weight_expand=weight_expand,
            weight_shrink=weight_shrink,
        )
    vmem = pl.BlockSpec(memory_space=pltpu.VMEM)
    hbm = pl.BlockSpec(memory_space=pl.ANY)
    streams = 2
    in_specs = [hbm] * streams + [vmem] * (len(inputs) - streams)

    shape = jax.ShapeDtypeStruct
    columns = 4 * width + hidden + 256
    large = dict(
        patch_rows=shape((images, patches, width), BF16),
        first_rows=shape((pairs, width, lanes), BF16),
        grad_rows=shape((pairs, width, lanes), BF16),
        triple_turned=shape((3 * width, width), BF16),
        merge_turned=shape((width, width), BF16),
        expand_turned=shape((hidden, width), BF16),
        shrink_turned=shape((width, hidden), BF16),
    )
    small = dict(
        stat=shape((pairs, 8, lanes), F32),
        class_packed=shape((images, 3 * width), F32),
        class_context=shape((images, width), F32),
        class_middle=shape((images, width), F32),
        class_slope=shape((images, hidden), F32),
        query_map=shape((images, HEADS8, width), F32),
        class_probs=shape((images, HEADS8, patches), F32),
        class_scores=shape((images, HEADS8, patches), F32),
        self_prob=shape((images, HEADS8, 128), F32),
        class_dk=shape((images, HEADS8, width), F32),
        class_dv=shape((images, HEADS8, width), F32),
    )
    if inside:
        small |= dict(
            class_up=shape((images, width), BF16),
            region_out=shape((images, width), BF16),
            grads_out=shape((shard, columns), F32),
            shrink_out=shape((shard_ff, width), F32),
        )
    else:
        small |= dict(class_out=shape((images, width), BF16))
    outputs = large | small
    out_specs = [hbm] * len(large) + [vmem] * len(small)

    v = pltpu.VMEM
    dma = pltpu.SemaphoreType.DMA
    working = dict(
        gainT=v((width, lanes), F32),
        regainT=v((width, lanes), F32),
        qkv=v((3 * width, lanes), BF16),
        ctx=v((width, lanes), BF16),
        probs=v((2 * heads, patches, patches), BF16),
        shares=v((2, HEADS8, patches), F32),
        class_weights=v((2, HEADS8, patches), F32),
        active=v((hidden, lanes), BF16),
        slope=v((hidden, lanes), BF16),
        packed_grad=v((3 * width, lanes), BF16),
        low_grad=v((width, lanes), BF16),
        class_k=v((images, HEADS8, width), F32),
        class_v=v((images, HEADS8, width), F32),
        mixed=v((images, HEADS8, width), F32),
        firstT=v((pairs, width, lanes), BF16),
        input_grad=v((pairs, width, lanes), BF16),
        first_sem=dma((pairs,)),
        grad_sem=dma((pairs,)),
    )
    turned = dict(
        tripleT=v((3 * width, width), BF16),
        mergeT=v((width, width), BF16),
        expandT=v((hidden, width), BF16),
        shrinkT=v((width, hidden), BF16),
    )
    scratch = working | turned | dict(
        tok=v((images, patches, width), BF16),
        cot=v((images, patches, width), BF16),
        class_first=v((images, HEADS8, width), F32),
        self_score=v((images, HEADS8, 128), F32),
        tok_sem=dma((pairs,)),
        cot_sem=dma((pairs,)),
        out_sem=dma((pairs,)),
        turn_sem=dma((len(turned),)),
    )
    if inside:
        deep = PAD * n_img
        scratch |= dict(
            class_out=v((images, width), BF16),
            crossed=v((n_img, images, width), BF16),
            crossed_grad=v((images, width), BF16),
            returned=v((images, width), BF16),
            shard_gains=v((8, 128), F32),
            w_own=v((2, PAD, 4 * width), BF16),
            w_all=v((2, n_img, PAD, 4 * width), BF16),
            s_own=v((2, shard_ff // 2, width), BF16),
            s_all=v((2, n_img, shard_ff // 2, width), BF16),
            region_shrink=v((hidden, width), BF16),
            region_first=v((deep, keys), BF16),
            region_context=v((deep, keys), BF16),
            region_second=v((deep, keys), BF16),
            region_active=v((hidden, keys), BF16),
            region_rows=v((keys, width), F32),
            gain_columns=v((width, 128), F32),
            grads=v((shard, columns), F32),
            grads_in=v((shard, columns), F32),
            grads_shrink=v((shard_ff, width), F32),
            grads_shrink_in=v((shard_ff, width), F32),
            l_weights=dma((2,)),
            l_shrink=dma((2,)),
            l_forward=dma((2,)),
            l_forward_shrink=dma((2,)),
            l_crossed=dma((2,)),
            l_returned=dma((2,)),
            l_grads=dma((2,)),
            l_grads_shrink=dma((2,)),
        )
    sizes = dict(
        n_img=n_img,
        width=width,
        hidden=hidden,
        images=images,
        patches=patches,
        inside=inside,
        early=pairs - LATE,
    )
    limit = dict(vmem_limit_bytes=60 * 1024 * 1024)
    remote = dict(collective_id=0, has_side_effects=True) if inside else {}
    names = list(inputs) + list(outputs) + list(scratch)
    results = pl.pallas_call(
        functools.partial(patch_kernel, SimpleNamespace(names=names, **sizes)),
        out_shape=list(outputs.values()),
        in_specs=in_specs,
        out_specs=out_specs,
        scratch_shapes=list(scratch.values()),
        compiler_params=pltpu.CompilerParams(**limit, **remote),
    )(*inputs.values())
    done = dict(zip(outputs, results, strict=True))

    if not inside:
        class_out = done.pop(list(small)[-1])
        region_output, class_up, grads = region_outside(
            class_out.reshape(class_tokens.shape),
            region_number,
            region_cotangent,
            (gain_first, weight_triple, weight_merge, gain_second, weight_expand, weight_shrink),
        )
        done |= dict(class_up=class_up.reshape(images, width))

    streamed = [done.pop(name) for name in large]
    done = SimpleNamespace(**done)
    tripleT, mergeT, expandT, shrinkT = streamed[-len(turned) :]
    stages = (
        dict(class_packed=done.class_packed, stat=done.stat, tripleT=tripleT),
        dict(mergeT=mergeT, frozen_shrink=frozen_shrink, expandT=expandT),
        dict(
            shrinkT=shrinkT,
            frozen_expand=frozen_expand,
            frozen_merge=frozen_merge,
            frozen_triple=frozen_triple,
            class_dk=done.class_dk,
            class_dv=done.class_dv,
        ),
        dict(class_tokens=class_rows) | vars(done),
    )
    staged, bounds = {}, ()
    for stage in stages:
        staged |= {name: a for name, a in stage.items() if name not in staged}
        bounds += (len(staged),)
    inputs = dict(
        tokens=patch_tokens.reshape(images, patches, width),
        cotangent=patch_cotangent.reshape(images, patches, width),
        patch_rows=streamed[0],
        first_rows=streamed[1],
        grad_rows=streamed[2],
    )
    inputs |= staged
    inputs |= dict(frozen_gain=frozen_gain, frozen_regain=frozen_regain)
    outputs = dict(
        patch_output=shape((images, patches, width), BF16),
        patch_gradient=shape((images, patches, width), BF16),
        class_gradient=shape((images, width), BF16),
    )
    out_specs = [hbm] * 2 + [vmem]
    if inside:
        ready = dict(
            region_output=shape((images, width), BF16),
            first_gradient=shape((1, shard), F32),
            triple_gradient=shape((shard, 3 * width), F32),
            merge_gradient=shape((shard, width), F32),
            second_gradient=shape((1, shard), F32),
            expand_gradient=shape((shard, hidden), F32),
            shrink_gradient=shape((shard_ff, width), F32),
        )
        outputs |= ready
        out_specs += [vmem] * len(ready)
    scratch = working | dict(
        tok=v((2 * LATE, patches, width), BF16),
        cot=v((2 * LATE, patches, width), BF16),
        result=v((images, patches, width), BF16),
        ungainT=v((width, patches), F32),
        low_map=v((images, HEADS8, width), F32),
        class_total=v((images, HEADS8, 128), F32),
        load_sem=dma((len(staged),)),
        ready=v((images - 2 * LATE, patches, width), BF16),
        late_sem=dma((5,)),
        back_sem=dma((pairs,)),
    )
    scratch |= {name + BESIDE: v(a.shape, a.dtype) for name, a in staged.items()}
    names = list(inputs) + list(outputs) + list(scratch)
    sizes |= dict(names=names, staged=list(staged), bounds=bounds)
    results = pl.pallas_call(
        functools.partial(finish_kernel, SimpleNamespace(**sizes)),
        out_shape=list(outputs.values()),
        in_specs=[hbm] * (len(inputs) - 2) + [vmem] * 2,
        out_specs=out_specs,
        scratch_shapes=list(scratch.values()),
        compiler_params=pltpu.CompilerParams(**limit),
    )(*inputs.values())
    done = SimpleNamespace(**dict(zip(outputs, results, strict=True)))
    if inside:
        region_output = done.region_output.reshape(class_tokens.shape)
        grads = (
            done.first_gradient.reshape(shard),
            done.triple_gradient,
            done.merge_gradient,
            done.second_gradient.reshape(shard),
            done.expand_gradient,
            done.shrink_gradient,
        )
    return (
        done.patch_output.reshape(patch_tokens.shape),
        region_output,
        done.patch_gradient.reshape(patch_tokens.shape),
        done.class_gradient.reshape(class_tokens.shape),
        *grads,
    )


def solution(mesh):
    patch, row = P(SEG, IMG, None, None), P(SEG, IMG, None)
    gain, weight, whole = P(IMG), P(IMG, None), P()
    block = (gain, weight, weight, gain, weight, weight)
    placed = (patch, row, P(SEG, None)) + (whole,) * 6 + block + (patch, row)
    return jax.shard_map(
        functools.partial(local, mesh.shape[IMG]),
        mesh=mesh,
        in_specs=placed,
        out_specs=(patch, row, patch, row) + block,
        check_vma=False,
    )
```
